32 devices in a mesh: rep: 4 (over x, core), fsdp: 8 (over z, y).
Axes of the slice: x: 2, y: 2, z: 4, core: 2. Of those that a mesh axis runs over, the one named last changes fastest.
Arguments:
- block_input: bfloat16 [8192, 1024], P(('rep', 'fsdp')), may hold values from -6 to 6
- segments: int32 [32, 256], P(('rep', 'fsdp')), may hold values from 0 to 7, never falling along the last dimension, each value on 1 to 128 neighbouring positions
- cotangent: bfloat16 [8192, 1024], P(('rep', 'fsdp')), may hold values from -6 to 6
- first_gain: bfloat16 [1024], P('fsdp'), may hold values from 0.5 to 1.5
- first_shift: bfloat16 [1024], P('fsdp'), may hold values from -3 to 3
- mix_weight: bfloat16 [1024, 3072], P('fsdp'), may hold values from -0.1875 to 0.1875
- mix_bias: bfloat16 [3072], P('fsdp'), may hold values from -3 to 3
- dense_weight: bfloat16 [1024, 1024], P('fsdp'), may hold values from -0.75 to 0.75
- dense_bias: bfloat16 [1024], P('fsdp'), may hold values from -3 to 3
- second_gain: bfloat16 [1024], P('fsdp'), may hold values from 0.5 to 1.5
- second_shift: bfloat16 [1024], P('fsdp'), may hold values from -3 to 3
- expand_weight: bfloat16 [1024, 4096], P('fsdp'), may hold values from -0.1875 to 0.1875
- expand_bias: bfloat16 [4096], P('fsdp'), may hold values from -3 to 3
- shrink_weight: bfloat16 [4096, 1024], P('fsdp'), may hold values from -0.09375 to 0.09375
- shrink_bias: bfloat16 [1024], P('fsdp'), may hold values from -3 to 3
Outputs:
- block_out: bfloat16 [8192, 1024], P(('rep', 'fsdp'))
- input_grad: float32 [8192, 1024], P(('rep', 'fsdp'))
- first_gain_grad: float32 [1024], P('fsdp')
- first_shift_grad: float32 [1024], P('fsdp')
- mix_weight_grad: float32 [1024, 3072], P('fsdp')
- mix_bias_grad: float32 [3072], P('fsdp')
- dense_weight_grad: float32 [1024, 1024], P('fsdp')
- dense_bias_grad: float32 [1024], P('fsdp')
- second_gain_grad: float32 [1024], P('fsdp')
- second_shift_grad: float32 [1024], P('fsdp')
- expand_weight_grad: float32 [1024, 4096], P('fsdp')
- expand_bias_grad: float32 [4096], P('fsdp')
- shrink_weight_grad: float32 [4096, 1024], P('fsdp')
- shrink_bias_grad: float32 [1024], P('fsdp')
The draws below stay inside these ranges and needn't reach their ends.
Inputs may be any that keep to these rules, and one draw needn't show every extreme that they name: `segments`: within each row of 256 tokens the document numbers never fall; each document holds 1 to 128 tokens.
All inputs are finite; a program needn't handle non-finite values.
Results may differ from the reference program's by a relative error of at most 0.0099.
Values may be sent and summed in bfloat16 or wider, within the bound.
No kernel may reach another device: no remote copies, remote signals or barrier semaphores. Data moves between devices by JAX's collectives and lax.ppermute only.
A program may use at most 192 MiB of HBM per device.

```python
import math
import jax
import jax.numpy as jnp
import numpy as np
from jax import lax

D = 1024
HEADS = 16
HEAD = 64
ROT = 16
FF = 4096
TOK_DEV = 256
DOCS = 8
SEQS = 32
TOKENS = 8192


def block_scale(key, dims, split, least, top_value):
    level = 1.0
    for dim, blocks in split:
        heights = jax.random.uniform(jax.random.fold_in(jax.random.fold_in(key, 6), dim), (blocks,), jnp.float32, least / len(split), top_value / len(split))
        level = level * jnp.repeat(jnp.exp(heights), dims[dim] // blocks).reshape((-1,) + (1,) * (len(dims) - 1 - dim))
    return level


def split_up(amount, total, bound, skew):
    portions = [(1 << 20) // math.isqrt(standing ** skew) + 1 for standing in range(2, amount + 1)]
    surplus, given = total - bound - (amount - 1), [1] * (amount - 1)
    while surplus > 0:
        movable = [i for i in range(amount - 1) if given[i] < bound]
        pool, remaining = sum([portions[i] for i in movable]), surplus
        for i in movable:
            more = min(bound - given[i], max(1, remaining * portions[i] // pool), surplus)
            given[i] = given[i] + more
            surplus = surplus - more
    return np.array([bound] + given)


def ragged_sizes(rng, amount, total, limit, skew):
    if amount == 2:
        one = jax.random.randint(rng, (), max(1, total - limit), min(limit, total - 1) + 1)
        return jnp.stack([one, total - one])
    tallies = jnp.asarray(split_up(amount, total, limit, skew), jnp.int32)
    pairs = (amount - 1) // 2
    giver, sink = tallies[1:1 + 2 * pairs:2], tallies[2:2 + 2 * pairs:2]
    room = jnp.minimum(giver - 1, limit - sink)
    moved = jax.random.randint(jax.random.fold_in(rng, 1), (pairs,), 0, 1 << 20) % (room + 1)
    tallies = tallies.at[1:1 + 2 * pairs:2].set(giver - moved).at[2:2 + 2 * pairs:2].set(sink + moved)
    return tallies[jax.random.permutation(jax.random.fold_in(rng, 2), amount)]


def normal_values(stream_key, shape, width, limit, cuts=(), held_as=jnp.bfloat16):
    gain = block_scale(stream_key, shape, cuts, -0.22, 0.18) if cuts else 1.0
    entries = jax.random.normal(stream_key, shape, jnp.float32) * width * gain
    return jnp.minimum(jnp.maximum(entries, -limit), limit).astype(held_as)


def setup_inputs(seed: int = 0) -> dict:
    keys = jax.random.split(jax.random.key(seed), 16)
    return {
        "block_input": normal_values(keys[0], (TOKENS, D), 1.0, 6.0, ((0, 32),)),
        "segments": jax.vmap(lambda own: jnp.searchsorted(jnp.cumsum(ragged_sizes(own, DOCS, TOK_DEV, TOK_DEV // 2, 1)), jnp.arange(TOK_DEV), side="right"))(jax.random.split(keys[1], SEQS)).reshape((SEQS, TOK_DEV)).astype(jnp.int32),
        "cotangent": normal_values(keys[2], (TOKENS, D), 1.0, 6.0, ((0, 32),)),
        "first_gain": jnp.clip(1.0 + 0.1 * jax.random.normal(keys[3], (D,), jnp.float32), 0.5, 1.5).astype(jnp.bfloat16),
        "first_shift": normal_values(keys[4], (D,), 0.5, 3.0, ((0, 8),)),
        "mix_weight": normal_values(keys[5], (D, 3 * D), D ** -0.5, 0.1875, ((0, 8),)),
        "mix_bias": normal_values(keys[6], (3 * D,), 0.5, 3.0, ((0, 8),)),
        "dense_weight": normal_values(keys[7], (D, D), (D // 16) ** -0.5, 0.75, ((0, 8),)),
        "dense_bias": normal_values(keys[8], (D,), 0.5, 3.0, ((0, 8),)),
        "second_gain": jnp.clip(1.0 + 0.1 * jax.random.normal(keys[9], (D,), jnp.float32), 0.5, 1.5).astype(jnp.bfloat16),
        "second_shift": normal_values(keys[10], (D,), 0.5, 3.0, ((0, 8),)),
        "expand_weight": normal_values(keys[11], (D, FF), D ** -0.5, 0.1875, ((0, 8),)),
        "expand_bias": normal_values(keys[12], (FF,), 0.5, 3.0, ((0, 8),)),
        "shrink_weight": normal_values(keys[13], (FF, D), FF ** -0.5, 0.09375, ((0, 8),)),
        "shrink_bias": normal_values(keys[14], (D,), 0.5, 3.0, ((0, 8),)),
    }


@jax.custom_vjp
def low(v):
    return lax.optimization_barrier(v.astype(jnp.bfloat16)).astype(jnp.float32)

@jax.custom_vjp
def low_back(v):
    return v

def low_keep(v):
    return (low(v), None)

def low_pass(kept, grad):
    return (grad,)

def back_keep(v):
    return (v, None)

def back_low(kept, grad):
    return (low(grad),)
low.defvjp(low_keep, low_pass)
low_back.defvjp(back_keep, back_low)
EPSILON = 1e-05
HIGHEST = lax.Precision.HIGHEST

def layer_norm(inputs, gain_row, shift_row):
    average = lax.optimization_barrier(jnp.mean(inputs, axis=-1, keepdims=True))
    centred = inputs - average
    variance = lax.optimization_barrier(jnp.mean(centred * centred, axis=-1, keepdims=True))
    return centred * lax.rsqrt(variance + EPSILON) * gain_row + shift_row

def rotate(heads_in, cos_table, sin_table):
    half_rot = ROT // 2
    first_half = heads_in[..., :half_rot]
    second_half = heads_in[..., half_rot:ROT]
    return jnp.concatenate([first_half * cos_table - second_half * sin_table, second_half * cos_table + first_half * sin_table, heads_in[..., ROT:]], axis=-1)

def rotary_tables(segment_rows):
    length = segment_rows.shape[-1]
    same_doc = segment_rows[..., :, None] == segment_rows[..., None, :]
    row_index = lax.broadcasted_iota(jnp.int32, (length, length), 0)
    col_index = lax.broadcasted_iota(jnp.int32, (length, length), 1)
    earlier = jnp.where(same_doc & (col_index < row_index), 1.0, 0.0)
    position = lax.optimization_barrier(jnp.sum(earlier, axis=-1)).astype(jnp.float32)
    allowed = same_doc & (col_index <= row_index)
    frequency = jnp.power(10000.0, -2.0 * jnp.arange(ROT // 2).astype(jnp.float32) / ROT)
    phases = position[..., None] * frequency
    return (jnp.cos(phases)[..., None, :], jnp.sin(phases)[..., None, :], allowed)

def block_forward(params, inputs, segment_rows):
    first_gain, first_shift, mix_weight, mix_bias, dense_weight, dense_bias, second_gain, second_shift, expand_weight, expand_bias, shrink_weight, shrink_bias = params
    seq_count = inputs.shape[0]
    flat_rows = inputs.reshape(-1, D)
    normed_one = low(layer_norm(flat_rows, first_gain, first_shift))
    mixed_rows = low_back(jnp.dot(normed_one, mix_weight, precision=HIGHEST) + mix_bias)
    triple = mixed_rows.reshape(seq_count, TOK_DEV, 3, HEADS, HEAD)
    cos_table, sin_table, allowed = rotary_tables(segment_rows)
    queries = low(rotate(triple[:, :, 0], cos_table, sin_table))
    keys_all = low(rotate(triple[:, :, 1], cos_table, sin_table))
    values_all = low(triple[:, :, 2])
    scores = low_back(jnp.einsum('sqhd,skhd->shqk', queries, keys_all, precision=HIGHEST) * HEAD ** (-0.5))
    masked = jnp.where(allowed[:, None], scores, -1e+30)
    row_peak = lax.optimization_barrier(jnp.max(masked, axis=-1, keepdims=True))
    weights_raw = jnp.exp(masked - row_peak)
    probs_low = low(weights_raw / lax.optimization_barrier(jnp.sum(weights_raw, axis=-1, keepdims=True)))
    context = jnp.einsum('shqk,skhd->sqhd', probs_low, values_all, precision=HIGHEST)
    context = low(low_back(context.reshape(-1, D)))
    attention_branch = jnp.dot(context, dense_weight, precision=HIGHEST) + dense_bias
    normed_two = low(layer_norm(flat_rows, second_gain, second_shift))
    hidden_pre = low_back(jnp.dot(normed_two, expand_weight, precision=HIGHEST) + expand_bias)
    hidden_act = low(jax.nn.gelu(hidden_pre, approximate=False))
    feedforward_branch = jnp.dot(hidden_act, shrink_weight, precision=HIGHEST) + shrink_bias
    return (flat_rows + attention_branch + feedforward_branch).reshape(inputs.shape)

def reference(block_input, segments, cotangent, first_gain, first_shift, mix_weight, mix_bias, dense_weight, dense_bias, second_gain, second_shift, expand_weight, expand_bias, shrink_weight, shrink_bias):
    params = jax.tree.map(lambda entry: entry.astype(jnp.float32), (first_gain, first_shift, mix_weight, mix_bias, dense_weight, dense_bias, second_gain, second_shift, expand_weight, expand_bias, shrink_weight, shrink_bias))
    group_size = max((divisor for divisor in range(1, SEQS + 1) if SEQS % divisor == 0 and divisor * TOK_DEV <= max(4096, TOK_DEV)))
    count_groups = SEQS // group_size
    inputs = block_input.astype(jnp.float32).reshape(count_groups, group_size, TOK_DEV, D)
    seg_groups = segments.reshape(count_groups, group_size, TOK_DEV)

    def whole_layer(params_in, inputs_in):
        group_step = jax.checkpoint(lambda group_item: block_forward(params_in, group_item[0], group_item[1]))
        return lax.map(group_step, (inputs_in, seg_groups))
    outputs, pullback = jax.vjp(whole_layer, params, inputs)
    param_grads, input_grads = pullback(cotangent.astype(jnp.float32).reshape(outputs.shape))
    first_gain_grad, first_shift_grad, mix_weight_grad, mix_bias_grad, dense_weight_grad, dense_bias_grad, second_gain_grad, second_shift_grad, expand_weight_grad, expand_bias_grad, shrink_weight_grad, shrink_bias_grad = param_grads
    return (outputs.reshape(TOKENS, D).astype(jnp.bfloat16), input_grads.reshape(TOKENS, D), first_gain_grad, first_shift_grad, mix_weight_grad, mix_bias_grad, dense_weight_grad, dense_bias_grad, second_gain_grad, second_shift_grad, expand_weight_grad, expand_bias_grad, shrink_weight_grad, shrink_bias_grad)
```

```python
import jax
import jax.numpy as jnp
from jax import lax
from jax.sharding import PartitionSpec as P

HEADS = 16
HEAD = 64
ROT = 16


EPSILON = 1e-05


def layer_norm(inputs, gain_row, shift_row):
    average = jnp.mean(inputs, axis=-1, keepdims=True)
    centred = inputs - average
    variance = jnp.mean(centred * centred, axis=-1, keepdims=True)
    return centred * lax.rsqrt(variance + EPSILON) * gain_row + shift_row


def rotate(heads_in, cos_table, sin_table):
    half_rot = ROT // 2
    first_half = heads_in[..., :half_rot]
    second_half = heads_in[..., half_rot:ROT]
    return jnp.concatenate(
        [
            first_half * cos_table - second_half * sin_table,
            second_half * cos_table + first_half * sin_table,
            heads_in[..., ROT:],
        ],
        axis=-1,
    )


def rotary_tables(segment_row):
    length = segment_row.shape[0]
    same_doc = segment_row[:, None] == segment_row[None, :]
    row_index = lax.broadcasted_iota(jnp.int32, (length, length), 0)
    col_index = lax.broadcasted_iota(jnp.int32, (length, length), 1)
    earlier = jnp.where(same_doc & (col_index < row_index), 1.0, 0.0)
    position = jnp.sum(earlier, axis=-1).astype(jnp.float32)
    allowed = same_doc & (col_index <= row_index)
    frequency = jnp.power(10000.0, -2.0 * jnp.arange(ROT // 2).astype(jnp.float32) / ROT)
    phases = position[:, None] * frequency
    return (jnp.cos(phases)[:, None, :], jnp.sin(phases)[:, None, :], allowed)


def product_left(left, right):
    return lax.dot_general(
        left, right, (((0,), (0,)), ((), ())), preferred_element_type=jnp.float32
    )


def product_right(left, right):
    return lax.dot_general(
        left, right, (((1,), (1,)), ((), ())), preferred_element_type=jnp.float32
    )


def norm_backward(inputs, gain_row, shift_row, upstream):
    _, pullback = jax.vjp(layer_norm, inputs, gain_row, shift_row)
    return pullback(upstream)


def local_general(
    block_input,
    segments,
    cotangent,
    first_gain,
    first_shift,
    mix_weight,
    mix_bias,
    dense_weight,
    dense_bias,
    second_gain,
    second_shift,
    expand_weight,
    expand_bias,
    shrink_weight,
    shrink_bias,
):
    attention_parts = (
        lax.all_gather(first_gain, "fsdp", axis=0, tiled=True),
        lax.all_gather(first_shift, "fsdp", axis=0, tiled=True),
        lax.all_gather(mix_weight, "fsdp", axis=0, tiled=True),
        lax.all_gather(mix_bias, "fsdp", axis=0, tiled=True),
        lax.all_gather(dense_weight, "fsdp", axis=0, tiled=True),
        lax.all_gather(dense_bias, "fsdp", axis=0, tiled=True),
    )
    feed_parts = (
        lax.all_gather(second_gain, "fsdp", axis=0, tiled=True),
        lax.all_gather(second_shift, "fsdp", axis=0, tiled=True),
        lax.all_gather(expand_weight, "fsdp", axis=0, tiled=True),
        lax.all_gather(expand_bias, "fsdp", axis=0, tiled=True),
        lax.all_gather(shrink_weight, "fsdp", axis=0, tiled=True),
        lax.all_gather(shrink_bias, "fsdp", axis=0, tiled=True),
    )
    token_count = block_input.shape[0]
    feature_count = block_input.shape[1]
    score_scale = HEAD ** (-0.5)
    block_float = block_input.astype(jnp.float32)
    cot_float = cotangent.astype(jnp.float32)
    cos_table, sin_table, allowed = rotary_tables(segments[0])
    normed_one = layer_norm(
        block_float, attention_parts[0].astype(jnp.float32), attention_parts[1].astype(jnp.float32)
    ).astype(jnp.bfloat16)
    mixed_rows = jnp.dot(normed_one, attention_parts[2], preferred_element_type=jnp.float32)
    mixed_rows = mixed_rows + attention_parts[3].astype(jnp.float32)
    triple = mixed_rows.reshape(token_count, 3, HEADS, HEAD)
    queries = rotate(triple[:, 0], cos_table, sin_table).astype(jnp.bfloat16)
    keys_all = rotate(triple[:, 1], cos_table, sin_table).astype(jnp.bfloat16)
    values_all = triple[:, 2].astype(jnp.bfloat16)

    def masked_scores():
        raw_scores = (
            jnp.einsum("qhd,khd->hqk", queries, keys_all, preferred_element_type=jnp.float32)
            * score_scale
        )
        return jnp.where(allowed[None], raw_scores, -1e30)

    forward_scores = masked_scores()
    row_peak = jnp.max(forward_scores, axis=-1, keepdims=True)
    weights_raw = jnp.exp(forward_scores - row_peak)
    row_total = jnp.sum(weights_raw, axis=-1, keepdims=True)
    log_total = row_peak + jnp.log(row_total)
    probs_low = (weights_raw / row_total).astype(jnp.bfloat16)
    context = jnp.einsum("hqk,khd->qhd", probs_low, values_all, preferred_element_type=jnp.float32)
    context = context.reshape(token_count, feature_count).astype(jnp.bfloat16)
    attention_branch = jnp.dot(context, attention_parts[4], preferred_element_type=jnp.float32)
    attention_branch = attention_branch + attention_parts[5].astype(jnp.float32)
    normed_two = layer_norm(
        block_float, feed_parts[0].astype(jnp.float32), feed_parts[1].astype(jnp.float32)
    ).astype(jnp.bfloat16)
    hidden_pre = jnp.dot(normed_two, feed_parts[2], preferred_element_type=jnp.float32)
    hidden_pre = hidden_pre + feed_parts[3].astype(jnp.float32)
    hidden_act = jax.nn.gelu(hidden_pre, approximate=False).astype(jnp.bfloat16)
    feedforward_branch = jnp.dot(hidden_act, feed_parts[4], preferred_element_type=jnp.float32)
    feedforward_branch = feedforward_branch + feed_parts[5].astype(jnp.float32)
    block_out = (block_float + attention_branch + feedforward_branch).astype(jnp.bfloat16)
    feed_back = (
        lax.all_gather(second_gain, "fsdp", axis=0, tiled=True),
        lax.all_gather(second_shift, "fsdp", axis=0, tiled=True),
        lax.all_gather(expand_weight, "fsdp", axis=0, tiled=True),
        lax.all_gather(expand_bias, "fsdp", axis=0, tiled=True),
        lax.all_gather(shrink_weight, "fsdp", axis=0, tiled=True),
        lax.all_gather(shrink_bias, "fsdp", axis=0, tiled=True),
    )
    bias_sum = jnp.sum(cot_float, axis=0)
    shrink_grad = product_left(hidden_act, cotangent)
    grad_act = product_right(cotangent, feed_back[4])
    _, gelu_pull = jax.vjp(lambda pre_value: jax.nn.gelu(pre_value, approximate=False), hidden_pre)
    grad_pre = gelu_pull(grad_act)[0].astype(jnp.bfloat16)
    expand_grad = product_left(normed_two, grad_pre)
    expand_bias_grad = jnp.sum(grad_pre.astype(jnp.float32), axis=0)
    grad_normed_two = product_right(grad_pre, feed_back[2])
    part_two, second_gain_grad, second_shift_grad = norm_backward(
        block_float,
        feed_back[0].astype(jnp.float32),
        feed_back[1].astype(jnp.float32),
        grad_normed_two,
    )
    feed_grads = (
        lax.psum_scatter(second_gain_grad, "fsdp", scatter_dimension=0, tiled=True),
        lax.psum_scatter(second_shift_grad, "fsdp", scatter_dimension=0, tiled=True),
        lax.psum_scatter(expand_grad, "fsdp", scatter_dimension=0, tiled=True),
        lax.psum_scatter(expand_bias_grad, "fsdp", scatter_dimension=0, tiled=True),
        lax.psum_scatter(shrink_grad, "fsdp", scatter_dimension=0, tiled=True),
        lax.psum_scatter(bias_sum, "fsdp", scatter_dimension=0, tiled=True),
    )
    gain_two_sum, shift_two_sum, expand_sum, expand_bias_sum, shrink_sum, shrink_bias_sum = (
        feed_grads
    )
    attention_back = (
        lax.all_gather(first_gain, "fsdp", axis=0, tiled=True),
        lax.all_gather(first_shift, "fsdp", axis=0, tiled=True),
        lax.all_gather(mix_weight, "fsdp", axis=0, tiled=True),
        lax.all_gather(mix_bias, "fsdp", axis=0, tiled=True),
        lax.all_gather(dense_weight, "fsdp", axis=0, tiled=True),
        lax.all_gather(dense_bias, "fsdp", axis=0, tiled=True),
    )
    dense_grad = product_left(context, cotangent)
    grad_context = product_right(cotangent, attention_back[4]).astype(jnp.bfloat16)
    grad_context = grad_context.reshape(token_count, HEADS, HEAD)
    grad_values = jnp.einsum(
        "hqk,qhd->khd", probs_low, grad_context, preferred_element_type=jnp.float32
    )
    grad_probs = jnp.einsum(
        "qhd,khd->hqk", grad_context, values_all, preferred_element_type=jnp.float32
    )
    probs_exact = jnp.exp(masked_scores() - log_total)
    grad_scores = probs_exact * (
        grad_probs - jnp.sum(probs_exact * grad_probs, axis=-1, keepdims=True)
    )
    grad_scores = grad_scores.astype(jnp.bfloat16)
    grad_queries = (
        jnp.einsum("hqk,khd->qhd", grad_scores, keys_all, preferred_element_type=jnp.float32)
        * score_scale
    )
    grad_keys = (
        jnp.einsum("hqk,qhd->khd", grad_scores, queries, preferred_element_type=jnp.float32)
        * score_scale
    )
    _, rotate_pull = jax.vjp(lambda heads_in: rotate(heads_in, cos_table, sin_table), grad_queries)
    grad_mixed = jnp.stack(
        [rotate_pull(grad_queries)[0], rotate_pull(grad_keys)[0], grad_values], axis=1
    )
    grad_mixed = grad_mixed.reshape(token_count, 3 * feature_count).astype(jnp.bfloat16)
    mix_grad = product_left(normed_one, grad_mixed)
    mix_bias_grad = jnp.sum(grad_mixed.astype(jnp.float32), axis=0)
    grad_normed_one = product_right(grad_mixed, attention_back[2])
    part_one, first_gain_grad, first_shift_grad = norm_backward(
        block_float,
        attention_back[0].astype(jnp.float32),
        attention_back[1].astype(jnp.float32),
        grad_normed_one,
    )
    attention_grads = (
        lax.psum_scatter(first_gain_grad, "fsdp", scatter_dimension=0, tiled=True),
        lax.psum_scatter(first_shift_grad, "fsdp", scatter_dimension=0, tiled=True),
        lax.psum_scatter(mix_grad, "fsdp", scatter_dimension=0, tiled=True),
        lax.psum_scatter(mix_bias_grad, "fsdp", scatter_dimension=0, tiled=True),
        lax.psum_scatter(dense_grad, "fsdp", scatter_dimension=0, tiled=True),
        lax.psum_scatter(bias_sum, "fsdp", scatter_dimension=0, tiled=True),
    )
    gain_one_sum, shift_one_sum, mix_sum, mix_bias_sum, dense_sum, dense_bias_sum = attention_grads
    (
        gain_one_sum,
        shift_one_sum,
        mix_sum,
        mix_bias_sum,
        dense_sum,
        dense_bias_sum,
        gain_two_sum,
        shift_two_sum,
        expand_sum,
        expand_bias_sum,
        shrink_sum,
        shrink_bias_sum,
    ) = lax.psum(
        (
            gain_one_sum,
            shift_one_sum,
            mix_sum,
            mix_bias_sum,
            dense_sum,
            dense_bias_sum,
            gain_two_sum,
            shift_two_sum,
            expand_sum,
            expand_bias_sum,
            shrink_sum,
            shrink_bias_sum,
        ),
        "rep",
    )
    input_grad = cot_float + part_one + part_two
    return (
        block_out,
        input_grad,
        gain_one_sum,
        shift_one_sum,
        mix_sum,
        mix_bias_sum,
        dense_sum,
        dense_bias_sum,
        gain_two_sum,
        shift_two_sum,
        expand_sum,
        expand_bias_sum,
        shrink_sum,
        shrink_bias_sum,
    )


TP_REP = 4
TP_FSDP = 8


def coordinates():
    rep = lax.axis_index("rep")
    shard = lax.axis_index("fsdp")
    return rep // 2, rep % 2, shard // 4, (shard // 2) % 2, shard % 2


def permute(value, target):
    pairs = []
    for rep in range(TP_REP):
        for shard in range(TP_FSDP):
            place = (rep // 2, rep % 2, shard // 4, (shard // 2) % 2, shard % 2)
            goal = target(*place)
            if goal is not None:
                x, core, high, low, y = goal
                pairs.append((rep * TP_FSDP + shard, (2 * x + core) * TP_FSDP + 4 * high + 2 * low + y))
    return lax.ppermute(value, ("rep", "fsdp"), pairs)


def swap_x(value):
    return permute(value, lambda x, c, h, l, y: (1 - x, c, h, l, y))


def swap_core(value):
    return permute(value, lambda x, c, h, l, y: (x, 1 - c, h, l, y))


def swap_high(value):
    return permute(value, lambda x, c, h, l, y: (x, c, 1 - h, l, y))


def swap_low(value):
    return permute(value, lambda x, c, h, l, y: (x, c, h, 1 - l, y))


def swap_y(value):
    return permute(value, lambda x, c, h, l, y: (x, c, h, l, 1 - y))


def swap_x_low(value):
    return permute(value, lambda x, c, h, l, y: (1 - x, c, h, 1 - l, y))


def shift_z(value, step):
    def target(x, c, h, l, y):
        moved = (2 * h + l + step) % 4
        return (x, c, moved // 2, moved % 2, y)

    return permute(value, target)


def gather_sequences(own):
    near = jnp.stack([own, swap_low(own), swap_x(own), swap_x_low(own)])
    return jnp.concatenate([near, swap_core(near)])


def scatter_sequences(blocks):
    four = blocks[:4].astype(jnp.float32) + swap_core(blocks[4:]).astype(jnp.float32)
    half = four[2:].astype(jnp.bfloat16)
    two = four[:2] + swap_x(half).astype(jnp.float32)
    return two[0] + swap_low(two[1].astype(jnp.bfloat16)).astype(jnp.float32)


def pick(array, index, axis=0):
    return lax.dynamic_index_in_dim(array, index, axis, keepdims=False)


def gather_pieces(mine, other, place):
    _, _, high, low, y = place
    z = 2 * high + low
    along = [mine, shift_z(other, 1), shift_z(mine, 2), shift_z(other, 3)]
    across = [swap_y(along[0])] + list(swap_y(jnp.stack(along[1:])))
    pieces = jnp.zeros((4, 2) + mine.shape, mine.dtype)
    zeros = (0,) * mine.ndim
    for step in range(4):
        source = (z + 4 - step) % 4
        pieces = lax.dynamic_update_slice(pieces, along[step][None, None], (source, y) + zeros)
        pieces = lax.dynamic_update_slice(pieces, across[step][None, None], (source, 1 - y) + zeros)
    return pieces.reshape((8,) + mine.shape)


def reduce_pieces(partial, place):
    _, _, high, _, y = place
    cut = partial.reshape((2, 2, 2) + partial.shape[1:])
    sent = swap_y(pick(cut, 1 - y, 2).astype(jnp.bfloat16))
    total = pick(cut, y, 2).astype(jnp.float32) + sent.astype(jnp.float32)
    sent = swap_high(pick(total, 1 - high).astype(jnp.bfloat16))
    return pick(total, high) + sent.astype(jnp.float32)


def ordered(first, second, bit):
    return jnp.stack([jnp.where(bit == 0, first, second), jnp.where(bit == 0, second, first)])


def share_slices(total, vectors, place):
    x, core, _, low, _ = place
    shape = total.shape[1:]
    total = total.astype(jnp.bfloat16)
    mine = pick(total, low)
    got = swap_low(pick(total, 1 - low))
    pair = ordered(mine, got, low)
    got = swap_x(pair)
    four = ordered(pair, got, x)
    got = swap_core(four)
    return ordered(four, got, core)


def reduce_vectors(total, place):
    _, _, _, low, _ = place
    total = total.astype(jnp.bfloat16)
    total = pick(total, low).astype(jnp.float32) + swap_low(pick(total, 1 - low)).astype(jnp.float32)
    total = total.astype(jnp.bfloat16)
    total = (total.astype(jnp.float32) + swap_x(total).astype(jnp.float32)).astype(jnp.bfloat16)
    return total.astype(jnp.float32) + swap_core(total).astype(jnp.float32)


def fetch_dense(dense_weight, place):
    x, core, high, _, y = place
    got = permute(dense_weight, lambda x, c, h, l, y: (x, c, h, l, 1 - y) if y == c else None)
    held = jnp.where(y == core, dense_weight, got)
    got = permute(held, lambda x, c, h, l, y: (x, c, 1 - h, l, y) if h == x else None)
    return jnp.where(high == x, held, got)


def return_dense(partial, place):
    x, core, high, _, y = place
    got = permute(partial.astype(jnp.bfloat16), lambda x, c, h, l, y: (x, c, h, l, 1 - y) if y != c else None)
    total = partial + got.astype(jnp.float32)
    got = permute(total.astype(jnp.bfloat16), lambda x, c, h, l, y: (x, c, 1 - h, l, y) if h != x else None)
    total = (total + got.astype(jnp.float32)).astype(jnp.bfloat16)
    got = permute(total, lambda x, c, h, l, y: (1 - x, c, h, l, y) if h == x else None)
    total = jnp.where(high == x, total, got)
    got = permute(total, lambda x, c, h, l, y: (x, 1 - c, h, l, y) if y == c else None)
    return jnp.where(y == core, total, got)


def local(
    block_input,
    segments,
    cotangent,
    first_gain,
    first_shift,
    mix_weight,
    mix_bias,
    dense_weight,
    dense_bias,
    second_gain,
    second_shift,
    expand_weight,
    expand_bias,
    shrink_weight,
    shrink_bias,
):
    f32, bf16 = jnp.float32, jnp.bfloat16
    place = coordinates()
    x, core, high, low, y = place
    rank = 4 * x + 2 * low + core
    mate = rank ^ 2
    tokens, width = block_input.shape
    rows = mix_weight.shape[0]
    group = 8

    marks = jnp.pad(segments.astype(bf16), ((0, 15), (0, width - tokens)))
    near_all = gather_sequences(jnp.concatenate([block_input, marks]))
    cot_all = gather_sequences(cotangent)

    small = jnp.concatenate(
        [first_gain, first_shift, second_gain, second_shift, dense_bias, shrink_bias, mix_bias, expand_bias]
    )
    small = jnp.pad(small, (0, 16 * 384 - small.shape[0])).reshape(16, 384)
    mix_cut = mix_weight.reshape(rows, 3, group, 128)

    def mix_slice(which):
        return jnp.concatenate([pick(mix_cut, which, 2).reshape(rows, 384), small])

    mix_pieces = gather_pieces(mix_slice(rank), mix_slice(mate), place)
    expand_cut = expand_weight.reshape(rows, group, group, 64)
    expand_pieces = gather_pieces(
        pick(expand_cut, rank, 2).reshape(rows, 512), pick(expand_cut, mate, 2).reshape(rows, 512), place
    )
    shrink_cut = shrink_weight.reshape(group, 64, width)
    shrink_pieces = gather_pieces(pick(shrink_cut, rank), pick(shrink_cut, mate), place)
    dense = fetch_dense(dense_weight, place)

    mix = mix_pieces[:, :rows].reshape(width, 384)
    smalls = mix_pieces[:, rows:].reshape(8, 16 * 384).astype(f32)
    parts, start = [], 0
    for size in (rows,) * 6 + (mix_bias.shape[0], expand_bias.shape[0]):
        parts.append(smalls[:, start : start + size].reshape(-1))
        start += size
    gain_one, shift_one, gain_two, shift_two, dense_bias_all, shrink_bias_all, mix_bias_all, expand_bias_all = parts
    mix_bias_own = pick(mix_bias_all.reshape(3, group, 128), rank, 1)
    expand_bias_own = pick(expand_bias_all.reshape(group, group, 64), rank, 1).reshape(512)
    expand = expand_pieces.reshape(width, 512)
    shrink = shrink_pieces.reshape(512, width)

    inputs = near_all[:, :tokens].astype(f32)
    segs = near_all[:, tokens, :tokens].astype(jnp.int32)
    average = jnp.mean(inputs, axis=-1, keepdims=True)
    centred = inputs - average
    scale = lax.rsqrt(jnp.mean(centred * centred, axis=-1, keepdims=True) + EPSILON)
    normed = (centred * scale).reshape(group * tokens, width)
    normed_one = (normed * gain_one + shift_one).astype(bf16)
    normed_two = (normed * gain_two + shift_two).astype(bf16)

    score_scale = HEAD ** (-0.5)
    cos_table, sin_table, allowed = jax.vmap(rotary_tables)(segs)
    mixed = jnp.dot(normed_one, mix, preferred_element_type=f32) + mix_bias_own.reshape(384)
    triple = mixed.reshape(group, tokens, 3, 2, HEAD)
    queries = rotate(triple[:, :, 0], cos_table, sin_table).astype(bf16)
    keys_all = rotate(triple[:, :, 1], cos_table, sin_table).astype(bf16)
    values_all = triple[:, :, 2].astype(bf16)
    scores = jnp.einsum("sqhd,skhd->shqk", queries, keys_all, preferred_element_type=f32) * score_scale
    scores = jnp.where(allowed[:, None], scores, -1e30)
    weights_raw = jnp.exp(scores - jnp.max(scores, axis=-1, keepdims=True))
    probs = weights_raw / jnp.sum(weights_raw, axis=-1, keepdims=True)
    probs_low = probs.astype(bf16)
    context = jnp.einsum("shqk,skhd->sqhd", probs_low, values_all, preferred_element_type=f32)
    context = context.reshape(group * tokens, 128).astype(bf16)

    hidden_pre = jnp.dot(normed_two, expand, preferred_element_type=f32) + expand_bias_own
    hidden_act = jax.nn.gelu(hidden_pre, approximate=False).astype(bf16)
    branch = jnp.dot(context, dense, preferred_element_type=f32)
    branch = branch + jnp.dot(hidden_act, shrink, preferred_element_type=f32)
    branch = scatter_sequences(branch.astype(bf16).reshape(group, tokens, width))
    block_out = block_input.astype(f32) + branch + (dense_bias_all + shrink_bias_all)
    block_out = block_out.astype(bf16)

    cots = cot_all.reshape(group * tokens, width)
    shrink_grad = product_left(hidden_act, cots)
    shrink_total = reduce_pieces(shrink_grad.reshape(8, 64, width), place)
    grad_act = product_right(cots, shrink)
    _, gelu_pull = jax.vjp(lambda pre_value: jax.nn.gelu(pre_value, approximate=False), hidden_pre)
    grad_pre = gelu_pull(grad_act)[0].astype(bf16)
    expand_grad = product_left(normed_two, grad_pre)
    expand_total = reduce_pieces(expand_grad.reshape(8, rows, 512), place)
    expand_bias_grad = jnp.sum(grad_pre.astype(f32), axis=0)
    error_two = product_right(grad_pre, expand)

    dense_grad = return_dense(product_left(context, cots), place)
    grad_context = product_right(cots, dense).astype(bf16).reshape(group, tokens, 2, HEAD)
    grad_values = jnp.einsum("shqk,sqhd->skhd", probs_low, grad_context, preferred_element_type=f32)
    grad_probs = jnp.einsum("sqhd,skhd->shqk", grad_context, values_all, preferred_element_type=f32)
    grad_scores = probs * (grad_probs - jnp.sum(probs * grad_probs, axis=-1, keepdims=True))
    grad_scores = grad_scores.astype(bf16)
    grad_queries = jnp.einsum("shqk,skhd->sqhd", grad_scores, keys_all, preferred_element_type=f32) * score_scale
    grad_keys = jnp.einsum("shqk,sqhd->skhd", grad_scores, queries, preferred_element_type=f32) * score_scale
    grad_mixed = jnp.stack(
        [rotate(grad_queries, cos_table, -sin_table), rotate(grad_keys, cos_table, -sin_table), grad_values], axis=2
    )
    grad_mixed = grad_mixed.reshape(group * tokens, 384).astype(bf16)
    mix_grad = product_left(normed_one, grad_mixed)
    mix_bias_grad = jnp.sum(grad_mixed.astype(f32), axis=0)
    error_one = product_right(grad_mixed, mix)

    upstream = (error_one * gain_one + error_two * gain_two).astype(bf16)
    upstream = scatter_sequences(upstream.reshape(group, tokens, width))
    own = normed[:tokens]
    pulled = upstream - jnp.mean(upstream, axis=-1, keepdims=True)
    pulled = pulled - own * jnp.mean(upstream * own, axis=-1, keepdims=True)
    input_grad = cotangent.astype(f32) + scale[0] * pulled

    spread_mix = jnp.zeros((3, group, 128), f32)
    spread_mix = lax.dynamic_update_slice(spread_mix, mix_bias_grad.reshape(3, 1, 128), (0, rank, 0))
    spread_expand = jnp.zeros((group, group, 64), f32)
    spread_expand = lax.dynamic_update_slice(spread_expand, expand_bias_grad.reshape(group, 1, 64), (0, rank, 0))
    vectors = jnp.concatenate(
        [
            jnp.sum(error_one * normed, axis=0).reshape(8, -1),
            jnp.sum(error_one, axis=0).reshape(8, -1),
            jnp.sum(error_two * normed, axis=0).reshape(8, -1),
            jnp.sum(error_two, axis=0).reshape(8, -1),
            jnp.sum(cotangent.astype(f32), axis=0).reshape(8, -1),
            spread_mix.reshape(8, -1),
            spread_expand.reshape(8, -1),
        ],
        axis=1,
    )
    vectors = vectors.reshape(8, -1, 128)
    mix_total = reduce_pieces(mix_grad.reshape(8, rows, 384), place)
    vector_total = reduce_vectors(reduce_pieces(vectors, place), place).reshape(-1)
    shards, start = [], 0
    for size in (rows,) * 5 + (mix_bias.shape[0], expand_bias.shape[0]):
        shards.append(vector_total[start : start + size])
        start += size
    gain_one_grad, shift_one_grad, gain_two_grad, shift_two_grad, cot_sum, mix_bias_sum, expand_bias_sum = shards

    shrink_out = share_slices(shrink_total, None, place).transpose(1, 2, 0, 3, 4).reshape(512, width)
    expand_out = share_slices(expand_total, None, place).reshape(2, 2, 2, rows, group, 64)
    expand_out = expand_out.transpose(3, 4, 1, 2, 0, 5).reshape(rows, 4096)
    mix_out = share_slices(mix_total, None, place).reshape(2, 2, 2, rows, 3, 128)
    mix_out = mix_out.transpose(3, 4, 1, 2, 0, 5).reshape(rows, 3072)
    return (
        block_out,
        input_grad,
        gain_one_grad,
        shift_one_grad,
        mix_out.astype(f32),
        mix_bias_sum,
        dense_grad.astype(f32),
        cot_sum,
        gain_two_grad,
        shift_two_grad,
        expand_out.astype(f32),
        expand_bias_sum,
        shrink_out.astype(f32),
        cot_sum,
    )


def solution(mesh):
    tensor_parallel = mesh.shape["rep"] == TP_REP and mesh.shape["fsdp"] == TP_FSDP
    return jax.shard_map(
        local if tensor_parallel else local_general,
        mesh=mesh,
        in_specs=(
            P(("rep", "fsdp"), None),
            P(("rep", "fsdp"), None),
            P(("rep", "fsdp"), None),
            P("fsdp"),
            P("fsdp"),
            P("fsdp", None),
            P("fsdp"),
            P("fsdp", None),
            P("fsdp"),
            P("fsdp"),
            P("fsdp"),
            P("fsdp", None),
            P("fsdp"),
            P("fsdp", None),
            P("fsdp"),
        ),
        out_specs=(
            P(("rep", "fsdp"), None),
            P(("rep", "fsdp"), None),
            P("fsdp"),
            P("fsdp"),
            P("fsdp", None),
            P("fsdp"),
            P("fsdp", None),
            P("fsdp"),
            P("fsdp"),
            P("fsdp"),
            P("fsdp", None),
            P("fsdp"),
            P("fsdp", None),
            P("fsdp"),
        ),
        check_vma=False,
    )
```

```python
import jax
import jax.numpy as jnp
import numpy as np
from jax import lax
from jax.experimental import pallas as pl
from jax.experimental.pallas import tpu as pltpu
from jax.sharding import PartitionSpec as P

HEADS = 16
HEAD = 64
ROT = 16


EPSILON = 1e-05


def layer_norm(inputs, gain_row, shift_row):
    average = jnp.mean(inputs, axis=-1, keepdims=True)
    centred = inputs - average
    variance = jnp.mean(centred * centred, axis=-1, keepdims=True)
    return centred * lax.rsqrt(variance + EPSILON) * gain_row + shift_row


def rotate(heads_in, cos_table, sin_table):
    half_rot = ROT // 2
    first_half = heads_in[..., :half_rot]
    second_half = heads_in[..., half_rot:ROT]
    return jnp.concatenate(
        [
            first_half * cos_table - second_half * sin_table,
            second_half * cos_table + first_half * sin_table,
            heads_in[..., ROT:],
        ],
        axis=-1,
    )


def rotary_tables(segment_row):
    length = segment_row.shape[0]
    same_doc = segment_row[:, None] == segment_row[None, :]
    row_index = lax.broadcasted_iota(jnp.int32, (length, length), 0)
    col_index = lax.broadcasted_iota(jnp.int32, (length, length), 1)
    earlier = jnp.where(same_doc & (col_index < row_index), 1.0, 0.0)
    position = jnp.sum(earlier, axis=-1).astype(jnp.float32)
    allowed = same_doc & (col_index <= row_index)
    frequency = jnp.power(10000.0, -2.0 * jnp.arange(ROT // 2).astype(jnp.float32) / ROT)
    phases = position[:, None] * frequency
    return (jnp.cos(phases)[:, None, :], jnp.sin(phases)[:, None, :], allowed)


def product_left(left, right):
    return lax.dot_general(
        left, right, (((0,), (0,)), ((), ())), preferred_element_type=jnp.float32
    )


def product_right(left, right):
    return lax.dot_general(
        left, right, (((1,), (1,)), ((), ())), preferred_element_type=jnp.float32
    )


def norm_backward(inputs, gain_row, shift_row, upstream):
    _, pullback = jax.vjp(layer_norm, inputs, gain_row, shift_row)
    return pullback(upstream)


def local_general(
    block_input,
    segments,
    cotangent,
    first_gain,
    first_shift,
    mix_weight,
    mix_bias,
    dense_weight,
    dense_bias,
    second_gain,
    second_shift,
    expand_weight,
    expand_bias,
    shrink_weight,
    shrink_bias,
):
    attention_parts = (
        lax.all_gather(first_gain, "fsdp", axis=0, tiled=True),
        lax.all_gather(first_shift, "fsdp", axis=0, tiled=True),
        lax.all_gather(mix_weight, "fsdp", axis=0, tiled=True),
        lax.all_gather(mix_bias, "fsdp", axis=0, tiled=True),
        lax.all_gather(dense_weight, "fsdp", axis=0, tiled=True),
        lax.all_gather(dense_bias, "fsdp", axis=0, tiled=True),
    )
    feed_parts = (
        lax.all_gather(second_gain, "fsdp", axis=0, tiled=True),
        lax.all_gather(second_shift, "fsdp", axis=0, tiled=True),
        lax.all_gather(expand_weight, "fsdp", axis=0, tiled=True),
        lax.all_gather(expand_bias, "fsdp", axis=0, tiled=True),
        lax.all_gather(shrink_weight, "fsdp", axis=0, tiled=True),
        lax.all_gather(shrink_bias, "fsdp", axis=0, tiled=True),
    )
    token_count = block_input.shape[0]
    feature_count = block_input.shape[1]
    score_scale = HEAD ** (-0.5)
    block_float = block_input.astype(jnp.float32)
    cot_float = cotangent.astype(jnp.float32)
    cos_table, sin_table, allowed = rotary_tables(segments[0])
    normed_one = layer_norm(
        block_float, attention_parts[0].astype(jnp.float32), attention_parts[1].astype(jnp.float32)
    ).astype(jnp.bfloat16)
    mixed_rows = jnp.dot(normed_one, attention_parts[2], preferred_element_type=jnp.float32)
    mixed_rows = mixed_rows + attention_parts[3].astype(jnp.float32)
    triple = mixed_rows.reshape(token_count, 3, HEADS, HEAD)
    queries = rotate(triple[:, 0], cos_table, sin_table).astype(jnp.bfloat16)
    keys_all = rotate(triple[:, 1], cos_table, sin_table).astype(jnp.bfloat16)
    values_all = triple[:, 2].astype(jnp.bfloat16)

    def masked_scores():
        raw_scores = (
            jnp.einsum("qhd,khd->hqk", queries, keys_all, preferred_element_type=jnp.float32)
            * score_scale
        )
        return jnp.where(allowed[None], raw_scores, -1e30)

    forward_scores = masked_scores()
    row_peak = jnp.max(forward_scores, axis=-1, keepdims=True)
    weights_raw = jnp.exp(forward_scores - row_peak)
    row_total = jnp.sum(weights_raw, axis=-1, keepdims=True)
    log_total = row_peak + jnp.log(row_total)
    probs_low = (weights_raw / row_total).astype(jnp.bfloat16)
    context = jnp.einsum("hqk,khd->qhd", probs_low, values_all, preferred_element_type=jnp.float32)
    context = context.reshape(token_count, feature_count).astype(jnp.bfloat16)
    attention_branch = jnp.dot(context, attention_parts[4], preferred_element_type=jnp.float32)
    attention_branch = attention_branch + attention_parts[5].astype(jnp.float32)
    normed_two = layer_norm(
        block_float, feed_parts[0].astype(jnp.float32), feed_parts[1].astype(jnp.float32)
    ).astype(jnp.bfloat16)
    hidden_pre = jnp.dot(normed_two, feed_parts[2], preferred_element_type=jnp.float32)
    hidden_pre = hidden_pre + feed_parts[3].astype(jnp.float32)
    hidden_act = jax.nn.gelu(hidden_pre, approximate=False).astype(jnp.bfloat16)
    feedforward_branch = jnp.dot(hidden_act, feed_parts[4], preferred_element_type=jnp.float32)
    feedforward_branch = feedforward_branch + feed_parts[5].astype(jnp.float32)
    block_out = (block_float + attention_branch + feedforward_branch).astype(jnp.bfloat16)
    feed_back = (
        lax.all_gather(second_gain, "fsdp", axis=0, tiled=True),
        lax.all_gather(second_shift, "fsdp", axis=0, tiled=True),
        lax.all_gather(expand_weight, "fsdp", axis=0, tiled=True),
        lax.all_gather(expand_bias, "fsdp", axis=0, tiled=True),
        lax.all_gather(shrink_weight, "fsdp", axis=0, tiled=True),
        lax.all_gather(shrink_bias, "fsdp", axis=0, tiled=True),
    )
    bias_sum = jnp.sum(cot_float, axis=0)
    shrink_grad = product_left(hidden_act, cotangent)
    grad_act = product_right(cotangent, feed_back[4])
    _, gelu_pull = jax.vjp(lambda pre_value: jax.nn.gelu(pre_value, approximate=False), hidden_pre)
    grad_pre = gelu_pull(grad_act)[0].astype(jnp.bfloat16)
    expand_grad = product_left(normed_two, grad_pre)
    expand_bias_grad = jnp.sum(grad_pre.astype(jnp.float32), axis=0)
    grad_normed_two = product_right(grad_pre, feed_back[2])
    part_two, second_gain_grad, second_shift_grad = norm_backward(
        block_float,
        feed_back[0].astype(jnp.float32),
        feed_back[1].astype(jnp.float32),
        grad_normed_two,
    )
    feed_grads = (
        lax.psum_scatter(second_gain_grad, "fsdp", scatter_dimension=0, tiled=True),
        lax.psum_scatter(second_shift_grad, "fsdp", scatter_dimension=0, tiled=True),
        lax.psum_scatter(expand_grad, "fsdp", scatter_dimension=0, tiled=True),
        lax.psum_scatter(expand_bias_grad, "fsdp", scatter_dimension=0, tiled=True),
        lax.psum_scatter(shrink_grad, "fsdp", scatter_dimension=0, tiled=True),
        lax.psum_scatter(bias_sum, "fsdp", scatter_dimension=0, tiled=True),
    )
    gain_two_sum, shift_two_sum, expand_sum, expand_bias_sum, shrink_sum, shrink_bias_sum = (
        feed_grads
    )
    attention_back = (
        lax.all_gather(first_gain, "fsdp", axis=0, tiled=True),
        lax.all_gather(first_shift, "fsdp", axis=0, tiled=True),
        lax.all_gather(mix_weight, "fsdp", axis=0, tiled=True),
        lax.all_gather(mix_bias, "fsdp", axis=0, tiled=True),
        lax.all_gather(dense_weight, "fsdp", axis=0, tiled=True),
        lax.all_gather(dense_bias, "fsdp", axis=0, tiled=True),
    )
    dense_grad = product_left(context, cotangent)
    grad_context = product_right(cotangent, attention_back[4]).astype(jnp.bfloat16)
    grad_context = grad_context.reshape(token_count, HEADS, HEAD)
    grad_values = jnp.einsum(
        "hqk,qhd->khd", probs_low, grad_context, preferred_element_type=jnp.float32
    )
    grad_probs = jnp.einsum(
        "qhd,khd->hqk", grad_context, values_all, preferred_element_type=jnp.float32
    )
    probs_exact = jnp.exp(masked_scores() - log_total)
    grad_scores = probs_exact * (
        grad_probs - jnp.sum(probs_exact * grad_probs, axis=-1, keepdims=True)
    )
    grad_scores = grad_scores.astype(jnp.bfloat16)
    grad_queries = (
        jnp.einsum("hqk,khd->qhd", grad_scores, keys_all, preferred_element_type=jnp.float32)
        * score_scale
    )
    grad_keys = (
        jnp.einsum("hqk,qhd->khd", grad_scores, queries, preferred_element_type=jnp.float32)
        * score_scale
    )
    _, rotate_pull = jax.vjp(lambda heads_in: rotate(heads_in, cos_table, sin_table), grad_queries)
    grad_mixed = jnp.stack(
        [rotate_pull(grad_queries)[0], rotate_pull(grad_keys)[0], grad_values], axis=1
    )
    grad_mixed = grad_mixed.reshape(token_count, 3 * feature_count).astype(jnp.bfloat16)
    mix_grad = product_left(normed_one, grad_mixed)
    mix_bias_grad = jnp.sum(grad_mixed.astype(jnp.float32), axis=0)
    grad_normed_one = product_right(grad_mixed, attention_back[2])
    part_one, first_gain_grad, first_shift_grad = norm_backward(
        block_float,
        attention_back[0].astype(jnp.float32),
        attention_back[1].astype(jnp.float32),
        grad_normed_one,
    )
    attention_grads = (
        lax.psum_scatter(first_gain_grad, "fsdp", scatter_dimension=0, tiled=True),
        lax.psum_scatter(first_shift_grad, "fsdp", scatter_dimension=0, tiled=True),
        lax.psum_scatter(mix_grad, "fsdp", scatter_dimension=0, tiled=True),
        lax.psum_scatter(mix_bias_grad, "fsdp", scatter_dimension=0, tiled=True),
        lax.psum_scatter(dense_grad, "fsdp", scatter_dimension=0, tiled=True),
        lax.psum_scatter(bias_sum, "fsdp", scatter_dimension=0, tiled=True),
    )
    gain_one_sum, shift_one_sum, mix_sum, mix_bias_sum, dense_sum, dense_bias_sum = attention_grads
    (
        gain_one_sum,
        shift_one_sum,
        mix_sum,
        mix_bias_sum,
        dense_sum,
        dense_bias_sum,
        gain_two_sum,
        shift_two_sum,
        expand_sum,
        expand_bias_sum,
        shrink_sum,
        shrink_bias_sum,
    ) = lax.psum(
        (
            gain_one_sum,
            shift_one_sum,
            mix_sum,
            mix_bias_sum,
            dense_sum,
            dense_bias_sum,
            gain_two_sum,
            shift_two_sum,
            expand_sum,
            expand_bias_sum,
            shrink_sum,
            shrink_bias_sum,
        ),
        "rep",
    )
    input_grad = cot_float + part_one + part_two
    return (
        block_out,
        input_grad,
        gain_one_sum,
        shift_one_sum,
        mix_sum,
        mix_bias_sum,
        dense_sum,
        dense_bias_sum,
        gain_two_sum,
        shift_two_sum,
        expand_sum,
        expand_bias_sum,
        shrink_sum,
        shrink_bias_sum,
    )


TP_REP = 4
TP_FSDP = 8
GROUP = 8
NEAR = (0, 2, 4, 6)
MIX_COLS = 384
HIDDEN = 512
SMALL = 16
LANES = 128
FIRST_ROWS = MIX_COLS + SMALL + HIDDEN
MIX_ROWS = MIX_COLS + SMALL
FEED_ROWS = 2 * HIDDEN
F32 = jnp.float32
BF16 = jnp.bfloat16
VMEM_LIMIT = 56 * 1024 * 1024


def permute(value, target):
    pairs = []
    for rep in range(TP_REP):
        for shard in range(TP_FSDP):
            goal = target(rep // 2, rep % 2, shard // 4, (shard // 2) % 2, shard % 2)
            if goal is not None:
                x, core, high, low, y = goal
                pairs.append((rep * TP_FSDP + shard, (2 * x + core) * TP_FSDP + 4 * high + 2 * low + y))
    return lax.ppermute(value, ("rep", "fsdp"), pairs)


def swap(value, x=0, core=0, high=0, low=0, y=0):
    return permute(value, lambda a, b, c, d, e: (a ^ x, b ^ core, c ^ high, d ^ low, e ^ y))


def nt(left, right):
    return lax.dot_general(left, right, (((1,), (1,)), ((), ())), preferred_element_type=F32)


def nn(left, right):
    return lax.dot_general(left, right, (((1,), (0,)), ((), ())), preferred_element_type=F32)


def tn(left, right):
    return lax.dot_general(left, right, (((0,), (0,)), ((), ())), preferred_element_type=F32)


def whole(shape):
    return pl.BlockSpec(shape, lambda *_: (0,) * len(shape))


def call(body, info, operands, in_specs, outs, out_specs, grid=(1,), scratch=(), aliases=None, micros=4):
    return pl.pallas_call(
        body,
        grid_spec=pltpu.PrefetchScalarGridSpec(
            num_scalar_prefetch=1,
            grid=grid,
            in_specs=in_specs,
            out_specs=out_specs,
            scratch_shapes=list(scratch),
        ),
        out_shape=[jax.ShapeDtypeStruct(shape, dtype) for shape, dtype in outs],
        input_output_aliases=aliases or {},
        compiler_params=pltpu.CompilerParams(vmem_limit_bytes=VMEM_LIMIT),
        cost_estimate=pl.CostEstimate(flops=micros * 10**9, bytes_accessed=micros * 3 * 10**6, transcendentals=0),
    )(info, *operands)


def as_columns(matrix):
    size = matrix.shape[1]
    rows = lax.broadcasted_iota(jnp.int32, (size, size), 0)
    cols = lax.broadcasted_iota(jnp.int32, (size, size), 1)
    return nt((rows == cols).astype(BF16), matrix)


def aligned(index, unit):
    return pl.ds(pl.multiple_of(index * unit, unit), unit)


def cut_body(info, mix, expand, shrink, dense, cot, *rest):
    vectors, (own, other, own_last, other_last, other_shrink), small = rest[:8], rest[8:13], rest[13]
    row = 0
    small[...] = jnp.zeros_like(small)
    for vector in vectors:
        count = vector.shape[0]
        small[row : row + count, :] = vector[...].astype(F32)
        row = row + count if row + count != 6 else 8
    lane = lax.broadcasted_iota(jnp.int32, (LANES, LANES), 1)
    for out, rank in ((own, info[1]), (other, info[1] ^ 2)):
        for part in range(3):
            out[part * LANES : (part + 1) * LANES, :] = mix[:, aligned(8 * part + rank, LANES)]
        out[MIX_COLS:MIX_ROWS, :] = small[...].astype(BF16)
        upper = jnp.bitwise_and(rank, 1) == 1
        for pair in range(4):
            first = expand[:, aligned(8 * pair + rank // 2, LANES)].astype(F32)
            second = expand[:, aligned(8 * pair + 4 + rank // 2, LANES)].astype(F32)
            first = jnp.where(upper, pltpu.roll(first, 64, 1), first)
            second = jnp.where(upper, second, pltpu.roll(second, 64, 1))
            joined = jnp.where(lane < 64, first, second).astype(BF16)
            out[MIX_ROWS + pair * LANES : MIX_ROWS + (pair + 1) * LANES, :] = joined
    rows = cot.shape[0] // 2
    own_last[:64, :] = shrink[aligned(info[1], 64), :]
    own_last[64:, :] = dense[...]
    other_shrink[...] = shrink[aligned(info[1] ^ 2, 64), :]
    other_last[:64, :] = other_shrink[...]
    other_last[64:, :] = cot[rows:, :]


def cut_slices(info, mix, expand, shrink, dense, cot, vectors):
    operands = [mix, expand, shrink, dense, cot] + [vector.reshape(-1, LANES) for vector in vectors]
    width = shrink.shape[1]
    outs = [((FIRST_ROWS, LANES), BF16)] * 2
    outs += [((64 + rows, width), BF16) for rows in (dense.shape[0], cot.shape[0] // 2, 0)]
    return call(
        cut_body,
        info,
        operands,
        [whole(operand.shape) for operand in operands],
        outs,
        [whole(shape) for shape, _ in outs],
        scratch=[pltpu.VMEM((SMALL, LANES), F32)],
    )


def turn(heads, cos, sin, lane):
    ahead = pltpu.roll(heads, LANES - 8, 1)
    behind = pltpu.roll(heads, 8, 1)
    return heads * cos + jnp.where(lane % HEAD < 8, -ahead, behind) * sin


def spread_tables(table, frequency):
    spread = frequency[8:16, :].astype(BF16)
    high = table.astype(BF16)
    low = (table - high.astype(F32)).astype(BF16)
    cos = tn(high[:8], spread) + tn(low[:8], spread) + frequency[16:17, :]
    return cos, tn(high[8:], spread) + tn(low[8:], spread)


def gelu_parts(hidden):
    bell = jnp.exp(hidden * hidden * -0.5)
    point = 1.0 / (1.0 + (0.3275911 * 0.5**0.5) * jnp.abs(hidden))
    series = 1.061405429 * point - 1.453152027
    for factor in (1.421413741, -0.284496736, 0.254829592):
        series = series * point + factor
    tail = 0.5 * series * point * bell
    normal = jnp.where(hidden < 0.0, tail, 1.0 - tail)
    return normal, hidden * bell * ((2.0 * np.pi) ** -0.5)


def near_forward_body(info, inputs, along, across, frequency, *outs):
    mix, expand, vectors, bias = outs[7:]
    shard, rank = info[0], info[1]

    @pl.when(pl.program_id(0) == 0)
    def _():
        for number in range(8):
            piece = (across if number % 2 else along).at[number // 2]
            block = aligned(shard ^ number, LANES)
            for part in range(3):
                mix[block, part * LANES : (part + 1) * LANES] = piece[part * LANES : (part + 1) * LANES, :]
            vectors[:, block] = piece[MIX_COLS:MIX_ROWS, :].astype(F32)
            for pair in range(4):
                start = MIX_ROWS + pair * LANES
                expand[block, pair * LANES : (pair + 1) * LANES] = piece[start : start + LANES, :]
        lane = lax.broadcasted_iota(jnp.int32, (8, LANES), 1)
        upper = jnp.bitwise_and(rank, 1) == 1
        bias[...] = jnp.zeros_like(bias)
        line = lax.broadcasted_iota(jnp.int32, (8, LANES), 0)

        def chosen_row(block, number):
            row = jnp.sum(jnp.where(line == number, block, 0.0), axis=0, keepdims=True)
            return jnp.broadcast_to(row, (8, LANES))

        for pair in range(4):
            one = chosen_row(vectors[8:16, 2 * pair * LANES : (2 * pair + 1) * LANES], 3 + rank // 2)
            two = chosen_row(vectors[8:16, (2 * pair + 1) * LANES : (2 * pair + 2) * LANES], 3 + rank // 2)
            one = jnp.where(upper, pltpu.roll(one, 64, 1), one)
            two = jnp.where(upper, two, pltpu.roll(two, 64, 1))
            joined = jnp.where(lane < 64, one, two)
            bias[0:1, pair * LANES : (pair + 1) * LANES] = joined[0:1, :]
        for part in range(3):
            place = 8 * part + rank
            held = chosen_row(vectors[8:16, aligned(place // 3, LANES)], place % 3)
            bias[1:2, part * LANES : (part + 1) * LANES] = held[0:1, :]

    forward_step(inputs, frequency, mix, expand, vectors, bias, *outs[:7])


def far_forward_body(info, inputs, mix, expand, vectors, bias, frequency, *rest):
    forward_step(inputs, frequency, mix, expand, vectors, bias, *rest[7:])


def forward_step(
    rows, frequency, mix, expand, vectors, bias,
    normed_out, heads_out, tables_out, probs_out, context_out, act_out, slope_out,
):
    tokens = normed_out.shape[1]
    flat = (2 * tokens, normed_out.shape[2])
    rows = rows[...]
    inputs = rows[:, :tokens].reshape(flat).astype(F32)
    average = jnp.mean(inputs, axis=-1, keepdims=True)
    centred = inputs - average
    variance = jnp.mean(centred * centred, axis=-1, keepdims=True)
    normed = centred * lax.rsqrt(variance + EPSILON)
    one = (normed * vectors[0:1, :] + vectors[1:2, :]).astype(BF16)
    two = (normed * vectors[2:3, :] + vectors[3:4, :]).astype(BF16)
    normed_out[...] = normed.astype(BF16).reshape(normed_out.shape)
    mixed = nn(one, mix[...]) + bias[1:2, :MIX_COLS]

    row_index = lax.broadcasted_iota(jnp.int32, (tokens, tokens), 0)
    col_index = lax.broadcasted_iota(jnp.int32, (tokens, tokens), 1)
    lane = lax.broadcasted_iota(jnp.int32, (tokens, LANES), 1)
    for sequence in range(2):
        marks = rows[sequence, tokens : tokens + 16, :tokens].astype(F32)[0:1, :]
        across_marks = jnp.broadcast_to(marks, (tokens, tokens))
        same = across_marks == across_marks.T
        allowed = same & (col_index <= row_index)
        position = jnp.sum(jnp.where(same & (row_index < col_index), 1.0, 0.0), axis=0, keepdims=True)
        phases = jnp.broadcast_to(position, (8, tokens)) * frequency[0:8, 0:1]
        table = jnp.concatenate([jnp.cos(phases), jnp.sin(phases)], axis=0)
        tables_out[sequence] = table
        cos, sin = spread_tables(table, frequency)
        part = mixed[sequence * tokens : (sequence + 1) * tokens]
        queries = turn(part[:, :LANES], cos, sin, lane).astype(BF16)
        keys = turn(part[:, LANES : 2 * LANES], cos, sin, lane).astype(BF16)
        values = part[:, 2 * LANES :].astype(BF16)
        heads_out[sequence, :, :LANES] = queries
        heads_out[sequence, :, LANES : 2 * LANES] = keys
        heads_out[sequence, :, 2 * LANES :] = values
        context = jnp.zeros((tokens, LANES), F32)
        for head in range(2):
            chosen = lane // HEAD == head
            scores = nt(jnp.where(chosen, queries, 0).astype(BF16), keys) * HEAD ** (-0.5)
            scores = jnp.where(allowed, scores, -1e30)
            weights = jnp.exp(scores - jnp.max(scores, axis=-1, keepdims=True))
            probs = weights * (1.0 / jnp.sum(weights, axis=-1, keepdims=True))
            probs_out[sequence, head] = probs
            context = context + nn(probs.astype(BF16), jnp.where(chosen, values, 0).astype(BF16))
        context_out[sequence] = context.astype(BF16)

    hidden = nn(two, expand[...]) + bias[0:1, :]
    normal, slope = gelu_parts(hidden)
    act_out[...] = (hidden * normal).astype(BF16).reshape(act_out.shape)
    slope_out[...] = (normal + slope).reshape(slope_out.shape)


def turn_constants():
    frequency = np.zeros((24, LANES), np.float32)
    powers = np.power(np.float32(10000.0), -2.0 * np.arange(ROT // 2, dtype=np.float32) / np.float32(ROT))
    frequency[0:8, :] = powers[:, None]
    for lane in range(LANES):
        if lane % HEAD < ROT:
            frequency[8 + lane % 8, lane] = 1.0
        else:
            frequency[16, lane] = 1.0
    return frequency


def forward(info, inputs, weights, frequency, tokens, width, held=None):
    far = held is not None
    outs = [
        ((GROUP, tokens, width), BF16),
        ((GROUP, tokens, MIX_COLS), BF16),
        ((GROUP, 2 * 8, tokens), F32),
        ((GROUP, 2, tokens, tokens), F32),
        ((GROUP, tokens, LANES), BF16),
        ((GROUP, tokens, HIDDEN), BF16),
        ((GROUP, tokens, HIDDEN), F32),
    ]
    fixed = [((width, MIX_COLS), BF16), ((width, HIDDEN), BF16), ((SMALL, width), F32), ((8, HIDDEN), F32)]
    operands = [inputs] + list(weights) + [frequency]
    in_specs = [pairs(inputs.shape)] + [whole(operand.shape) for operand in operands[1:]]
    out_specs = [pairs(shape, 2 * far) for shape, _ in outs]
    if far:
        aliases = {1 + len(operands) + number: number for number in range(len(outs))}
        in_specs += [pl.BlockSpec(memory_space=pl.ANY)] * len(outs)
        return call(
            far_forward_body, info, operands + list(held), in_specs, outs, out_specs, grid=(2,), aliases=aliases, micros=10
        )
    out_specs += [whole(shape) for shape, _ in fixed]
    return call(near_forward_body, info, operands, in_specs, outs + fixed, out_specs, grid=(2,), micros=10)


def pairs(shape, first=0):
    rest = (0,) * (len(shape) - 1)
    return pl.BlockSpec((2,) + shape[1:], lambda i, _: (i + first,) + rest)


def far_project_body(info, context, act, dense, along, across, out, shrink):
    @pl.when(pl.program_id(0) == 0)
    def _():
        for number in range(8):
            piece = across if number % 2 else along
            start = 64 * (number // 2)
            shrink[aligned(info[0] ^ number, 64), :] = piece[start : start + 64, :]

    near_project_body(info, context, act, dense, shrink, out)


def near_project_body(info, context, act, dense, shrink, out):
    rows = 2 * context.shape[1]
    total = nn(context[...].reshape(rows, LANES), dense[...]) + nn(act[...].reshape(rows, HIDDEN), shrink[...])
    out[...] = total.astype(BF16).reshape(out.shape)


def project(info, context, act, dense, shrink, far):
    tokens, width = context.shape[1], dense.shape[1]
    operands = [context, act, dense] + (list(shrink) if far else [shrink])
    in_specs = [pairs(context.shape, 2 * far), pairs(act.shape, 2 * far)]
    in_specs += [whole(operand.shape) for operand in operands[2:]]
    outs = [((4, tokens, width), BF16)] + [((HIDDEN, width), BF16)] * far
    out_specs = [pairs(outs[0][0])] + [whole((HIDDEN, width))] * far
    body = far_project_body if far else near_project_body
    return call(body, info, operands, in_specs, outs, out_specs, grid=(2,), micros=5)


def halves(near, far):
    block = (2,) + near.shape[1:]
    return [
        pl.BlockSpec(block, lambda i, _: (jnp.minimum(i, 1), 0, 0)),
        pl.BlockSpec(block, lambda i, _: (jnp.maximum(i - 2, 0), 0, 0)),
    ]


def chosen_half(near, far):
    rows = jnp.where(pl.program_id(0) < 2, near[...], far[...])
    return rows.reshape(rows.shape[0] * rows.shape[1], rows.shape[2])


def flat(ref):
    return ref[...].reshape(ref.shape[0] * ref.shape[1], ref.shape[2])


def clear(*refs):
    @pl.when(pl.program_id(0) == 0)
    def _():
        for ref in refs:
            ref[...] = jnp.zeros_like(ref)


def each_shard(info, mine, other):
    unit = mine.shape[0] // 4
    for place, z in enumerate((1, 0, 3, 2)):
        rows = pl.ds(place * unit, unit)
        yield info[0] ^ (2 * z), mine.at[rows]
        yield info[0] ^ (2 * z + 1), other.at[rows]


def last_grad_body(info, near, far, act, context, mine, other, total, dense_total):
    clear(total, dense_total)
    cot = chosen_half(near, far)
    total[...] += tn(flat(act), cot)
    dense_total[...] += tn(flat(context), cot)

    @pl.when(pl.program_id(0) == 3)
    def _():
        shrink_rows = 4 * HIDDEN
        for shard, out in each_shard(info, mine.at[:shrink_rows], other.at[:shrink_rows]):
            for part in range(8):
                rows = total[aligned(shard, 64), part * LANES : (part + 1) * LANES]
                out[64 * part : 64 * (part + 1), :] = rows.astype(BF16)
        for part in range(8):
            start = shrink_rows + LANES * part
            block = dense_total[:, part * LANES : (part + 1) * LANES].astype(BF16)
            mine[start : start + LANES, :] = block
            other[start : start + LANES, :] = block


def last_backward(info, near, far, act, context):
    width = near.shape[2]
    outs = [((4 * HIDDEN + width, LANES), BF16)] * 2
    return call(
        last_grad_body,
        info,
        [near, far, act, context],
        halves(near, far) + [pairs(act.shape), pairs(context.shape)],
        outs,
        [whole(shape) for shape, _ in outs],
        grid=(4,),
        scratch=[pltpu.VMEM((HIDDEN, width), F32), pltpu.VMEM((LANES, width), F32)],
        micros=8,
    )


def norm_products(total, column, weight, gain, shift):
    lines = as_columns(weight)
    column = column[:, 0:1]
    grad = total * gain + column * shift
    return grad, jnp.sum(lines * total, axis=0, keepdims=True), jnp.sum(lines * column, axis=0, keepdims=True)


def expand_grad_body(
    info, near, far, slope, normed, shrink, expand, vectors, pre_out, bias_out, sums, mine, other, total, column
):
    clear(total, column, bias_out, sums)
    grad_act = nt(chosen_half(near, far), shrink[...])
    grad_pre = (grad_act * flat(slope)).astype(BF16)
    pre_out[...] = grad_pre.reshape(pre_out.shape)
    bias_out[...] += jnp.broadcast_to(jnp.sum(grad_pre.astype(F32), axis=0, keepdims=True), bias_out.shape)
    total[...] += tn(grad_pre, flat(normed))
    column[...] += tn(grad_pre, jnp.ones((grad_pre.shape[0], LANES), BF16))

    @pl.when(pl.program_id(0) == 3)
    def _():
        grad, sums[0:1, :], sums[1:2, :] = norm_products(
            total[...], column, expand[...], vectors[2:3, :], vectors[3:4, :]
        )
        total[...] = grad
        for shard, out in each_shard(info, mine, other):
            out[...] = total[:, aligned(shard, LANES)].astype(BF16)


def expand_backward(info, near, far, slope, normed, shrink, expand, vectors):
    tokens, width = near.shape[1:]
    operands = [near, far, slope, normed, shrink, expand, vectors]
    in_specs = halves(near, far) + [pairs(slope.shape), pairs(normed.shape)]
    in_specs += [whole(operand.shape) for operand in operands[4:]]
    outs = [((GROUP, tokens, HIDDEN), BF16), ((8, HIDDEN), F32), ((8, width), F32)] + [((4 * HIDDEN, LANES), BF16)] * 2
    out_specs = [pairs(outs[0][0])] + [whole(shape) for shape, _ in outs[1:]]
    scratch = [pltpu.VMEM((HIDDEN, width), F32), pltpu.VMEM((HIDDEN, LANES), F32)]
    return call(expand_grad_body, info, operands, in_specs, outs, out_specs, grid=(4,), scratch=scratch, micros=12)


def attention_grad_body(
    info, near, far, normed, heads, tables, probs, dense, mix, vectors, bias_grad, feed_sums, frequency,
    mixed_out, mine, other, total, column, sums, piece,
):
    step = pl.program_id(0)
    rank = info[1]
    tokens = near.shape[1]
    clear(total, column, sums)
    cot = chosen_half(near, far)
    lane = lax.broadcasted_iota(jnp.int32, (tokens, LANES), 1)
    grad_context = nt(cot, dense[...]).astype(BF16)
    grad_mixed = []
    for sequence in range(2):
        queries = heads[sequence, :, :LANES]
        keys = heads[sequence, :, LANES : 2 * LANES]
        values = heads[sequence, :, 2 * LANES :]
        grad_queries = jnp.zeros((tokens, LANES), F32)
        grad_keys = jnp.zeros((tokens, LANES), F32)
        grad_values = jnp.zeros((tokens, LANES), F32)
        for head in range(2):
            chosen = lane // HEAD == head
            exact = probs[sequence, head]
            part = grad_context[sequence * tokens : (sequence + 1) * tokens]
            part = jnp.where(chosen, part, 0).astype(BF16)
            grad_probs = nt(part, values)
            grad_scores = exact * (grad_probs - jnp.sum(exact * grad_probs, axis=-1, keepdims=True))
            grad_scores = grad_scores.astype(BF16)
            grad_values = grad_values + tn(exact.astype(BF16), part)
            grad_queries = grad_queries + nn(grad_scores, jnp.where(chosen, keys, 0).astype(BF16))
            grad_keys = grad_keys + tn(grad_scores, jnp.where(chosen, queries, 0).astype(BF16))
        cos, sin = spread_tables(tables[sequence], frequency)
        joined = [
            turn(grad_queries * HEAD ** (-0.5), cos, -sin, lane),
            turn(grad_keys * HEAD ** (-0.5), cos, -sin, lane),
            grad_values,
        ]
        grad_mixed.append(jnp.concatenate(joined, axis=1).astype(BF16))
    grad_mixed = jnp.concatenate(grad_mixed, axis=0)
    mixed_out[...] = grad_mixed.reshape(mixed_out.shape)
    total[...] += tn(grad_mixed, flat(normed))
    column[...] += tn(grad_mixed, jnp.ones((grad_mixed.shape[0], LANES), BF16))
    sums[5:6, :MIX_COLS] += jnp.sum(grad_mixed.astype(F32), axis=0, keepdims=True)

    @pl.when(step == 0)
    def _():
        sums[4:5, :] = jnp.sum(near[0].astype(F32), axis=0, keepdims=True)

    @pl.when(step == 3)
    def _():
        grad, sums[0:1, :], sums[1:2, :] = norm_products(
            total[...], column, mix[...], vectors[0:1, :], vectors[1:2, :]
        )
        total[...] = grad
        sums[2:4, :] = feed_sums[0:2, :]
        line = lax.broadcasted_iota(jnp.int32, (8, LANES), 1)
        for shard, out in each_shard(info, mine, other):
            block = aligned(shard, LANES)
            out[:MIX_COLS, :] = total[:, block].astype(BF16)
            piece[...] = jnp.zeros_like(piece)
            piece[0:5, :] = sums[0:5, block]
            for row in range(3):
                place = 3 * shard + row
                spread = jnp.zeros((1, LANES), F32)
                for part in range(3):
                    held = sums[5:6, part * LANES : (part + 1) * LANES]
                    spread = spread + jnp.where(place == 8 * part + rank, held, 0.0)
                piece[5 + row : 6 + row, :] = spread
            packed = bias_grad[:, aligned(shard // 2, LANES)]
            moved = jnp.where(jnp.bitwise_and(shard ^ rank, 1) == 1, pltpu.roll(packed, 64, 1), packed)
            moved = jnp.where(line // 64 == jnp.bitwise_and(rank, 1), moved, 0.0)
            for row in range(4):
                piece[8 + row : 9 + row, :] = jnp.where(rank // 2 == row, moved[0:1, :], 0.0)
            out[MIX_COLS:, :] = piece[...].astype(BF16)


def attention_backward(info, near, far, saved, dense, fixed):
    tokens, width = near.shape[1:]
    operands = [near, far] + list(saved) + [dense] + list(fixed)
    in_specs = halves(near, far) + [pairs(operand.shape) for operand in saved]
    in_specs += [whole(operand.shape) for operand in operands[2 + len(saved) :]]
    outs = [((GROUP, tokens, MIX_COLS), BF16)] + [((4 * MIX_ROWS, LANES), BF16)] * 2
    out_specs = [pairs(outs[0][0])] + [whole(shape) for shape, _ in outs[1:]]
    scratch = [
        pltpu.VMEM((MIX_COLS, width), F32),
        pltpu.VMEM((MIX_COLS, LANES), F32),
        pltpu.VMEM((8, width), F32),
        pltpu.VMEM((SMALL, LANES), F32),
    ]
    return call(attention_grad_body, info, operands, in_specs, outs, out_specs, grid=(4,), scratch=scratch, micros=14)


def input_grad_body(info, mixed, pre, mix, expand, vectors, out):
    total = nt(flat(mixed), mix[...]) * vectors[0:1, :] + nt(flat(pre), expand[...]) * vectors[2:3, :]
    out[...] = total.astype(BF16).reshape(out.shape)


def input_backward(info, mixed, pre, mix, expand, vectors, far):
    tokens, width = mixed.shape[1], mix.shape[0]
    operands = [mixed, pre, mix, expand, vectors]
    in_specs = [pairs(mixed.shape, 2 * far), pairs(pre.shape, 2 * far)]
    in_specs += [whole(operand.shape) for operand in operands[2:]]
    shape = (4, tokens, width)
    return call(input_grad_body, info, operands, in_specs, [(shape, BF16)], [pairs(shape)], grid=(2,), micros=6)[0]


def norm_body(info, block, cot, upstream, out):
    inputs = block[...].astype(F32)
    average = jnp.mean(inputs, axis=-1, keepdims=True)
    centred = inputs - average
    scale = lax.rsqrt(jnp.mean(centred * centred, axis=-1, keepdims=True) + EPSILON)
    normed = centred * scale
    pulled = upstream[...]
    pulled = pulled - jnp.mean(pulled, axis=-1, keepdims=True) - normed * jnp.mean(pulled * normed, axis=-1, keepdims=True)
    out[...] = cot[...].astype(F32) + scale * pulled


def each_rank(near, far, unit):
    for place, number in enumerate(NEAR):
        rows = pl.ds(place * unit, unit)
        yield number, near.at[rows], far.at[rows]


def expand_out_body(info, near, far, out):
    rank = info[1]
    upper = jnp.bitwise_and(rank, 1) == 1
    for number, one, two in each_rank(near, far, HIDDEN):
        place = (rank ^ number) // 2
        for shard in range(8):
            rows = slice(64 * shard, 64 * (shard + 1))
            lower_rows = jnp.where(upper, two[rows, :], one[rows, :])
            upper_rows = jnp.where(upper, one[rows, :], two[rows, :])
            joined = jnp.concatenate([lower_rows, upper_rows], axis=0)
            out[:, aligned(4 * shard + place, LANES)] = as_columns(joined)


def last_out_body(info, near, far, own_dense, shrink_out, dense_out):
    rank = info[1]
    for number, one, two in each_rank(near, far, HIDDEN):
        for piece, place in ((one, rank ^ number), (two, rank ^ number ^ 1)):
            for part in range(8):
                rows = piece[64 * part : 64 * (part + 1), :]
                shrink_out[aligned(place, 64), part * LANES : (part + 1) * LANES] = rows.astype(F32)
    for part in range(8):
        start = 4 * HIDDEN + part * LANES
        rows = jnp.where(own_dense[0] == 1, near[start : start + LANES, :], far[start : start + LANES, :])
        dense_out[:, part * LANES : (part + 1) * LANES] = rows.astype(F32)


def mix_out_body(info, near, far, mix_out):
    rank = info[1]
    for number, one, two in each_rank(near, far, MIX_ROWS):
        for piece, place in ((one, rank ^ number), (two, rank ^ number ^ 1)):
            for part in range(3):
                mix_out[:, aligned(8 * part + place, LANES)] = as_columns(piece[part * LANES : (part + 1) * LANES, :])


def after(value, *others):
    return lax.optimization_barrier((value,) + others)[0]


def gather_first(upper, lower):
    return swap(upper, x=1), swap(lower, low=1)


def gather_second(upper, lower, upper_x, lower_low):
    upper_pair = swap(jnp.stack([upper, upper_x]), low=1)
    lower_pair = swap(jnp.stack([lower, lower_low]), x=1)
    return (
        jnp.stack([upper, upper_pair[0], upper_x, upper_pair[1]]),
        jnp.stack([lower, lower_low, lower_pair[0], lower_pair[1]]),
    )


def reduce_first(mine, other, unit):
    got = swap(other, y=1)
    total = mine.astype(F32) + got.astype(F32)
    return total, total[2 * unit :].astype(BF16)


def reduce_second(total, sent, unit):
    kept = jnp.concatenate([total[: 2 * unit], total[4 * unit :]])
    return (kept + swap(sent, high=1).astype(F32)).astype(BF16)


def share_first(slices, unit):
    away, own = slices[:unit], slices[unit:]
    return own, swap(away, low=1), swap(own, x=1), swap(away, x=1, low=1)


def scatter_first(near, far_got):
    cut = near.shape[1] // 2
    total = near.astype(F32) + far_got.astype(F32)
    sent_x = total[2:, :cut].astype(BF16)
    sent_low = total[1::2, cut:].astype(BF16)
    return total[:2, :cut], sent_x, total[0::2, cut:], sent_low


def scatter_second(kept_x, sent_x, kept_low, sent_low):
    upper = kept_x + swap(sent_x, x=1).astype(F32)
    lower = kept_low + swap(sent_low, low=1).astype(F32)
    return upper[0], upper[1].astype(BF16), lower[0], lower[1].astype(BF16)


def scatter_third(upper, sent_upper, lower, sent_lower):
    upper = upper + swap(sent_upper, low=1).astype(F32)
    lower = lower + swap(sent_lower, x=1).astype(F32)
    return jnp.concatenate([upper, lower])


def local(
    block_input,
    segments,
    cotangent,
    first_gain,
    first_shift,
    mix_weight,
    mix_bias,
    dense_weight,
    dense_bias,
    second_gain,
    second_shift,
    expand_weight,
    expand_bias,
    shrink_weight,
    shrink_bias,
):
    rep = lax.axis_index("rep")
    shard = lax.axis_index("fsdp")
    x, core, high, low, y = rep // 2, rep % 2, shard // 4, (shard // 2) % 2, shard % 2
    info = jnp.stack([shard, 4 * x + 2 * low + core]).astype(jnp.int32)
    tokens, width = block_input.shape
    rows = mix_weight.shape[0]

    own_y, own_x = y == core, x == high

    small = (first_gain, first_shift, second_gain, second_shift, dense_bias, shrink_bias, mix_bias, expand_bias)
    cut = tokens // 2
    marks = jnp.pad(segments.astype(BF16), ((0, 15), (0, width - tokens)))
    upper, lower = block_input[:cut], jnp.concatenate([block_input[cut:], marks])
    upper_x, lower_low = gather_first(upper, lower)
    own, other, own_last, other_last, other_shrink = cut_slices(
        info, mix_weight, expand_weight, shrink_weight, dense_weight, cotangent, small
    )
    along = swap(other, low=1), swap(own, high=1), swap(other, high=1, low=1)
    upper_x, lower_low = after((upper_x, lower_low), own)
    near = gather_second(upper, lower, upper_x, lower_low)
    along = jnp.stack((own,) + along)
    across = swap(along, y=1)
    near = jnp.concatenate(after(near, along), axis=1)
    far = swap(near, core=1)

    own_last, other_last, other_shrink, cot_upper = after((own_last, other_last, other_shrink, cotangent[:cut]), near)
    low_last = swap(other_last, low=1)
    high_last = swap(own_last, high=1)
    both_last = swap(other_shrink, high=1, low=1)
    cot_upper_x = swap(cot_upper, x=1)

    frequency = jnp.asarray(turn_constants())
    *saved, mix, expand, vectors, bias = forward(info, near, (along, across), frequency, tokens, width)
    dense_held = jnp.where(own_x, dense_weight, high_last[64:])
    last = jnp.concatenate([own_last[:64], low_last[:64], high_last[:64], both_last, dense_held])
    last = after(last, mix)
    last_across = swap(last, y=1)
    cot_upper_x, cot_lower_low = after((cot_upper_x, low_last[64:]), mix)
    cot_near = gather_second(cot_upper, cotangent[cut:], cot_upper_x, cot_lower_low)
    far = after(far, last, cot_upper_x, cot_lower_low)
    saved = forward(info, far, (mix, expand, vectors, bias), frequency, tokens, width, saved)
    normed, heads, tables, probs, context, act, slope = saved
    last_across = after(last_across, context)
    dense = jnp.where(own_y, dense_held, last_across[256:])
    branch_far, shrink = project(info, context, act, dense, (last, last_across), True)
    branch_got = swap(branch_far, core=1)
    cot_near = jnp.concatenate(after(cot_near, branch_far), axis=1)
    cot_far = swap(cot_near, core=1)
    (branch_near,) = project(info, context, act, dense, after(shrink, cot_near), False)
    branch = scatter_first(branch_near, branch_got)

    cot_near, cot_far = after((cot_near, cot_far), branch[1], branch[3])
    last_mine, last_other = last_backward(info, cot_near, cot_far, act, context)
    grad_pre, bias_grad, feed_sums, expand_mine, expand_other = expand_backward(
        info, cot_near, cot_far, slope, normed, after(shrink, last_mine), expand, vectors
    )
    branch = scatter_second(*branch)
    last_part = reduce_first(last_mine, last_other, HIDDEN)
    saved = (normed, heads, tables, probs)
    fixed = (mix, vectors, bias_grad, feed_sums, frequency)
    grad_mixed, mix_mine, mix_other = attention_backward(
        info, cot_near, cot_far, saved, after(dense, branch[1], branch[3], last_part[1]), fixed
    )
    expand_part = reduce_first(expand_mine, expand_other, HIDDEN)
    last_slices = reduce_second(*last_part, HIDDEN)
    branch = scatter_third(*branch)
    block_out = (block_input.astype(F32) + branch + (vectors[4] + vectors[5])).astype(BF16)
    error_far = input_backward(
        info, after(grad_mixed, expand_part[1], last_slices), grad_pre, mix, expand, vectors, True
    )
    error_got = swap(error_far, core=1)
    own_part, low_part, x_part, both_part = share_first(last_slices, HIDDEN)
    dense_part = jnp.where(own_x, own_part[HIDDEN:], x_part[HIDDEN:])
    last_near = jnp.concatenate([own_part[:HIDDEN], low_part, x_part[:HIDDEN], both_part, dense_part])
    last_far = swap(last_near, core=1)
    error_near = input_backward(
        info, after(grad_mixed, error_far, last_near), grad_pre, mix, expand, vectors, False
    )
    error = scatter_first(error_near, error_got)

    mix_part = reduce_first(mix_mine, mix_other, MIX_ROWS)
    mix_part = after(mix_part, error[1], error[3])
    expand_slices = after(reduce_second(*expand_part, HIDDEN), mix_part[1])
    expand_near = jnp.concatenate(share_first(expand_slices, HIDDEN))
    expand_far = swap(expand_near, core=1)
    mix_slices = reduce_second(*mix_part, MIX_ROWS)
    mix_parts = share_first(mix_slices, MIX_ROWS)
    mix_near = jnp.concatenate(mix_parts)
    mix_sums = [part[MIX_COLS:].astype(F32) for part in mix_parts]
    mix_sums = ((mix_sums[0] + mix_sums[1]) + (mix_sums[2] + mix_sums[3])).astype(BF16)
    mix_near = jnp.concatenate([mix_near, mix_sums])
    mix_far = swap(mix_near, core=1)
    sums = mix_sums.astype(F32) + mix_far[4 * MIX_ROWS :].astype(F32)
    upstream = scatter_third(*scatter_second(*error))

    def out(body, near, far, shapes, flag=None):
        operands = [near, far]
        in_specs = [whole(near.shape), whole(far.shape)]
        if flag is not None:
            operands.append(flag)
            in_specs.append(pl.BlockSpec(memory_space=pltpu.SMEM))
        return call(body, info, operands, in_specs, [(shape, F32) for shape in shapes], [whole(shape) for shape in shapes])

    flag = own_y.astype(jnp.int32).reshape(1)
    shrink_out, dense_out = out(last_out_body, last_near, last_far, [shrink_weight.shape, dense_weight.shape], flag)
    (expand_out,) = out(expand_out_body, expand_near, expand_far, [expand_weight.shape])
    (mix_out,) = out(mix_out_body, mix_near, mix_far, [mix_weight.shape])
    (input_grad,) = call(
        norm_body,
        info,
        [block_input, cotangent, upstream],
        [whole(block_input.shape)] * 3,
        [(block_input.shape, F32)],
        [whole(block_input.shape)],
    )
    return (
        block_out,
        input_grad,
        sums[0],
        sums[1],
        mix_out,
        sums[5:8].reshape(-1),
        dense_out,
        sums[4],
        sums[2],
        sums[3],
        expand_out,
        sums[8:12].reshape(-1),
        shrink_out,
        sums[4],
    )


def solution(mesh):
    tensor_parallel = mesh.shape["rep"] == TP_REP and mesh.shape["fsdp"] == TP_FSDP
    return jax.shard_map(
        local if tensor_parallel else local_general,
        mesh=mesh,
        in_specs=(
            P(("rep", "fsdp"), None),
            P(("rep", "fsdp"), None),
            P(("rep", "fsdp"), None),
            P("fsdp"),
            P("fsdp"),
            P("fsdp", None),
            P("fsdp"),
            P("fsdp", None),
            P("fsdp"),
            P("fsdp"),
            P("fsdp"),
            P("fsdp", None),
            P("fsdp"),
            P("fsdp", None),
            P("fsdp"),
        ),
        out_specs=(
            P(("rep", "fsdp"), None),
            P(("rep", "fsdp"), None),
            P("fsdp"),
            P("fsdp"),
            P("fsdp", None),
            P("fsdp"),
            P("fsdp", None),
            P("fsdp"),
            P("fsdp"),
            P("fsdp"),
            P("fsdp", None),
            P("fsdp"),
            P("fsdp", None),
            P("fsdp"),
        ),
        check_vma=False,
    )
```

```python
import jax
import jax.numpy as jnp
import numpy as np
from jax import lax
from jax.experimental import pallas as pl
from jax.experimental.pallas import tpu as pltpu
from jax.sharding import PartitionSpec as P

HEADS = 16
HEAD = 64
ROT = 16


EPSILON = 1e-05


def layer_norm(inputs, gain_row, shift_row):
    average = jnp.mean(inputs, axis=-1, keepdims=True)
    centred = inputs - average
    variance = jnp.mean(centred * centred, axis=-1, keepdims=True)
    return centred * lax.rsqrt(variance + EPSILON) * gain_row + shift_row


def rotate(heads_in, cos_table, sin_table):
    half_rot = ROT // 2
    first_half = heads_in[..., :half_rot]
    second_half = heads_in[..., half_rot:ROT]
    return jnp.concatenate(
        [
            first_half * cos_table - second_half * sin_table,
            second_half * cos_table + first_half * sin_table,
            heads_in[..., ROT:],
        ],
        axis=-1,
    )


def rotary_tables(segment_row):
    length = segment_row.shape[0]
    same_doc = segment_row[:, None] == segment_row[None, :]
    row_index = lax.broadcasted_iota(jnp.int32, (length, length), 0)
    col_index = lax.broadcasted_iota(jnp.int32, (length, length), 1)
    earlier = jnp.where(same_doc & (col_index < row_index), 1.0, 0.0)
    position = jnp.sum(earlier, axis=-1).astype(jnp.float32)
    allowed = same_doc & (col_index <= row_index)
    frequency = jnp.power(10000.0, -2.0 * jnp.arange(ROT // 2).astype(jnp.float32) / ROT)
    phases = position[:, None] * frequency
    return (jnp.cos(phases)[:, None, :], jnp.sin(phases)[:, None, :], allowed)


def product_left(left, right):
    return lax.dot_general(
        left, right, (((0,), (0,)), ((), ())), preferred_element_type=jnp.float32
    )


def product_right(left, right):
    return lax.dot_general(
        left, right, (((1,), (1,)), ((), ())), preferred_element_type=jnp.float32
    )


def norm_backward(inputs, gain_row, shift_row, upstream):
    _, pullback = jax.vjp(layer_norm, inputs, gain_row, shift_row)
    return pullback(upstream)


def local_general(
    block_input,
    segments,
    cotangent,
    first_gain,
    first_shift,
    mix_weight,
    mix_bias,
    dense_weight,
    dense_bias,
    second_gain,
    second_shift,
    expand_weight,
    expand_bias,
    shrink_weight,
    shrink_bias,
):
    attention_parts = (
        lax.all_gather(first_gain, "fsdp", axis=0, tiled=True),
        lax.all_gather(first_shift, "fsdp", axis=0, tiled=True),
        lax.all_gather(mix_weight, "fsdp", axis=0, tiled=True),
        lax.all_gather(mix_bias, "fsdp", axis=0, tiled=True),
        lax.all_gather(dense_weight, "fsdp", axis=0, tiled=True),
        lax.all_gather(dense_bias, "fsdp", axis=0, tiled=True),
    )
    feed_parts = (
        lax.all_gather(second_gain, "fsdp", axis=0, tiled=True),
        lax.all_gather(second_shift, "fsdp", axis=0, tiled=True),
        lax.all_gather(expand_weight, "fsdp", axis=0, tiled=True),
        lax.all_gather(expand_bias, "fsdp", axis=0, tiled=True),
        lax.all_gather(shrink_weight, "fsdp", axis=0, tiled=True),
        lax.all_gather(shrink_bias, "fsdp", axis=0, tiled=True),
    )
    token_count = block_input.shape[0]
    feature_count = block_input.shape[1]
    score_scale = HEAD ** (-0.5)
    block_float = block_input.astype(jnp.float32)
    cot_float = cotangent.astype(jnp.float32)
    cos_table, sin_table, allowed = rotary_tables(segments[0])
    normed_one = layer_norm(
        block_float, attention_parts[0].astype(jnp.float32), attention_parts[1].astype(jnp.float32)
    ).astype(jnp.bfloat16)
    mixed_rows = jnp.dot(normed_one, attention_parts[2], preferred_element_type=jnp.float32)
    mixed_rows = mixed_rows + attention_parts[3].astype(jnp.float32)
    triple = mixed_rows.reshape(token_count, 3, HEADS, HEAD)
    queries = rotate(triple[:, 0], cos_table, sin_table).astype(jnp.bfloat16)
    keys_all = rotate(triple[:, 1], cos_table, sin_table).astype(jnp.bfloat16)
    values_all = triple[:, 2].astype(jnp.bfloat16)

    def masked_scores():
        raw_scores = (
            jnp.einsum("qhd,khd->hqk", queries, keys_all, preferred_element_type=jnp.float32)
            * score_scale
        )
        return jnp.where(allowed[None], raw_scores, -1e30)

    forward_scores = masked_scores()
    row_peak = jnp.max(forward_scores, axis=-1, keepdims=True)
    weights_raw = jnp.exp(forward_scores - row_peak)
    row_total = jnp.sum(weights_raw, axis=-1, keepdims=True)
    log_total = row_peak + jnp.log(row_total)
    probs_low = (weights_raw / row_total).astype(jnp.bfloat16)
    context = jnp.einsum("hqk,khd->qhd", probs_low, values_all, preferred_element_type=jnp.float32)
    context = context.reshape(token_count, feature_count).astype(jnp.bfloat16)
    attention_branch = jnp.dot(context, attention_parts[4], preferred_element_type=jnp.float32)
    attention_branch = attention_branch + attention_parts[5].astype(jnp.float32)
    normed_two = layer_norm(
        block_float, feed_parts[0].astype(jnp.float32), feed_parts[1].astype(jnp.float32)
    ).astype(jnp.bfloat16)
    hidden_pre = jnp.dot(normed_two, feed_parts[2], preferred_element_type=jnp.float32)
    hidden_pre = hidden_pre + feed_parts[3].astype(jnp.float32)
    hidden_act = jax.nn.gelu(hidden_pre, approximate=False).astype(jnp.bfloat16)
    feedforward_branch = jnp.dot(hidden_act, feed_parts[4], preferred_element_type=jnp.float32)
    feedforward_branch = feedforward_branch + feed_parts[5].astype(jnp.float32)
    block_out = (block_float + attention_branch + feedforward_branch).astype(jnp.bfloat16)
    feed_back = (
        lax.all_gather(second_gain, "fsdp", axis=0, tiled=True),
        lax.all_gather(second_shift, "fsdp", axis=0, tiled=True),
        lax.all_gather(expand_weight, "fsdp", axis=0, tiled=True),
        lax.all_gather(expand_bias, "fsdp", axis=0, tiled=True),
        lax.all_gather(shrink_weight, "fsdp", axis=0, tiled=True),
        lax.all_gather(shrink_bias, "fsdp", axis=0, tiled=True),
    )
    bias_sum = jnp.sum(cot_float, axis=0)
    shrink_grad = product_left(hidden_act, cotangent)
    grad_act = product_right(cotangent, feed_back[4])
    _, gelu_pull = jax.vjp(lambda pre_value: jax.nn.gelu(pre_value, approximate=False), hidden_pre)
    grad_pre = gelu_pull(grad_act)[0].astype(jnp.bfloat16)
    expand_grad = product_left(normed_two, grad_pre)
    expand_bias_grad = jnp.sum(grad_pre.astype(jnp.float32), axis=0)
    grad_normed_two = product_right(grad_pre, feed_back[2])
    part_two, second_gain_grad, second_shift_grad = norm_backward(
        block_float,
        feed_back[0].astype(jnp.float32),
        feed_back[1].astype(jnp.float32),
        grad_normed_two,
    )
    feed_grads = (
        lax.psum_scatter(second_gain_grad, "fsdp", scatter_dimension=0, tiled=True),
        lax.psum_scatter(second_shift_grad, "fsdp", scatter_dimension=0, tiled=True),
        lax.psum_scatter(expand_grad, "fsdp", scatter_dimension=0, tiled=True),
        lax.psum_scatter(expand_bias_grad, "fsdp", scatter_dimension=0, tiled=True),
        lax.psum_scatter(shrink_grad, "fsdp", scatter_dimension=0, tiled=True),
        lax.psum_scatter(bias_sum, "fsdp", scatter_dimension=0, tiled=True),
    )
    gain_two_sum, shift_two_sum, expand_sum, expand_bias_sum, shrink_sum, shrink_bias_sum = (
        feed_grads
    )
    attention_back = (
        lax.all_gather(first_gain, "fsdp", axis=0, tiled=True),
        lax.all_gather(first_shift, "fsdp", axis=0, tiled=True),
        lax.all_gather(mix_weight, "fsdp", axis=0, tiled=True),
        lax.all_gather(mix_bias, "fsdp", axis=0, tiled=True),
        lax.all_gather(dense_weight, "fsdp", axis=0, tiled=True),
        lax.all_gather(dense_bias, "fsdp", axis=0, tiled=True),
    )
    dense_grad = product_left(context, cotangent)
    grad_context = product_right(cotangent, attention_back[4]).astype(jnp.bfloat16)
    grad_context = grad_context.reshape(token_count, HEADS, HEAD)
    grad_values = jnp.einsum(
        "hqk,qhd->khd", probs_low, grad_context, preferred_element_type=jnp.float32
    )
    grad_probs = jnp.einsum(
        "qhd,khd->hqk", grad_context, values_all, preferred_element_type=jnp.float32
    )
    probs_exact = jnp.exp(masked_scores() - log_total)
    grad_scores = probs_exact * (
        grad_probs - jnp.sum(probs_exact * grad_probs, axis=-1, keepdims=True)
    )
    grad_scores = grad_scores.astype(jnp.bfloat16)
    grad_queries = (
        jnp.einsum("hqk,khd->qhd", grad_scores, keys_all, preferred_element_type=jnp.float32)
        * score_scale
    )
    grad_keys = (
        jnp.einsum("hqk,qhd->khd", grad_scores, queries, preferred_element_type=jnp.float32)
        * score_scale
    )
    _, rotate_pull = jax.vjp(lambda heads_in: rotate(heads_in, cos_table, sin_table), grad_queries)
    grad_mixed = jnp.stack(
        [rotate_pull(grad_queries)[0], rotate_pull(grad_keys)[0], grad_values], axis=1
    )
    grad_mixed = grad_mixed.reshape(token_count, 3 * feature_count).astype(jnp.bfloat16)
    mix_grad = product_left(normed_one, grad_mixed)
    mix_bias_grad = jnp.sum(grad_mixed.astype(jnp.float32), axis=0)
    grad_normed_one = product_right(grad_mixed, attention_back[2])
    part_one, first_gain_grad, first_shift_grad = norm_backward(
        block_float,
        attention_back[0].astype(jnp.float32),
        attention_back[1].astype(jnp.float32),
        grad_normed_one,
    )
    attention_grads = (
        lax.psum_scatter(first_gain_grad, "fsdp", scatter_dimension=0, tiled=True),
        lax.psum_scatter(first_shift_grad, "fsdp", scatter_dimension=0, tiled=True),
        lax.psum_scatter(mix_grad, "fsdp", scatter_dimension=0, tiled=True),
        lax.psum_scatter(mix_bias_grad, "fsdp", scatter_dimension=0, tiled=True),
        lax.psum_scatter(dense_grad, "fsdp", scatter_dimension=0, tiled=True),
        lax.psum_scatter(bias_sum, "fsdp", scatter_dimension=0, tiled=True),
    )
    gain_one_sum, shift_one_sum, mix_sum, mix_bias_sum, dense_sum, dense_bias_sum = attention_grads
    (
        gain_one_sum,
        shift_one_sum,
        mix_sum,
        mix_bias_sum,
        dense_sum,
        dense_bias_sum,
        gain_two_sum,
        shift_two_sum,
        expand_sum,
        expand_bias_sum,
        shrink_sum,
        shrink_bias_sum,
    ) = lax.psum(
        (
            gain_one_sum,
            shift_one_sum,
            mix_sum,
            mix_bias_sum,
            dense_sum,
            dense_bias_sum,
            gain_two_sum,
            shift_two_sum,
            expand_sum,
            expand_bias_sum,
            shrink_sum,
            shrink_bias_sum,
        ),
        "rep",
    )
    input_grad = cot_float + part_one + part_two
    return (
        block_out,
        input_grad,
        gain_one_sum,
        shift_one_sum,
        mix_sum,
        mix_bias_sum,
        dense_sum,
        dense_bias_sum,
        gain_two_sum,
        shift_two_sum,
        expand_sum,
        expand_bias_sum,
        shrink_sum,
        shrink_bias_sum,
    )


TP_REP = 4
TP_FSDP = 8
GROUP = 8
NEAR = (0, 2, 4, 6)
MIX_COLS = 384
HIDDEN = 512
SMALL = 16
LANES = 128
FIRST_ROWS = MIX_COLS + SMALL + HIDDEN
MIX_ROWS = MIX_COLS + SMALL
FEED_ROWS = 2 * HIDDEN
F32 = jnp.float32
BF16 = jnp.bfloat16
COST = 4000
VMEM_LIMIT = 18 * 1024 * 1024
VMEM_FIRST = 36 * 1024 * 1024
VMEM_WHOLE = 56 * 1024 * 1024


def permute(value, target):
    pairs = []
    for rep in range(TP_REP):
        for shard in range(TP_FSDP):
            goal = target(rep // 2, rep % 2, shard // 4, (shard // 2) % 2, shard % 2)
            if goal is not None:
                x, core, high, low, y = goal
                pairs.append((rep * TP_FSDP + shard, (2 * x + core) * TP_FSDP + 4 * high + 2 * low + y))
    return lax.ppermute(value, ("rep", "fsdp"), pairs)


def swap(value, x=0, core=0, high=0, low=0, y=0):
    return permute(value, lambda a, b, c, d, e: (a ^ x, b ^ core, c ^ high, d ^ low, e ^ y))


def nt(left, right):
    return lax.dot_general(left, right, (((1,), (1,)), ((), ())), preferred_element_type=F32)


def nn(left, right):
    return lax.dot_general(left, right, (((1,), (0,)), ((), ())), preferred_element_type=F32)


def tn(left, right):
    return lax.dot_general(left, right, (((0,), (0,)), ((), ())), preferred_element_type=F32)


def whole(shape):
    return pl.BlockSpec(shape, lambda *_: (0,) * len(shape))


def call(body, info, operands, in_specs, outs, out_specs, grid=(1,), scratch=(), micros=4, vmem=VMEM_LIMIT):
    return pl.pallas_call(
        body,
        grid_spec=pltpu.PrefetchScalarGridSpec(
            num_scalar_prefetch=1,
            grid=grid,
            in_specs=in_specs,
            out_specs=out_specs,
            scratch_shapes=list(scratch),
        ),
        out_shape=[jax.ShapeDtypeStruct(shape, dtype) for shape, dtype in outs],
        compiler_params=pltpu.CompilerParams(vmem_limit_bytes=vmem),
        cost_estimate=pl.CostEstimate(flops=micros * COST * 10**6, bytes_accessed=micros * COST * 3 * 10**3, transcendentals=0),
    )(info, *operands)


def as_columns(matrix):
    size = matrix.shape[1]
    rows = lax.broadcasted_iota(jnp.int32, (size, size), 0)
    cols = lax.broadcasted_iota(jnp.int32, (size, size), 1)
    return nt((rows == cols).astype(BF16), matrix)


def aligned(index, unit):
    return pl.ds(pl.multiple_of(index * unit, unit), unit)


def cut_body(info, mix, expand, *rest):
    vectors, (own, other), small = rest[:8], rest[8:10], rest[10]
    row = 0
    small[...] = jnp.zeros_like(small)
    for vector in vectors:
        count = vector.shape[0]
        small[row : row + count, :] = vector[...].astype(F32)
        row = row + count if row + count != 6 else 8
    lane = lax.broadcasted_iota(jnp.int32, (LANES, LANES), 1)
    for out, rank in ((own, info[1]), (other, info[1] ^ 2)):
        for part in range(3):
            out[part * LANES : (part + 1) * LANES, :] = mix[:, aligned(8 * part + rank, LANES)]
        out[MIX_COLS:MIX_ROWS, :] = small[...].astype(BF16)
        upper = jnp.bitwise_and(rank, 1) == 1
        for pair in range(4):
            first = expand[:, aligned(8 * pair + rank // 2, LANES)].astype(F32)
            second = expand[:, aligned(8 * pair + 4 + rank // 2, LANES)].astype(F32)
            first = jnp.where(upper, pltpu.roll(first, 64, 1), first)
            second = jnp.where(upper, second, pltpu.roll(second, 64, 1))
            joined = jnp.where(lane < 64, first, second).astype(BF16)
            out[MIX_ROWS + pair * LANES : MIX_ROWS + (pair + 1) * LANES, :] = joined

def cut_slices(info, mix, expand, vectors):
    operands = [mix, expand] + [vector.reshape(-1, LANES) for vector in vectors]
    outs = [((FIRST_ROWS, LANES), BF16)] * 2
    return call(
        cut_body,
        info,
        operands,
        [whole(operand.shape) for operand in operands],
        outs,
        [whole(shape) for shape, _ in outs],
        scratch=[pltpu.VMEM((SMALL, LANES), F32)],
        vmem=VMEM_WHOLE,
    )


def cut_last_body(info, shrink, dense, cot, own, other, other_shrink):
    rows = cot.shape[0] // 2
    own[:64, :] = shrink[aligned(info[1], 64), :]
    own[64:, :] = dense[...]
    rest = shrink[aligned(info[1] ^ 2, 64), :]
    other_shrink[...] = rest
    other[:64, :] = rest
    other[64:, :] = cot[rows:, :]


def cut_last(info, shrink, dense, cot):
    operands = [shrink, dense, cot]
    shapes = [(64 + rows, shrink.shape[1]) for rows in (dense.shape[0], cot.shape[0] // 2, 0)]
    return call(
        cut_last_body,
        info,
        operands,
        [whole(operand.shape) for operand in operands],
        [(shape, BF16) for shape in shapes],
        [whole(shape) for shape in shapes],
        vmem=VMEM_WHOLE,
    )


def pack_body(info, own, low, high, both, dense, out, dense_high):
    out[:64, :] = own[:64, :]
    out[64:128, :] = low[:64, :]
    out[128:192, :] = high[:64, :]
    out[192:256, :] = both[...]
    same = info[1] // 4 == info[0] // 4
    out[256:, :] = jnp.where(same, dense[...], high[64:, :])
    dense_high[...] = out[256:, :]


def pack_last(info, own, low, high, both, dense):
    operands = [own, low, high, both, dense]
    shapes = [(256 + dense.shape[0], dense.shape[1]), dense.shape]
    return call(
        pack_body,
        info,
        operands,
        [whole(operand.shape) for operand in operands],
        [(shape, BF16) for shape in shapes],
        [whole(shape) for shape in shapes],
    )


def turn(heads, cos, sin, lane):
    ahead = pltpu.roll(heads, LANES - 8, 1)
    behind = pltpu.roll(heads, 8, 1)
    return heads * cos + jnp.where(lane % HEAD < 8, -ahead, behind) * sin


def spread_tables(table, frequency):
    spread = frequency[8:16, :].astype(BF16)
    high = table.astype(BF16)
    low = (table - high.astype(F32)).astype(BF16)
    cos = tn(high[:8], spread) + tn(low[:8], spread) + frequency[16:17, :]
    return cos, tn(high[8:], spread) + tn(low[8:], spread)


def gelu_parts(hidden):
    normal = 0.5 + 0.5 * lax.erf(hidden * (0.5**0.5))
    return normal, hidden * jnp.exp(hidden * hidden * -0.5) * ((2.0 * np.pi) ** -0.5)


def by_head(rows, lane):
    return jnp.concatenate([jnp.where(lane < HEAD, rows, 0), jnp.where(lane < HEAD, 0, rows)]).astype(BF16)


def from_heads(rows, lane):
    tokens = rows.shape[0] // 2
    return jnp.where(lane < HEAD, rows[:tokens], rows[tokens:])


def near_forward_body(info, inputs, own, over, along, across, frequency, *outs):
    mix, expand, vectors, bias = outs[7:]
    shard, rank = info[0], info[1]

    @pl.when(pl.program_id(0) == 0)
    def _():
        for number in range(8):
            if number < 2:
                piece = over if number else own
            else:
                piece = (across if number % 2 else along).at[number // 2 - 1]
            block = aligned(shard ^ number, LANES)
            for part in range(3):
                mix[block, part * LANES : (part + 1) * LANES] = piece[part * LANES : (part + 1) * LANES, :]
            vectors[:, block] = piece[MIX_COLS:MIX_ROWS, :].astype(F32)
            for pair in range(4):
                start = MIX_ROWS + pair * LANES
                expand[block, pair * LANES : (pair + 1) * LANES] = piece[start : start + LANES, :]
        lane = lax.broadcasted_iota(jnp.int32, (8, LANES), 1)
        upper = jnp.bitwise_and(rank, 1) == 1
        bias[...] = jnp.zeros_like(bias)
        line = lax.broadcasted_iota(jnp.int32, (8, LANES), 0)

        def chosen_row(block, number):
            row = jnp.sum(jnp.where(line == number, block, 0.0), axis=0, keepdims=True)
            return jnp.broadcast_to(row, (8, LANES))

        for pair in range(4):
            one = chosen_row(vectors[8:16, 2 * pair * LANES : (2 * pair + 1) * LANES], 3 + rank // 2)
            two = chosen_row(vectors[8:16, (2 * pair + 1) * LANES : (2 * pair + 2) * LANES], 3 + rank // 2)
            one = jnp.where(upper, pltpu.roll(one, 64, 1), one)
            two = jnp.where(upper, two, pltpu.roll(two, 64, 1))
            joined = jnp.where(lane < 64, one, two)
            bias[0:1, pair * LANES : (pair + 1) * LANES] = joined[0:1, :]
        for part in range(3):
            place = 8 * part + rank
            held = chosen_row(vectors[8:16, aligned(place // 3, LANES)], place % 3)
            bias[1:2, part * LANES : (part + 1) * LANES] = held[0:1, :]

    forward_step(inputs, frequency, mix, expand, vectors, bias, *outs[:7])


def far_forward_body(info, inputs, mix, expand, vectors, bias, frequency, *outs):
    forward_step(inputs, frequency, mix, expand, vectors, bias, *outs)


def forward_step(
    rows, frequency, mix, expand, vectors, bias,
    normed_out, heads_out, tables_out, probs_out, context_out, act_out, slope_out,
):
    tokens = normed_out.shape[1]
    flat = (2 * tokens, normed_out.shape[2])
    rows = rows[...]
    inputs = rows[:, :tokens].reshape(flat).astype(F32)
    average = jnp.mean(inputs, axis=-1, keepdims=True)
    centred = inputs - average
    variance = jnp.mean(centred * centred, axis=-1, keepdims=True)
    normed = centred * lax.rsqrt(variance + EPSILON)
    one = (normed * vectors[0:1, :] + vectors[1:2, :]).astype(BF16)
    two = (normed * vectors[2:3, :] + vectors[3:4, :]).astype(BF16)
    normed_out[...] = normed.astype(BF16).reshape(normed_out.shape)
    mixed = nn(one, mix[...]) + bias[1:2, :MIX_COLS]

    row_index = lax.broadcasted_iota(jnp.int32, (tokens, tokens), 0)
    col_index = lax.broadcasted_iota(jnp.int32, (tokens, tokens), 1)
    lane = lax.broadcasted_iota(jnp.int32, (tokens, LANES), 1)
    for sequence in range(2):
        marks = rows[sequence, tokens : tokens + 16, :tokens].astype(F32)[0:1, :]
        across_marks = jnp.broadcast_to(marks, (tokens, tokens))
        same = across_marks == across_marks.T
        allowed = same & (col_index <= row_index)
        position = jnp.sum(jnp.where(same & (row_index < col_index), 1.0, 0.0), axis=0, keepdims=True)
        phases = jnp.broadcast_to(position, (8, tokens)) * frequency[0:8, 0:1]
        table = jnp.concatenate([jnp.cos(phases), jnp.sin(phases)], axis=0)
        tables_out[sequence] = table
        cos, sin = spread_tables(table, frequency)
        part = mixed[sequence * tokens : (sequence + 1) * tokens]
        queries = turn(part[:, :LANES], cos, sin, lane).astype(BF16)
        keys = turn(part[:, LANES : 2 * LANES], cos, sin, lane).astype(BF16)
        values = part[:, 2 * LANES :].astype(BF16)
        heads_out[sequence, :, :LANES] = queries
        heads_out[sequence, :, LANES : 2 * LANES] = keys
        heads_out[sequence, :, 2 * LANES :] = values
        scores = nt(by_head(queries * HEAD ** (-0.5), lane), keys)
        scores = jnp.where(jnp.concatenate([allowed, allowed]), scores, -1e30)
        weights = jnp.exp(scores - jnp.max(scores, axis=-1, keepdims=True))
        probs = weights * (1.0 / jnp.sum(weights, axis=-1, keepdims=True))
        probs = probs.astype(BF16)
        probs_out[sequence] = probs.reshape(2, tokens, tokens)
        context_out[sequence] = from_heads(nn(probs, values), lane).astype(BF16)

    hidden = nn(two, expand[...]) + bias[0:1, :]
    normal, slope = gelu_parts(hidden)
    act_out[...] = (hidden * normal).astype(BF16).reshape(act_out.shape)
    slope_out[...] = (normal + slope).astype(BF16).reshape(slope_out.shape)


def turn_constants():
    frequency = np.zeros((24, LANES), np.float32)
    powers = np.power(np.float32(10000.0), -2.0 * np.arange(ROT // 2, dtype=np.float32) / np.float32(ROT))
    frequency[0:8, :] = powers[:, None]
    for lane in range(LANES):
        if lane % HEAD < ROT:
            frequency[8 + lane % 8, lane] = 1.0
        else:
            frequency[16, lane] = 1.0
    return frequency


def forward(info, inputs, weights, frequency, tokens, width, far=False):
    count = inputs.shape[0]
    outs = [
        ((count, tokens, width), BF16),
        ((count, tokens, MIX_COLS), BF16),
        ((count, 2 * 8, tokens), F32),
        ((count, 2, tokens, tokens), BF16),
        ((count, tokens, LANES), BF16),
        ((count, tokens, HIDDEN), BF16),
        ((count, tokens, HIDDEN), BF16),
    ]
    fixed = [((width, MIX_COLS), BF16), ((width, HIDDEN), BF16), ((SMALL, width), F32), ((8, HIDDEN), F32)]
    operands = [inputs] + list(weights) + [frequency]
    in_specs = [pairs(inputs.shape)] + [whole(operand.shape) for operand in operands[1:]]
    out_specs = [pairs(shape) for shape, _ in outs]
    if far:
        return call(far_forward_body, info, operands, in_specs, outs, out_specs, grid=(2,), micros=9)
    out_specs += [whole(shape) for shape, _ in fixed]
    return call(
        near_forward_body, info, operands, in_specs, outs + fixed, out_specs, grid=(2,), micros=9, vmem=VMEM_FIRST
    )


def pairs(shape, first=0):
    rest = (0,) * (len(shape) - 1)
    return pl.BlockSpec((2,) + shape[1:], lambda i, _: (i + first,) + rest)


def far_project_body(info, context, act, dense, along, across, out, shrink):
    @pl.when(pl.program_id(0) == 0)
    def _():
        for number in range(8):
            piece = across if number % 2 else along
            start = 64 * (number // 2)
            shrink[aligned(info[0] ^ number, 64), :] = piece[start : start + 64, :]

    near_project_body(info, context, act, dense, shrink, out)


def near_project_body(info, context, act, dense, shrink, out):
    rows = 2 * context.shape[1]
    total = nn(context[...].reshape(rows, LANES), dense[...]) + nn(act[...].reshape(rows, HIDDEN), shrink[...])
    out[...] = total.astype(BF16).reshape(out.shape)


def project(info, context, act, dense, shrink, far):
    tokens, width = context.shape[1], dense.shape[1]
    operands = [context, act, dense] + (list(shrink) if far else [shrink])
    in_specs = [pairs(context.shape), pairs(act.shape)]
    in_specs += [whole(operand.shape) for operand in operands[2:]]
    outs = [((4, tokens, width), BF16)] + [((HIDDEN, width), BF16)] * far
    out_specs = [pairs(outs[0][0])] + [whole((HIDDEN, width))] * far
    body = far_project_body if far else near_project_body
    return call(body, info, operands, in_specs, outs, out_specs, grid=(2,), micros=5)


def flat(ref):
    return ref[...].reshape(ref.shape[0] * ref.shape[1], ref.shape[2])


def clear(*refs):
    @pl.when(pl.program_id(0) == 0)
    def _():
        for ref in refs:
            ref[...] = jnp.zeros_like(ref)


def each_shard(info, mine, other):
    unit = mine.shape[0] // 4
    for place, z in enumerate((1, 0, 3, 2)):
        rows = pl.ds(place * unit, unit)
        yield info[0] ^ (2 * z), mine.at[rows]
        yield info[0] ^ (2 * z + 1), other.at[rows]


def last_grad_body(info, near, far, act, far_act, context, far_context, mine, other, total, dense_total):
    step = pl.program_id(0)
    total[...] = tn(act[...], near[...]) + tn(far_act[...], far[...])
    dense_total[...] = tn(context[...], near[...]) + tn(far_context[...], far[...])
    shrink_rows = 4 * HIDDEN
    for part in range(2):
        cols = slice(part * LANES, (part + 1) * LANES)
        for shard, out in each_shard(info, mine.at[:shrink_rows], other.at[:shrink_rows]):
            out[pl.ds(pl.multiple_of(64 * (2 * step + part), 64), 64), :] = total[aligned(shard, 64), cols].astype(BF16)
        block = dense_total[:, cols].astype(BF16)
        rows = pl.ds(pl.multiple_of(shrink_rows + LANES * (2 * step + part), LANES), LANES)
        mine[rows, :] = block
        other[rows, :] = block


def last_backward(info, near, far, act, context):
    operands = [array.reshape(-1, array.shape[2]) for array in (near, far) + act + context]
    near = operands[0]
    width = near.shape[1]
    outs = [((4 * HIDDEN + width, LANES), BF16)] * 2
    columns = pl.BlockSpec((near.shape[0], 2 * LANES), lambda i, _: (0, i))
    return call(
        last_grad_body,
        info,
        operands,
        [columns, columns] + [whole(operand.shape) for operand in operands[2:]],
        outs,
        [whole(shape) for shape, _ in outs],
        grid=(width // (2 * LANES),),
        scratch=[pltpu.VMEM((HIDDEN, 2 * LANES), F32), pltpu.VMEM((LANES, 2 * LANES), F32)],
        micros=5,
    )


def as_column(row):
    size = row.shape[1]
    high = row.astype(BF16)
    middle = (row - high.astype(F32)).astype(BF16)
    low = (row - high.astype(F32) - middle.astype(F32)).astype(BF16)
    parts = jnp.concatenate([jnp.broadcast_to(part, (16, size)) for part in (high, middle, low)])
    first = lax.broadcasted_iota(jnp.int32, (48, LANES), 0) % 16 == 0
    return tn(parts, first.astype(BF16))


def norm_products(block, grads, normed, far_normed, column, weight, vectors, row, total, sums):
    count = normed.shape[0]
    products = tn(grads[:count, :], normed[...]) + tn(grads[count:, :], far_normed[...])
    lines = as_columns(weight[block, :])
    shifts = column[:, 0:1]
    total[:, block] = products * vectors[row : row + 1, block] + shifts * vectors[row + 1 : row + 2, block]
    sums[0:1, block] = jnp.sum(lines * products, axis=0, keepdims=True)
    sums[1:2, block] = jnp.sum(lines * shifts, axis=0, keepdims=True)


def expand_grad_body(
    info, near, far, slope, far_slope, normed, far_normed, shrink, expand, vectors, pre_out, bias_out, sums, mine, other, held, total, column
):
    step = pl.program_id(0)
    clear(bias_out, sums)

    @pl.when(step < 4)
    def _():
        cot = jnp.where(step < 2, near[...], far[...])
        grad_act = nt(cot.reshape(cot.shape[0] * cot.shape[1], cot.shape[2]), shrink[...])
        slopes = jnp.where(step < 2, slope[...], far_slope[...]).reshape(grad_act.shape).astype(F32)
        grad_pre = (grad_act * slopes).astype(BF16)
        pre_out[...] = grad_pre.reshape(pre_out.shape)
        held[pl.ds(pl.multiple_of(step * grad_pre.shape[0], grad_pre.shape[0]), grad_pre.shape[0]), :] = grad_pre
        bias_out[...] += jnp.broadcast_to(jnp.sum(grad_pre.astype(F32), axis=0, keepdims=True), bias_out.shape)

    @pl.when(step == 3)
    def _():
        column[...] = as_column(bias_out[0:1, :])

    @pl.when(step >= 4)
    def _():
        block = aligned(step - 4, 2 * LANES)
        norm_products(block, held, normed, far_normed, column, expand, vectors, 2, total, sums)

    @pl.when(step == 7)
    def _():
        for shard, out in each_shard(info, mine, other):
            out[...] = total[:, aligned(shard, LANES)].astype(BF16)


def two_phases(pair):
    shape = pair[0].shape
    block, rest = (2,) + shape[1:], (0,) * (len(shape) - 1)
    return [
        pl.BlockSpec(block, lambda i, _: (jnp.minimum(i, 1),) + rest),
        pl.BlockSpec(block, lambda i, _: (jnp.clip(i - 2, 0, 1),) + rest),
    ]


def all_tokens(rows):
    return [pl.BlockSpec((rows, 2 * LANES), lambda i, _: (0, jnp.maximum(i - 4, 0)))] * 2


def in_first_phase(shape):
    rest = (0,) * (len(shape) - 1)
    return pl.BlockSpec((2,) + shape[1:], lambda i, _: (jnp.minimum(i, 3),) + rest)


def expand_backward(info, near, far, slope, normed, shrink, expand, vectors):
    tokens, width = near.shape[1:]
    columns = [half.reshape(-1, width) for half in normed]
    operands = [near, far, *slope, *columns, shrink, expand, vectors]
    in_specs = two_phases((near, far)) + two_phases(slope) + all_tokens(columns[0].shape[0])
    in_specs += [whole(operand.shape) for operand in operands[6:]]
    outs = [((GROUP, tokens, HIDDEN), BF16), ((8, HIDDEN), F32), ((8, width), F32)] + [((4 * HIDDEN, LANES), BF16)] * 2
    out_specs = [in_first_phase(outs[0][0])] + [whole(shape) for shape, _ in outs[1:]]
    scratch = [
        pltpu.VMEM((GROUP * tokens, HIDDEN), BF16),
        pltpu.VMEM((HIDDEN, width), F32),
        pltpu.VMEM((HIDDEN, LANES), F32),
    ]
    return call(expand_grad_body, info, operands, in_specs, outs, out_specs, grid=(8,), scratch=scratch, micros=9)


def attention_grad_body(
    info, near, far, normed, far_normed, heads, far_heads, tables, far_tables, probs, far_probs,
    dense, frequency, mix, vectors, bias_grad, feed_sums,
    mixed_out, mine, other, mixed_held, total, column, sums, piece,
):
    step = pl.program_id(0)
    rank = info[1]
    tokens = near.shape[1]
    clear(sums)

    @pl.when(step == 0)
    def _():
        sums[4:5, :] = jnp.sum(near[0].astype(F32), axis=0, keepdims=True)

    @pl.when(step < 4)
    def _():
        cot = jnp.where(step < 2, near[...], far[...])
        all_heads = jnp.where(step < 2, heads[...], far_heads[...])
        all_tables = jnp.where(step < 2, tables[...], far_tables[...])
        all_probs = jnp.where(step < 2, probs[...], far_probs[...])
        lane = lax.broadcasted_iota(jnp.int32, (tokens, LANES), 1)
        grad_context = nt(cot.reshape(2 * tokens, cot.shape[2]), dense[...]).astype(BF16)
        for sequence in range(2):
            queries = all_heads[sequence, :, :LANES]
            keys = all_heads[sequence, :, LANES : 2 * LANES]
            values = all_heads[sequence, :, 2 * LANES :]
            part = by_head(grad_context[sequence * tokens : (sequence + 1) * tokens], lane)
            low = all_probs[sequence].reshape(2 * tokens, tokens)
            exact = low.astype(F32)
            grad_probs = nt(part, values)
            grad_scores = exact * (grad_probs - jnp.sum(exact * grad_probs, axis=-1, keepdims=True))
            grad_scores = grad_scores.astype(BF16)
            grad_values = tn(low, part)
            grad_queries = from_heads(nn(grad_scores, keys), lane)
            grad_keys = tn(grad_scores, by_head(queries, lane))
            cos, sin = spread_tables(all_tables[sequence], frequency)
            joined = [
                turn(grad_queries * HEAD ** (-0.5), cos, -sin, lane),
                turn(grad_keys * HEAD ** (-0.5), cos, -sin, lane),
                grad_values,
            ]
            grad_mixed = jnp.concatenate(joined, axis=1).astype(BF16)
            mixed_out[sequence] = grad_mixed
            mixed_held[pl.ds(pl.multiple_of((2 * step + sequence) * tokens, tokens), tokens), :] = grad_mixed
            sums[5:6, :MIX_COLS] += jnp.sum(grad_mixed.astype(F32), axis=0, keepdims=True)

    @pl.when(step == 3)
    def _():
        column[...] = as_column(sums[5:6, :MIX_COLS])

    @pl.when(step >= 4)
    def _():
        block = aligned(step - 4, 2 * LANES)
        norm_products(block, mixed_held, normed, far_normed, column, mix, vectors, 0, total, sums)

    @pl.when(step == 7)
    def _():
        sums[2:4, :] = feed_sums[0:2, :]
        line = lax.broadcasted_iota(jnp.int32, (8, LANES), 1)
        for shard, out in each_shard(info, mine, other):
            block = aligned(shard, LANES)
            out[:MIX_COLS, :] = total[:, block].astype(BF16)
            piece[...] = jnp.zeros_like(piece)
            piece[0:5, :] = sums[0:5, block]
            for row in range(3):
                place = 3 * shard + row
                spread = jnp.zeros((1, LANES), F32)
                for part in range(3):
                    held = sums[5:6, part * LANES : (part + 1) * LANES]
                    spread = spread + jnp.where(place == 8 * part + rank, held, 0.0)
                piece[5 + row : 6 + row, :] = spread
            packed = bias_grad[:, aligned(shard // 2, LANES)]
            moved = jnp.where(jnp.bitwise_and(shard ^ rank, 1) == 1, pltpu.roll(packed, 64, 1), packed)
            moved = jnp.where(line // 64 == jnp.bitwise_and(rank, 1), moved, 0.0)
            for row in range(4):
                piece[8 + row : 9 + row, :] = jnp.where(rank // 2 == row, moved[0:1, :], 0.0)
            out[MIX_COLS:, :] = piece[...].astype(BF16)


def attention_backward(info, near, far, saved, fixed):
    tokens, width = near.shape[1:]
    normed, *saved = saved
    columns = [half.reshape(-1, width) for half in normed]
    operands = [near, far, *columns]
    in_specs = two_phases((near, far)) + all_tokens(columns[0].shape[0])
    for pair in saved:
        operands += pair
        in_specs += two_phases(pair)
    operands += list(fixed)
    in_specs += [whole(operand.shape) for operand in fixed]
    outs = [((GROUP, tokens, MIX_COLS), BF16)] + [((4 * MIX_ROWS, LANES), BF16)] * 2
    out_specs = [in_first_phase(outs[0][0])] + [whole(shape) for shape, _ in outs[1:]]
    scratch = [
        pltpu.VMEM((GROUP * tokens, MIX_COLS), BF16),
        pltpu.VMEM((MIX_COLS, width), F32),
        pltpu.VMEM((MIX_COLS, LANES), F32),
        pltpu.VMEM((8, width), F32),
        pltpu.VMEM((SMALL, LANES), F32),
    ]
    return call(
        attention_grad_body, info, operands, in_specs, outs, out_specs, grid=(8,), scratch=scratch, micros=13
    )


def input_grad_body(info, mixed, pre, mix, expand, vectors, out):
    total = nt(flat(mixed), mix[...]) * vectors[0:1, :] + nt(flat(pre), expand[...]) * vectors[2:3, :]
    out[...] = total.astype(BF16).reshape(out.shape)


def input_backward(info, mixed, pre, mix, expand, vectors, far):
    tokens, width = mixed.shape[1], mix.shape[0]
    operands = [mixed, pre, mix, expand, vectors]
    in_specs = [pairs(mixed.shape, 2 * far), pairs(pre.shape, 2 * far)]
    in_specs += [whole(operand.shape) for operand in operands[2:]]
    shape = (4, tokens, width)
    return call(input_grad_body, info, operands, in_specs, [(shape, BF16)], [pairs(shape)], grid=(2,), micros=6)[0]


def norm_body(info, block, cot, upper, upper_got, lower, lower_got, out):
    inputs = block[...].astype(F32)
    average = jnp.mean(inputs, axis=-1, keepdims=True)
    centred = inputs - average
    scale = lax.rsqrt(jnp.mean(centred * centred, axis=-1, keepdims=True) + EPSILON)
    normed = centred * scale
    pulled = jnp.concatenate(
        [upper[...] + upper_got[...].astype(F32), lower[...] + lower_got[...].astype(F32)]
    )
    pulled = pulled - jnp.mean(pulled, axis=-1, keepdims=True) - normed * jnp.mean(pulled * normed, axis=-1, keepdims=True)
    out[...] = cot[...].astype(F32) + scale * pulled


def each_rank(near, far, unit):
    for place, number in enumerate(NEAR):
        rows = pl.ds(place * unit, unit)
        yield number, near.at[rows], far.at[rows]


def last_out_body(info, near, far, own_dense, shrink_out, dense_out):
    rank = info[1]
    for number, one, two in each_rank(near, far, HIDDEN):
        for piece, held in ((one, rank ^ number), (two, rank ^ number ^ 1)):
            for part in range(8):
                rows = piece[64 * part : 64 * (part + 1), :]
                shrink_out[aligned(held, 64), part * LANES : (part + 1) * LANES] = rows.astype(F32)
    for part in range(8):
        start = 4 * HIDDEN + part * LANES
        rows = jnp.where(own_dense[0] == 1, near[start : start + LANES, :], far[start : start + LANES, :])
        dense_out[:, part * LANES : (part + 1) * LANES] = rows.astype(F32)


def last_grads_out_body(info, near, far, expand_out, mix_out):
    rank = info[1]
    upper = jnp.bitwise_and(rank, 1) == 1
    for number, one, two in each_rank(near, far, HIDDEN):
        place = (rank ^ number) // 2
        for shard in range(8):
            rows = slice(64 * shard, 64 * (shard + 1))
            lower_rows = jnp.where(upper, two[rows, :], one[rows, :])
            upper_rows = jnp.where(upper, one[rows, :], two[rows, :])
            joined = jnp.concatenate([lower_rows, upper_rows], axis=0)
            expand_out[:, aligned(4 * shard + place, LANES)] = as_columns(joined)
    size = 4 * HIDDEN
    for number, one, two in each_rank(near.at[size:], far.at[size:], MIX_ROWS):
        for piece, place in ((one, rank ^ number), (two, rank ^ number ^ 1)):
            for part in range(3):
                mix_out[:, aligned(8 * part + place, LANES)] = as_columns(piece[part * LANES : (part + 1) * LANES, :])


def after(value, *others):
    return jax.tree.map(lambda leaf: lax.optimization_barrier((leaf,) + others)[0], value)


def mark_body(info, out):
    out[...] = jnp.zeros_like(out) + info[0].astype(F32)


def mark(info, *others):
    return call(mark_body, after(info, *others), [], [], [((8, LANES), F32)], [whole((8, LANES))], micros=40)[0]


def gather_first(upper, lower):
    return swap(upper, x=1), swap(lower, low=1)


def gather_second(upper, lower, upper_x, lower_low):
    upper_pair = swap(jnp.stack([upper, upper_x]), low=1)
    lower_pair = swap(jnp.stack([lower, lower_low]), x=1)
    return (
        jnp.stack([upper, upper_pair[0], upper_x, upper_pair[1]]),
        jnp.stack([lower, lower_low, lower_pair[0], lower_pair[1]]),
    )


def reduce_first(mine, other, unit, *late):
    got = after(swap(other, y=1), *late)
    total = mine.astype(F32) + got.astype(F32)
    return total, total[2 * unit :].astype(BF16)


def reduce_second(total, sent, unit, *late):
    kept = jnp.concatenate([total[: 2 * unit], total[4 * unit :]])
    return (kept + after(swap(sent, high=1), *late).astype(F32)).astype(BF16)


def share_first(slices, unit):
    away, own = slices[:unit], slices[unit:]
    return own, swap(away, low=1), swap(own, x=1), swap(away, x=1, low=1)


def share_last(slices, own_x, *late):
    parts = after(share_first(slices, HIDDEN), *late)
    dense_part = jnp.where(own_x, parts[0][HIDDEN:], parts[2][HIDDEN:])
    return jnp.concatenate([part[:HIDDEN] for part in parts] + [dense_part])


def scatter_first(near, far_got):
    cut = near.shape[1] // 2
    total = near.astype(F32) + far_got.astype(F32)
    sent_x = total[2:, :cut].astype(BF16)
    sent_low = total[1::2, cut:].astype(BF16)
    return total[:2, :cut], sent_x, total[0::2, cut:], sent_low


def scatter_second(kept_x, sent_x, kept_low, sent_low, *late):
    upper = kept_x + after(swap(sent_x, x=1), *late).astype(F32)
    lower = kept_low + after(swap(sent_low, low=1), *late).astype(F32)
    return upper[0], upper[1].astype(BF16), lower[0], lower[1].astype(BF16)


def scatter_third(upper, sent_upper, lower, sent_lower, *late):
    upper = upper + after(swap(sent_upper, low=1), *late).astype(F32)
    lower = lower + after(swap(sent_lower, x=1), *late).astype(F32)
    return jnp.concatenate([upper, lower])


def local(
    block_input,
    segments,
    cotangent,
    first_gain,
    first_shift,
    mix_weight,
    mix_bias,
    dense_weight,
    dense_bias,
    second_gain,
    second_shift,
    expand_weight,
    expand_bias,
    shrink_weight,
    shrink_bias,
):
    rep = lax.axis_index("rep")
    shard = lax.axis_index("fsdp")
    x, core, high, low, y = rep // 2, rep % 2, shard // 4, (shard // 2) % 2, shard % 2
    info = jnp.stack([shard, 4 * x + 2 * low + core]).astype(jnp.int32)
    tokens, width = block_input.shape
    rows = mix_weight.shape[0]

    own_y, own_x = y == core, x == high

    small = (first_gain, first_shift, second_gain, second_shift, dense_bias, shrink_bias, mix_bias, expand_bias)
    half = tokens // 2
    own, other = cut_slices(info, mix_weight, expand_weight, small)
    marks = jnp.pad(segments.astype(BF16), ((0, 15), (0, width - tokens)))
    upper, lower = block_input[:half], jnp.concatenate([block_input[half:], marks])
    along = swap(other, low=1), swap(own, high=1), swap(other, high=1, low=1)
    upper_x, lower_low = gather_first(upper, lower)
    first = mark(info, own)
    upper_x, lower_low = after((upper_x, lower_low), first)
    over = swap(after(own, first), y=1)
    upper_pair = swap(jnp.stack([upper, upper_x]), low=1)
    lower_in = jnp.stack([lower, lower_low])
    second = mark(info, upper_x, lower_in)
    along = jnp.stack(after(along, second, over))
    across = swap(along, y=1)
    lower_pair = swap(after(lower_in, along), x=1)

    high_in, low_in, other_shrink = cut_last(after(info, first), shrink_weight, dense_weight, cotangent)
    high_last = swap(after(high_in, along), high=1)
    low_last = swap(after(low_in, along), low=1)
    third = mark(info, along, high_in, low_in)
    upper_pair, lower_pair, across = after((upper_pair, lower_pair, across), third)
    near = jnp.concatenate(
        [
            jnp.stack([upper, upper_pair[0], upper_x, upper_pair[1]]),
            jnp.stack([lower, lower_low, lower_pair[0], lower_pair[1]]),
        ],
        axis=1,
    )
    both_last = swap(after(other_shrink, near), high=1, low=1)
    far = swap(near, core=1)
    cot_upper = after(cotangent[:half], near)
    cot_upper_x = swap(cot_upper, x=1)
    frequency = jnp.asarray(turn_constants())
    *near_saved, mix, expand, vectors, bias = forward(info, near, (own, over, along, across), frequency, tokens, width)
    high_last, low_last, both_last, cot_upper_x, far = after((high_last, low_last, both_last, cot_upper_x, far), mix)
    last, dense_held = pack_last(info, high_in, low_last, high_last, both_last, dense_weight)
    last_across = swap(last, y=1)
    cot_near = gather_second(cot_upper, cotangent[half:], cot_upper_x, low_last[64:])
    far = after(far, last, cot_upper_x)
    far_saved = forward(info, far, (mix, expand, vectors, bias), frequency, tokens, width, True)
    normed, heads, tables, probs, context, act, slope = zip(near_saved, far_saved)
    last_across = after(last_across, context[1])
    dense = jnp.where(own_y, dense_held, last_across[256:])
    branch_far, shrink = project(info, context[1], act[1], dense, (last, last_across), True)
    branch_got = swap(branch_far, core=1)
    cot_near = jnp.concatenate(after(cot_near, branch_far), axis=1)
    cot_far = swap(cot_near, core=1)
    (branch_near,) = project(info, context[0], act[0], dense, after(shrink, cot_near), False)
    last_mine, last_other = last_backward(info, cot_near, after(cot_far, branch_near), act, context)
    branch = scatter_first(after(branch_near, last_mine), branch_got)
    grad_pre, bias_grad, feed_sums, expand_mine, expand_other = expand_backward(
        info, cot_near, cot_far, slope, normed, after(shrink, last_mine, branch[1], branch[3]), expand, vectors
    )
    branch = scatter_second(*branch, grad_pre)
    last_part = reduce_first(last_mine, last_other, HIDDEN, grad_pre)
    grad_mixed, mix_mine, mix_other = attention_backward(
        info,
        cot_near,
        cot_far,
        (normed, heads, tables, probs),
        (after(dense, last_part[1], branch[1], branch[3]), frequency, mix, vectors, bias_grad, feed_sums),
    )
    expand_part = reduce_first(expand_mine, expand_other, HIDDEN, grad_mixed)
    branch = scatter_third(*branch, grad_mixed)
    block_out = (block_input.astype(F32) + branch + (vectors[4] + vectors[5])).astype(BF16)
    error_far = input_backward(info, after(grad_mixed, expand_part[1]), grad_pre, mix, expand, vectors, True)
    error_got = swap(error_far, core=1)
    error_near = input_backward(info, after(grad_mixed, error_far), grad_pre, mix, expand, vectors, False)
    error = scatter_first(error_near, error_got)
    last_slices = reduce_second(*last_part, HIDDEN, error_near)
    mix_part = reduce_first(mix_mine, mix_other, MIX_ROWS, error[1], error[3])
    last_near = share_last(last_slices, own_x, error[1], error[3])
    last_far = swap(last_near, core=1)
    fourth = mark(info, error[1], mix_part[1], last_near)
    expand_slices = reduce_second(*expand_part, HIDDEN, fourth)
    error = scatter_second(*error, expand_slices)

    def out(body, near, far, shapes, flag=None):
        operands = [near, far]
        in_specs = [whole(near.shape), whole(far.shape)]
        if flag is not None:
            operands.append(flag)
            in_specs.append(pl.BlockSpec(memory_space=pltpu.SMEM))
        return call(body, info, operands, in_specs, [(shape, F32) for shape in shapes], [whole(shape) for shape in shapes])

    flag = own_y.astype(jnp.int32).reshape(1)
    shapes = [shrink_weight.shape, dense_weight.shape]
    shrink_out, dense_out = out(last_out_body, last_near, after(last_far, fourth), shapes, flag)
    mix_slices = reduce_second(*mix_part, MIX_ROWS, fourth)
    slices = [expand_slices[:HIDDEN], mix_slices[:MIX_ROWS], expand_slices[HIDDEN:], mix_slices[MIX_ROWS:]]
    slices = jnp.concatenate(slices)
    parts = share_first(slices, HIDDEN + MIX_ROWS)
    fifth = mark(info, slices, error[1], error[3])
    parts = after(parts, fifth)
    expand_near = jnp.concatenate([part[:HIDDEN] for part in parts])
    mix_parts = [part[HIDDEN:] for part in parts]
    mix_sums = [part[MIX_COLS:].astype(F32) for part in mix_parts]
    mix_sums = ((mix_sums[0] + mix_sums[1]) + (mix_sums[2] + mix_sums[3])).astype(BF16)
    near = jnp.concatenate([expand_near] + mix_parts + [mix_sums])
    far = swap(near, core=1)
    upper_got = after(swap(error[1], low=1), near)
    lower_got = after(swap(error[3], x=1), near)
    operands = [block_input, cotangent, error[0], upper_got, error[2], lower_got]
    (input_grad,) = call(
        norm_body,
        info,
        operands,
        [whole(operand.shape) for operand in operands],
        [(block_input.shape, F32)],
        [whole(block_input.shape)],
    )
    far = after(far, input_grad)
    sums = mix_sums.astype(F32) + far[4 * (HIDDEN + MIX_ROWS) :].astype(F32)
    expand_out, mix_out = out(last_grads_out_body, near, far, [expand_weight.shape, mix_weight.shape])
    return (
        block_out,
        input_grad,
        sums[0],
        sums[1],
        mix_out,
        sums[5:8].reshape(-1),
        dense_out,
        sums[4],
        sums[2],
        sums[3],
        expand_out,
        sums[8:12].reshape(-1),
        shrink_out,
        sums[4],
    )


def solution(mesh):
    tensor_parallel = mesh.shape["rep"] == TP_REP and mesh.shape["fsdp"] == TP_FSDP
    return jax.shard_map(
        local if tensor_parallel else local_general,
        mesh=mesh,
        in_specs=(
            P(("rep", "fsdp"), None),
            P(("rep", "fsdp"), None),
            P(("rep", "fsdp"), None),
            P("fsdp"),
            P("fsdp"),
            P("fsdp", None),
            P("fsdp"),
            P("fsdp", None),
            P("fsdp"),
            P("fsdp"),
            P("fsdp"),
            P("fsdp", None),
            P("fsdp"),
            P("fsdp", None),
            P("fsdp"),
        ),
        out_specs=(
            P(("rep", "fsdp"), None),
            P(("rep", "fsdp"), None),
            P("fsdp"),
            P("fsdp"),
            P("fsdp", None),
            P("fsdp"),
            P("fsdp", None),
            P("fsdp"),
            P("fsdp"),
            P("fsdp"),
            P("fsdp", None),
            P("fsdp"),
            P("fsdp", None),
            P("fsdp"),
        ),
        check_vma=False,
    )
```

```python
import jax
import jax.numpy as jnp
import numpy as np
from jax import lax
from jax.experimental import pallas as pl
from jax.experimental.pallas import tpu as pltpu
from jax.sharding import PartitionSpec as P

HEADS = 16
HEAD = 64
ROT = 16


EPSILON = 1e-05


def layer_norm(inputs, gain_row, shift_row):
    average = jnp.mean(inputs, axis=-1, keepdims=True)
    centred = inputs - average
    variance = jnp.mean(centred * centred, axis=-1, keepdims=True)
    return centred * lax.rsqrt(variance + EPSILON) * gain_row + shift_row


def rotate(heads_in, cos_table, sin_table):
    half_rot = ROT // 2
    first_half = heads_in[..., :half_rot]
    second_half = heads_in[..., half_rot:ROT]
    return jnp.concatenate(
        [
            first_half * cos_table - second_half * sin_table,
            second_half * cos_table + first_half * sin_table,
            heads_in[..., ROT:],
        ],
        axis=-1,
    )


def rotary_tables(segment_row):
    length = segment_row.shape[0]
    same_doc = segment_row[:, None] == segment_row[None, :]
    row_index = lax.broadcasted_iota(jnp.int32, (length, length), 0)
    col_index = lax.broadcasted_iota(jnp.int32, (length, length), 1)
    earlier = jnp.where(same_doc & (col_index < row_index), 1.0, 0.0)
    position = jnp.sum(earlier, axis=-1).astype(jnp.float32)
    allowed = same_doc & (col_index <= row_index)
    frequency = jnp.power(10000.0, -2.0 * jnp.arange(ROT // 2).astype(jnp.float32) / ROT)
    phases = position[:, None] * frequency
    return (jnp.cos(phases)[:, None, :], jnp.sin(phases)[:, None, :], allowed)


def product_left(left, right):
    return lax.dot_general(
        left, right, (((0,), (0,)), ((), ())), preferred_element_type=jnp.float32
    )


def product_right(left, right):
    return lax.dot_general(
        left, right, (((1,), (1,)), ((), ())), preferred_element_type=jnp.float32
    )


def norm_backward(inputs, gain_row, shift_row, upstream):
    _, pullback = jax.vjp(layer_norm, inputs, gain_row, shift_row)
    return pullback(upstream)


def local_general(
    block_input,
    segments,
    cotangent,
    first_gain,
    first_shift,
    mix_weight,
    mix_bias,
    dense_weight,
    dense_bias,
    second_gain,
    second_shift,
    expand_weight,
    expand_bias,
    shrink_weight,
    shrink_bias,
):
    attention_parts = (
        lax.all_gather(first_gain, "fsdp", axis=0, tiled=True),
        lax.all_gather(first_shift, "fsdp", axis=0, tiled=True),
        lax.all_gather(mix_weight, "fsdp", axis=0, tiled=True),
        lax.all_gather(mix_bias, "fsdp", axis=0, tiled=True),
        lax.all_gather(dense_weight, "fsdp", axis=0, tiled=True),
        lax.all_gather(dense_bias, "fsdp", axis=0, tiled=True),
    )
    feed_parts = (
        lax.all_gather(second_gain, "fsdp", axis=0, tiled=True),
        lax.all_gather(second_shift, "fsdp", axis=0, tiled=True),
        lax.all_gather(expand_weight, "fsdp", axis=0, tiled=True),
        lax.all_gather(expand_bias, "fsdp", axis=0, tiled=True),
        lax.all_gather(shrink_weight, "fsdp", axis=0, tiled=True),
        lax.all_gather(shrink_bias, "fsdp", axis=0, tiled=True),
    )
    token_count = block_input.shape[0]
    feature_count = block_input.shape[1]
    score_scale = HEAD ** (-0.5)
    block_float = block_input.astype(jnp.float32)
    cot_float = cotangent.astype(jnp.float32)
    cos_table, sin_table, allowed = rotary_tables(segments[0])
    normed_one = layer_norm(
        block_float, attention_parts[0].astype(jnp.float32), attention_parts[1].astype(jnp.float32)
    ).astype(jnp.bfloat16)
    mixed_rows = jnp.dot(normed_one, attention_parts[2], preferred_element_type=jnp.float32)
    mixed_rows = mixed_rows + attention_parts[3].astype(jnp.float32)
    triple = mixed_rows.reshape(token_count, 3, HEADS, HEAD)
    queries = rotate(triple[:, 0], cos_table, sin_table).astype(jnp.bfloat16)
    keys_all = rotate(triple[:, 1], cos_table, sin_table).astype(jnp.bfloat16)
    values_all = triple[:, 2].astype(jnp.bfloat16)

    def masked_scores():
        raw_scores = (
            jnp.einsum("qhd,khd->hqk", queries, keys_all, preferred_element_type=jnp.float32)
            * score_scale
        )
        return jnp.where(allowed[None], raw_scores, -1e30)

    forward_scores = masked_scores()
    row_peak = jnp.max(forward_scores, axis=-1, keepdims=True)
    weights_raw = jnp.exp(forward_scores - row_peak)
    row_total = jnp.sum(weights_raw, axis=-1, keepdims=True)
    log_total = row_peak + jnp.log(row_total)
    probs_low = (weights_raw / row_total).astype(jnp.bfloat16)
    context = jnp.einsum("hqk,khd->qhd", probs_low, values_all, preferred_element_type=jnp.float32)
    context = context.reshape(token_count, feature_count).astype(jnp.bfloat16)
    attention_branch = jnp.dot(context, attention_parts[4], preferred_element_type=jnp.float32)
    attention_branch = attention_branch + attention_parts[5].astype(jnp.float32)
    normed_two = layer_norm(
        block_float, feed_parts[0].astype(jnp.float32), feed_parts[1].astype(jnp.float32)
    ).astype(jnp.bfloat16)
    hidden_pre = jnp.dot(normed_two, feed_parts[2], preferred_element_type=jnp.float32)
    hidden_pre = hidden_pre + feed_parts[3].astype(jnp.float32)
    hidden_act = jax.nn.gelu(hidden_pre, approximate=False).astype(jnp.bfloat16)
    feedforward_branch = jnp.dot(hidden_act, feed_parts[4], preferred_element_type=jnp.float32)
    feedforward_branch = feedforward_branch + feed_parts[5].astype(jnp.float32)
    block_out = (block_float + attention_branch + feedforward_branch).astype(jnp.bfloat16)
    feed_back = (
        lax.all_gather(second_gain, "fsdp", axis=0, tiled=True),
        lax.all_gather(second_shift, "fsdp", axis=0, tiled=True),
        lax.all_gather(expand_weight, "fsdp", axis=0, tiled=True),
        lax.all_gather(expand_bias, "fsdp", axis=0, tiled=True),
        lax.all_gather(shrink_weight, "fsdp", axis=0, tiled=True),
        lax.all_gather(shrink_bias, "fsdp", axis=0, tiled=True),
    )
    bias_sum = jnp.sum(cot_float, axis=0)
    shrink_grad = product_left(hidden_act, cotangent)
    grad_act = product_right(cotangent, feed_back[4])
    _, gelu_pull = jax.vjp(lambda pre_value: jax.nn.gelu(pre_value, approximate=False), hidden_pre)
    grad_pre = gelu_pull(grad_act)[0].astype(jnp.bfloat16)
    expand_grad = product_left(normed_two, grad_pre)
    expand_bias_grad = jnp.sum(grad_pre.astype(jnp.float32), axis=0)
    grad_normed_two = product_right(grad_pre, feed_back[2])
    part_two, second_gain_grad, second_shift_grad = norm_backward(
        block_float,
        feed_back[0].astype(jnp.float32),
        feed_back[1].astype(jnp.float32),
        grad_normed_two,
    )
    feed_grads = (
        lax.psum_scatter(second_gain_grad, "fsdp", scatter_dimension=0, tiled=True),
        lax.psum_scatter(second_shift_grad, "fsdp", scatter_dimension=0, tiled=True),
        lax.psum_scatter(expand_grad, "fsdp", scatter_dimension=0, tiled=True),
        lax.psum_scatter(expand_bias_grad, "fsdp", scatter_dimension=0, tiled=True),
        lax.psum_scatter(shrink_grad, "fsdp", scatter_dimension=0, tiled=True),
        lax.psum_scatter(bias_sum, "fsdp", scatter_dimension=0, tiled=True),
    )
    gain_two_sum, shift_two_sum, expand_sum, expand_bias_sum, shrink_sum, shrink_bias_sum = (
        feed_grads
    )
    attention_back = (
        lax.all_gather(first_gain, "fsdp", axis=0, tiled=True),
        lax.all_gather(first_shift, "fsdp", axis=0, tiled=True),
        lax.all_gather(mix_weight, "fsdp", axis=0, tiled=True),
        lax.all_gather(mix_bias, "fsdp", axis=0, tiled=True),
        lax.all_gather(dense_weight, "fsdp", axis=0, tiled=True),
        lax.all_gather(dense_bias, "fsdp", axis=0, tiled=True),
    )
    dense_grad = product_left(context, cotangent)
    grad_context = product_right(cotangent, attention_back[4]).astype(jnp.bfloat16)
    grad_context = grad_context.reshape(token_count, HEADS, HEAD)
    grad_values = jnp.einsum(
        "hqk,qhd->khd", probs_low, grad_context, preferred_element_type=jnp.float32
    )
    grad_probs = jnp.einsum(
        "qhd,khd->hqk", grad_context, values_all, preferred_element_type=jnp.float32
    )
    probs_exact = jnp.exp(masked_scores() - log_total)
    grad_scores = probs_exact * (
        grad_probs - jnp.sum(probs_exact * grad_probs, axis=-1, keepdims=True)
    )
    grad_scores = grad_scores.astype(jnp.bfloat16)
    grad_queries = (
        jnp.einsum("hqk,khd->qhd", grad_scores, keys_all, preferred_element_type=jnp.float32)
        * score_scale
    )
    grad_keys = (
        jnp.einsum("hqk,qhd->khd", grad_scores, queries, preferred_element_type=jnp.float32)
        * score_scale
    )
    _, rotate_pull = jax.vjp(lambda heads_in: rotate(heads_in, cos_table, sin_table), grad_queries)
    grad_mixed = jnp.stack(
        [rotate_pull(grad_queries)[0], rotate_pull(grad_keys)[0], grad_values], axis=1
    )
    grad_mixed = grad_mixed.reshape(token_count, 3 * feature_count).astype(jnp.bfloat16)
    mix_grad = product_left(normed_one, grad_mixed)
    mix_bias_grad = jnp.sum(grad_mixed.astype(jnp.float32), axis=0)
    grad_normed_one = product_right(grad_mixed, attention_back[2])
    part_one, first_gain_grad, first_shift_grad = norm_backward(
        block_float,
        attention_back[0].astype(jnp.float32),
        attention_back[1].astype(jnp.float32),
        grad_normed_one,
    )
    attention_grads = (
        lax.psum_scatter(first_gain_grad, "fsdp", scatter_dimension=0, tiled=True),
        lax.psum_scatter(first_shift_grad, "fsdp", scatter_dimension=0, tiled=True),
        lax.psum_scatter(mix_grad, "fsdp", scatter_dimension=0, tiled=True),
        lax.psum_scatter(mix_bias_grad, "fsdp", scatter_dimension=0, tiled=True),
        lax.psum_scatter(dense_grad, "fsdp", scatter_dimension=0, tiled=True),
        lax.psum_scatter(bias_sum, "fsdp", scatter_dimension=0, tiled=True),
    )
    gain_one_sum, shift_one_sum, mix_sum, mix_bias_sum, dense_sum, dense_bias_sum = attention_grads
    (
        gain_one_sum,
        shift_one_sum,
        mix_sum,
        mix_bias_sum,
        dense_sum,
        dense_bias_sum,
        gain_two_sum,
        shift_two_sum,
        expand_sum,
        expand_bias_sum,
        shrink_sum,
        shrink_bias_sum,
    ) = lax.psum(
        (
            gain_one_sum,
            shift_one_sum,
            mix_sum,
            mix_bias_sum,
            dense_sum,
            dense_bias_sum,
            gain_two_sum,
            shift_two_sum,
            expand_sum,
            expand_bias_sum,
            shrink_sum,
            shrink_bias_sum,
        ),
        "rep",
    )
    input_grad = cot_float + part_one + part_two
    return (
        block_out,
        input_grad,
        gain_one_sum,
        shift_one_sum,
        mix_sum,
        mix_bias_sum,
        dense_sum,
        dense_bias_sum,
        gain_two_sum,
        shift_two_sum,
        expand_sum,
        expand_bias_sum,
        shrink_sum,
        shrink_bias_sum,
    )


TP_REP = 4
TP_FSDP = 8
GROUP = 8
NEAR = (0, 2, 4, 6)
MIX_COLS = 384
HIDDEN = 512
SMALL = 16
LANES = 128
FIRST_ROWS = MIX_COLS + SMALL + HIDDEN
MIX_ROWS = MIX_COLS + SMALL
FEED_ROWS = 2 * HIDDEN
F32 = jnp.float32
BF16 = jnp.bfloat16
COST = 5000
VMEM_LIMIT = 18 * 1024 * 1024
VMEM_FIRST = 28 * 1024 * 1024
VMEM_WHOLE = 56 * 1024 * 1024


def permute(value, target):
    pairs = []
    for rep in range(TP_REP):
        for shard in range(TP_FSDP):
            goal = target(rep // 2, rep % 2, shard // 4, (shard // 2) % 2, shard % 2)
            if goal is not None:
                x, core, high, low, y = goal
                pairs.append((rep * TP_FSDP + shard, (2 * x + core) * TP_FSDP + 4 * high + 2 * low + y))
    return lax.ppermute(value, ("rep", "fsdp"), pairs)


def swap(value, x=0, core=0, high=0, low=0, y=0):
    return permute(value, lambda a, b, c, d, e: (a ^ x, b ^ core, c ^ high, d ^ low, e ^ y))


def nt(left, right):
    return lax.dot_general(left, right, (((1,), (1,)), ((), ())), preferred_element_type=F32)


def nn(left, right):
    return lax.dot_general(left, right, (((1,), (0,)), ((), ())), preferred_element_type=F32)


def tn(left, right):
    return lax.dot_general(left, right, (((0,), (0,)), ((), ())), preferred_element_type=F32)


def whole(shape):
    return pl.BlockSpec(shape, lambda *_: (0,) * len(shape))


def call(body, info, operands, in_specs, outs, out_specs, grid=(1,), scratch=(), micros=4, vmem=VMEM_LIMIT):
    return pl.pallas_call(
        body,
        grid_spec=pltpu.PrefetchScalarGridSpec(
            num_scalar_prefetch=1,
            grid=grid,
            in_specs=in_specs,
            out_specs=out_specs,
            scratch_shapes=list(scratch),
        ),
        out_shape=[jax.ShapeDtypeStruct(shape, dtype) for shape, dtype in outs],
        compiler_params=pltpu.CompilerParams(vmem_limit_bytes=vmem),
        cost_estimate=pl.CostEstimate(flops=micros * COST * 10**6, bytes_accessed=micros * COST * 3 * 10**3, transcendentals=0),
    )(info, *operands)


def as_columns(matrix):
    size = matrix.shape[1]
    rows = lax.broadcasted_iota(jnp.int32, (size, size), 0)
    cols = lax.broadcasted_iota(jnp.int32, (size, size), 1)
    return nt((rows == cols).astype(BF16), matrix)


def aligned(index, unit):
    return pl.ds(pl.multiple_of(index * unit, unit), unit)


def cut_body(info, mix, expand, *rest):
    vectors, (own, other), small = rest[:8], rest[8:10], rest[10]
    row = 0
    small[...] = jnp.zeros_like(small)
    for vector in vectors:
        count = vector.shape[0]
        small[row : row + count, :] = vector[...].astype(F32)
        row = row + count if row + count != 6 else 8
    lane = lax.broadcasted_iota(jnp.int32, (LANES, LANES), 1)
    for out, rank in ((own, info[1]), (other, info[1] ^ 2)):
        for part in range(3):
            out[part * LANES : (part + 1) * LANES, :] = mix[:, aligned(8 * part + rank, LANES)]
        out[MIX_COLS:MIX_ROWS, :] = small[...].astype(BF16)
        upper = jnp.bitwise_and(rank, 1) == 1
        for pair in range(4):
            first = expand[:, aligned(8 * pair + rank // 2, LANES)].astype(F32)
            second = expand[:, aligned(8 * pair + 4 + rank // 2, LANES)].astype(F32)
            first = jnp.where(upper, pltpu.roll(first, 64, 1), first)
            second = jnp.where(upper, second, pltpu.roll(second, 64, 1))
            joined = jnp.where(lane < 64, first, second).astype(BF16)
            out[MIX_ROWS + pair * LANES : MIX_ROWS + (pair + 1) * LANES, :] = joined

def cut_slices(info, mix, expand, vectors):
    operands = [mix, expand] + [vector.reshape(-1, LANES) for vector in vectors]
    outs = [((FIRST_ROWS, LANES), BF16)] * 2
    return call(
        cut_body,
        info,
        operands,
        [whole(operand.shape) for operand in operands],
        outs,
        [whole(shape) for shape, _ in outs],
        scratch=[pltpu.VMEM((SMALL, LANES), F32)],
        vmem=VMEM_WHOLE,
    )


def cut_last_body(info, shrink, dense, cot, own, other, other_shrink):
    rows = cot.shape[0] // 2
    own[:64, :] = shrink[aligned(info[1], 64), :]
    own[64:, :] = dense[...]
    rest = shrink[aligned(info[1] ^ 2, 64), :]
    other_shrink[...] = rest
    other[:64, :] = rest
    other[64:, :] = cot[rows:, :]


def cut_last(info, shrink, dense, cot):
    operands = [shrink, dense, cot]
    shapes = [(64 + rows, shrink.shape[1]) for rows in (dense.shape[0], cot.shape[0] // 2, 0)]
    return call(
        cut_last_body,
        info,
        operands,
        [whole(operand.shape) for operand in operands],
        [(shape, BF16) for shape in shapes],
        [whole(shape) for shape in shapes],
        vmem=VMEM_WHOLE,
    )


def pack_body(info, own, low, high, both, dense, out, dense_high):
    out[:64, :] = own[:64, :]
    out[64:128, :] = low[:64, :]
    out[128:192, :] = high[:64, :]
    out[192:256, :] = both[...]
    same = info[1] // 4 == info[0] // 4
    out[256:, :] = jnp.where(same, dense[...], high[64:, :])
    dense_high[...] = out[256:, :]


def pack_last(info, own, low, high, both, dense):
    operands = [own, low, high, both, dense]
    shapes = [(256 + dense.shape[0], dense.shape[1]), dense.shape]
    return call(
        pack_body,
        info,
        operands,
        [whole(operand.shape) for operand in operands],
        [(shape, BF16) for shape in shapes],
        [whole(shape) for shape in shapes],
    )


def turn(heads, cos, sin, lane):
    ahead = pltpu.roll(heads, LANES - 8, 1)
    behind = pltpu.roll(heads, 8, 1)
    return heads * cos + jnp.where(lane % HEAD < 8, -ahead, behind) * sin


def spread_tables(table):
    high = table.astype(BF16)
    low = (table - high.astype(F32)).astype(BF16)
    row = lax.broadcasted_iota(jnp.int32, (32, 2 * LANES), 0)
    lane = lax.broadcasted_iota(jnp.int32, (32, 2 * LANES), 1)
    goes = ((row // 8) % 2 == lane // LANES) & (lane % HEAD < ROT) & (lane % 8 == row % 8)
    both = tn(jnp.concatenate([high, low]), goes.astype(BF16))
    still = lax.broadcasted_iota(jnp.int32, (1, LANES), 1) % HEAD >= ROT
    return both[:, :LANES] + still.astype(F32), both[:, LANES:]


def gelu_parts(hidden):
    normal = 0.5 + 0.5 * lax.erf(hidden * (0.5**0.5))
    return normal, hidden * jnp.exp(hidden * hidden * -0.5) * ((2.0 * np.pi) ** -0.5)


def by_head(rows, lane):
    return jnp.concatenate([jnp.where(lane < HEAD, rows, 0), jnp.where(lane < HEAD, 0, rows)]).astype(BF16)


def from_heads(rows, lane):
    tokens = rows.shape[0] // 2
    return jnp.where(lane < HEAD, rows[:tokens], rows[tokens:])


def near_forward_body(info, inputs, own, over, along, across, frequency, *outs):
    mix, expand, vectors, bias = outs[7:]
    shard, rank = info[0], info[1]

    @pl.when(pl.program_id(0) == 0)
    def _():
        for number in range(8):
            if number < 2:
                piece = over if number else own
            else:
                piece = (across if number % 2 else along).at[number // 2 - 1]
            block = aligned(shard ^ number, LANES)
            for part in range(3):
                mix[block, part * LANES : (part + 1) * LANES] = piece[part * LANES : (part + 1) * LANES, :]
            vectors[:, block] = piece[MIX_COLS:MIX_ROWS, :].astype(F32)
            for pair in range(4):
                start = MIX_ROWS + pair * LANES
                expand[block, pair * LANES : (pair + 1) * LANES] = piece[start : start + LANES, :]
        lane = lax.broadcasted_iota(jnp.int32, (8, LANES), 1)
        upper = jnp.bitwise_and(rank, 1) == 1
        bias[...] = jnp.zeros_like(bias)
        line = lax.broadcasted_iota(jnp.int32, (8, LANES), 0)

        def chosen_row(block, number):
            row = jnp.sum(jnp.where(line == number, block, 0.0), axis=0, keepdims=True)
            return jnp.broadcast_to(row, (8, LANES))

        for pair in range(4):
            one = chosen_row(vectors[8:16, 2 * pair * LANES : (2 * pair + 1) * LANES], 3 + rank // 2)
            two = chosen_row(vectors[8:16, (2 * pair + 1) * LANES : (2 * pair + 2) * LANES], 3 + rank // 2)
            one = jnp.where(upper, pltpu.roll(one, 64, 1), one)
            two = jnp.where(upper, two, pltpu.roll(two, 64, 1))
            joined = jnp.where(lane < 64, one, two)
            bias[0:1, pair * LANES : (pair + 1) * LANES] = joined[0:1, :]
        for part in range(3):
            place = 8 * part + rank
            held = chosen_row(vectors[8:16, aligned(place // 3, LANES)], place % 3)
            bias[1:2, part * LANES : (part + 1) * LANES] = held[0:1, :]

    forward_step(inputs, frequency, mix, expand, vectors, bias, *outs[:7])


def far_forward_body(info, inputs, mix, expand, vectors, bias, frequency, *outs):
    forward_step(inputs, frequency, mix, expand, vectors, bias, *outs)


def forward_step(
    rows, frequency, mix, expand, vectors, bias,
    normed_out, heads_out, tables_out, probs_out, context_out, act_out, slope_out,
):
    tokens = normed_out.shape[1]
    flat = (2 * tokens, normed_out.shape[2])
    rows = rows[...]
    inputs = rows[:, :tokens].reshape(flat).astype(F32)
    average = jnp.mean(inputs, axis=-1, keepdims=True)
    centred = inputs - average
    variance = jnp.mean(centred * centred, axis=-1, keepdims=True)
    normed = centred * lax.rsqrt(variance + EPSILON)
    one = (normed * vectors[0:1, :] + vectors[1:2, :]).astype(BF16)
    two = (normed * vectors[2:3, :] + vectors[3:4, :]).astype(BF16)
    normed_out[...] = normed.astype(BF16).reshape(normed_out.shape)
    mixed = nn(one, mix[...]) + bias[1:2, :MIX_COLS]

    row_index = lax.broadcasted_iota(jnp.int32, (tokens, tokens), 0)
    col_index = lax.broadcasted_iota(jnp.int32, (tokens, tokens), 1)
    lane = lax.broadcasted_iota(jnp.int32, (tokens, LANES), 1)
    for sequence in range(2):
        marks = rows[sequence, tokens : tokens + 16, :tokens].astype(F32)[0:1, :]
        across_marks = jnp.broadcast_to(marks, (tokens, tokens))
        same = across_marks == across_marks.T
        allowed = same & (col_index <= row_index)
        position = jnp.sum(jnp.where(same & (row_index < col_index), 1.0, 0.0), axis=0, keepdims=True)
        phases = jnp.broadcast_to(position, (8, tokens)) * frequency[0:8, 0:1]
        table = jnp.concatenate([jnp.cos(phases), jnp.sin(phases)], axis=0)
        tables_out[sequence] = table
        cos, sin = spread_tables(table)
        part = mixed[sequence * tokens : (sequence + 1) * tokens]
        queries = turn(part[:, :LANES], cos, sin, lane).astype(BF16)
        keys = turn(part[:, LANES : 2 * LANES], cos, sin, lane).astype(BF16)
        values = part[:, 2 * LANES :].astype(BF16)
        heads_out[sequence, :, :LANES] = queries
        heads_out[sequence, :, LANES : 2 * LANES] = keys
        heads_out[sequence, :, 2 * LANES :] = values
        scores = nt(by_head(queries * HEAD ** (-0.5), lane), keys)
        scores = jnp.where(jnp.concatenate([allowed, allowed]), scores, -1e30)
        weights = jnp.exp(scores - jnp.max(scores, axis=-1, keepdims=True))
        probs = weights * (1.0 / jnp.sum(weights, axis=-1, keepdims=True))
        probs = probs.astype(BF16)
        probs_out[sequence] = probs.reshape(2, tokens, tokens)
        context_out[sequence] = from_heads(nn(probs, values), lane).astype(BF16)

    hidden = nn(two, expand[...]) + bias[0:1, :]
    normal, slope = gelu_parts(hidden)
    act_out[...] = (hidden * normal).astype(BF16).reshape(act_out.shape)
    slope_out[...] = (normal + slope).astype(BF16).reshape(slope_out.shape)


def turn_constants():
    powers = np.power(np.float32(10000.0), -2.0 * np.arange(ROT // 2, dtype=np.float32) / np.float32(ROT))
    return np.tile(powers[:, None].astype(np.float32), (1, LANES))


def forward(info, inputs, weights, frequency, tokens, width, far=False):
    count = inputs.shape[0]
    outs = [
        ((count, tokens, width), BF16),
        ((count, tokens, MIX_COLS), BF16),
        ((count, 2 * 8, tokens), F32),
        ((count, 2, tokens, tokens), BF16),
        ((count, tokens, LANES), BF16),
        ((count, tokens, HIDDEN), BF16),
        ((count, tokens, HIDDEN), BF16),
    ]
    fixed = [((width, MIX_COLS), BF16), ((width, HIDDEN), BF16), ((SMALL, width), F32), ((8, HIDDEN), F32)]
    operands = [inputs] + list(weights) + [frequency]
    in_specs = [pairs(inputs.shape)] + [whole(operand.shape) for operand in operands[1:]]
    out_specs = [pairs(shape) for shape, _ in outs]
    if far:
        return call(far_forward_body, info, operands, in_specs, outs, out_specs, grid=(2,), micros=9)
    out_specs += [whole(shape) for shape, _ in fixed]
    return call(
        near_forward_body, info, operands, in_specs, outs + fixed, out_specs, grid=(2,), micros=9, vmem=VMEM_FIRST
    )


def pairs(shape, first=0):
    rest = (0,) * (len(shape) - 1)
    return pl.BlockSpec((2,) + shape[1:], lambda i, _: (i + first,) + rest)


def far_project_body(info, context, act, dense, along, across, out, shrink):
    @pl.when(pl.program_id(0) == 0)
    def _():
        for number in range(8):
            piece = across if number % 2 else along
            start = 64 * (number // 2)
            shrink[aligned(info[0] ^ number, 64), :] = piece[start : start + 64, :]

    near_project_body(info, context, act, dense, shrink, out)


def near_project_body(info, context, act, dense, shrink, out):
    rows = 2 * context.shape[1]
    total = nn(context[...].reshape(rows, LANES), dense[...]) + nn(act[...].reshape(rows, HIDDEN), shrink[...])
    out[...] = total.astype(BF16).reshape(out.shape)


def project(info, context, act, dense, shrink, far):
    tokens, width = context.shape[1], dense.shape[1]
    operands = [context, act, dense] + (list(shrink) if far else [shrink])
    in_specs = [pairs(context.shape), pairs(act.shape)]
    in_specs += [whole(operand.shape) for operand in operands[2:]]
    outs = [((4, tokens, width), BF16)] + [((HIDDEN, width), BF16)] * far
    out_specs = [pairs(outs[0][0])] + [whole((HIDDEN, width))] * far
    body = far_project_body if far else near_project_body
    return call(body, info, operands, in_specs, outs, out_specs, grid=(2,), micros=5)


def flat(ref):
    return ref[...].reshape(ref.shape[0] * ref.shape[1], ref.shape[2])


def clear(*refs):
    @pl.when(pl.program_id(0) == 0)
    def _():
        for ref in refs:
            ref[...] = jnp.zeros_like(ref)


def each_shard(info, mine, other):
    unit = mine.shape[0] // 4
    for place, z in enumerate((1, 0, 3, 2)):
        rows = pl.ds(place * unit, unit)
        yield info[0] ^ (2 * z), mine.at[rows]
        yield info[0] ^ (2 * z + 1), other.at[rows]


def last_grad_body(info, near, far, act, far_act, context, far_context, mine, other, dense_out, total, dense_total):
    step = pl.program_id(0)
    total[...] = tn(act[...], near[...]) + tn(far_act[...], far[...])
    dense_total[...] = tn(context[...], near[...]) + tn(far_context[...], far[...])
    for part in range(2):
        cols = slice(part * LANES, (part + 1) * LANES)
        for shard, out in each_shard(info, mine, other):
            out[pl.ds(pl.multiple_of(64 * (2 * step + part), 64), 64), :] = total[aligned(shard, 64), cols].astype(BF16)
        dense_out[pl.ds(pl.multiple_of(LANES * (2 * step + part), LANES), LANES), :] = dense_total[:, cols].astype(BF16)


def last_backward(info, near, far, act, context):
    operands = [array.reshape(-1, array.shape[2]) for array in (near, far) + act + context]
    near = operands[0]
    width = near.shape[1]
    outs = [((4 * HIDDEN, LANES), BF16)] * 2 + [((width, LANES), BF16)]
    columns = pl.BlockSpec((near.shape[0], 2 * LANES), lambda i, _: (0, i))
    return call(
        last_grad_body,
        info,
        operands,
        [columns, columns] + [whole(operand.shape) for operand in operands[2:]],
        outs,
        [whole(shape) for shape, _ in outs],
        grid=(width // (2 * LANES),),
        scratch=[pltpu.VMEM((HIDDEN, 2 * LANES), F32), pltpu.VMEM((LANES, 2 * LANES), F32)],
        micros=0,
    )


def as_column(row):
    size = row.shape[1]
    high = row.astype(BF16)
    middle = (row - high.astype(F32)).astype(BF16)
    low = (row - high.astype(F32) - middle.astype(F32)).astype(BF16)
    parts = jnp.concatenate([jnp.broadcast_to(part, (16, size)) for part in (high, middle, low)])
    first = lax.broadcasted_iota(jnp.int32, (48, LANES), 0) % 16 == 0
    return tn(parts, first.astype(BF16))


def norm_products(block, grads, normed, far_normed, column, weight, vectors, row, total, sums):
    count = normed.shape[0]
    products = tn(grads[:count, :], normed[...]) + tn(grads[count:, :], far_normed[...])
    lines = as_columns(weight[block, :])
    shifts = column[:, 0:1]
    total[:, block] = products * vectors[row : row + 1, block] + shifts * vectors[row + 1 : row + 2, block]
    sums[0:1, block] = jnp.sum(lines * products, axis=0, keepdims=True)
    sums[1:2, block] = jnp.sum(lines * shifts, axis=0, keepdims=True)


def expand_grad_body(
    info, near, far, slope, far_slope, normed, far_normed, shrink, expand, vectors, pre_out, bias_out, sums, mine, other, held, total, column
):
    step = pl.program_id(0)
    clear(bias_out, sums)

    @pl.when(step < 4)
    def _():
        cot = jnp.where(step < 2, near[...], far[...])
        grad_act = nt(cot.reshape(cot.shape[0] * cot.shape[1], cot.shape[2]), shrink[...])
        slopes = jnp.where(step < 2, slope[...], far_slope[...]).reshape(grad_act.shape).astype(F32)
        grad_pre = (grad_act * slopes).astype(BF16)
        pre_out[...] = grad_pre.reshape(pre_out.shape)
        held[pl.ds(pl.multiple_of(step * grad_pre.shape[0], grad_pre.shape[0]), grad_pre.shape[0]), :] = grad_pre
        bias_out[...] += jnp.broadcast_to(jnp.sum(grad_pre.astype(F32), axis=0, keepdims=True), bias_out.shape)

    @pl.when(step == 3)
    def _():
        column[...] = as_column(bias_out[0:1, :])

    @pl.when(step >= 4)
    def _():
        block = aligned(step - 4, 2 * LANES)
        norm_products(block, held, normed, far_normed, column, expand, vectors, 2, total, sums)

    @pl.when(step == 7)
    def _():
        for shard, out in each_shard(info, mine, other):
            out[...] = total[:, aligned(shard, LANES)].astype(BF16)


def two_phases(pair):
    shape = pair[0].shape
    block, rest = (2,) + shape[1:], (0,) * (len(shape) - 1)
    return [
        pl.BlockSpec(block, lambda i, _: (jnp.minimum(i, 1),) + rest),
        pl.BlockSpec(block, lambda i, _: (jnp.clip(i - 2, 0, 1),) + rest),
    ]


def all_tokens(rows):
    return [pl.BlockSpec((rows, 2 * LANES), lambda i, _: (0, jnp.maximum(i - 4, 0)))] * 2


def in_first_phase(shape):
    rest = (0,) * (len(shape) - 1)
    return pl.BlockSpec((2,) + shape[1:], lambda i, _: (jnp.minimum(i, 3),) + rest)


def expand_backward(info, near, far, slope, normed, shrink, expand, vectors):
    tokens, width = near.shape[1:]
    columns = [half.reshape(-1, width) for half in normed]
    operands = [near, far, *slope, *columns, shrink, expand, vectors]
    in_specs = two_phases((near, far)) + two_phases(slope) + all_tokens(columns[0].shape[0])
    in_specs += [whole(operand.shape) for operand in operands[6:]]
    outs = [((GROUP, tokens, HIDDEN), BF16), ((8, HIDDEN), F32), ((8, width), F32)] + [((4 * HIDDEN, LANES), BF16)] * 2
    out_specs = [in_first_phase(outs[0][0])] + [whole(shape) for shape, _ in outs[1:]]
    scratch = [
        pltpu.VMEM((GROUP * tokens, HIDDEN), BF16),
        pltpu.VMEM((HIDDEN, width), F32),
        pltpu.VMEM((HIDDEN, LANES), F32),
    ]
    return call(expand_grad_body, info, operands, in_specs, outs, out_specs, grid=(8,), scratch=scratch, micros=9)


def attention_grad_body(
    info, near, far, normed, far_normed, heads, far_heads, tables, far_tables, probs, far_probs,
    dense, frequency, mix, vectors, bias_grad, feed_sums,
    mixed_out, mine, other, mixed_held, total, column, sums, piece,
):
    step = pl.program_id(0)
    rank = info[1]
    tokens = near.shape[1]
    clear(sums)

    @pl.when(step == 0)
    def _():
        sums[4:5, :] = jnp.sum(near[0].astype(F32), axis=0, keepdims=True)

    @pl.when(step < 4)
    def _():
        cot = jnp.where(step < 2, near[...], far[...])
        all_heads = jnp.where(step < 2, heads[...], far_heads[...])
        all_tables = jnp.where(step < 2, tables[...], far_tables[...])
        all_probs = jnp.where(step < 2, probs[...], far_probs[...])
        lane = lax.broadcasted_iota(jnp.int32, (tokens, LANES), 1)
        grad_context = nt(cot.reshape(2 * tokens, cot.shape[2]), dense[...]).astype(BF16)
        for sequence in range(2):
            queries = all_heads[sequence, :, :LANES]
            keys = all_heads[sequence, :, LANES : 2 * LANES]
            values = all_heads[sequence, :, 2 * LANES :]
            part = by_head(grad_context[sequence * tokens : (sequence + 1) * tokens], lane)
            low = all_probs[sequence].reshape(2 * tokens, tokens)
            exact = low.astype(F32)
            grad_probs = nt(part, values)
            grad_scores = exact * (grad_probs - jnp.sum(exact * grad_probs, axis=-1, keepdims=True))
            grad_scores = grad_scores.astype(BF16)
            grad_values = tn(low, part)
            grad_queries = from_heads(nn(grad_scores, keys), lane)
            grad_keys = tn(grad_scores, by_head(queries, lane))
            cos, sin = spread_tables(all_tables[sequence])
            joined = [
                turn(grad_queries * HEAD ** (-0.5), cos, -sin, lane),
                turn(grad_keys * HEAD ** (-0.5), cos, -sin, lane),
                grad_values,
            ]
            grad_mixed = jnp.concatenate(joined, axis=1).astype(BF16)
            mixed_out[sequence] = grad_mixed
            mixed_held[pl.ds(pl.multiple_of((2 * step + sequence) * tokens, tokens), tokens), :] = grad_mixed
            sums[5:6, :MIX_COLS] += jnp.sum(grad_mixed.astype(F32), axis=0, keepdims=True)

    @pl.when(step == 3)
    def _():
        column[...] = as_column(sums[5:6, :MIX_COLS])

    @pl.when(step >= 4)
    def _():
        block = aligned(step - 4, 2 * LANES)
        norm_products(block, mixed_held, normed, far_normed, column, mix, vectors, 0, total, sums)

    @pl.when(step == 7)
    def _():
        sums[2:4, :] = feed_sums[0:2, :]
        line = lax.broadcasted_iota(jnp.int32, (8, LANES), 1)
        for shard, out in each_shard(info, mine, other):
            block = aligned(shard, LANES)
            out[:MIX_COLS, :] = total[:, block].astype(BF16)
            piece[...] = jnp.zeros_like(piece)
            piece[0:5, :] = sums[0:5, block]
            for row in range(3):
                place = 3 * shard + row
                spread = jnp.zeros((1, LANES), F32)
                for part in range(3):
                    held = sums[5:6, part * LANES : (part + 1) * LANES]
                    spread = spread + jnp.where(place == 8 * part + rank, held, 0.0)
                piece[5 + row : 6 + row, :] = spread
            packed = bias_grad[:, aligned(shard // 2, LANES)]
            moved = jnp.where(jnp.bitwise_and(shard ^ rank, 1) == 1, pltpu.roll(packed, 64, 1), packed)
            moved = jnp.where(line // 64 == jnp.bitwise_and(rank, 1), moved, 0.0)
            for row in range(4):
                piece[8 + row : 9 + row, :] = jnp.where(rank // 2 == row, moved[0:1, :], 0.0)
            out[MIX_COLS:, :] = piece[...].astype(BF16)


def attention_backward(info, near, far, saved, fixed):
    tokens, width = near.shape[1:]
    normed, *saved = saved
    columns = [half.reshape(-1, width) for half in normed]
    operands = [near, far, *columns]
    in_specs = two_phases((near, far)) + all_tokens(columns[0].shape[0])
    for pair in saved:
        operands += pair
        in_specs += two_phases(pair)
    operands += list(fixed)
    in_specs += [whole(operand.shape) for operand in fixed]
    outs = [((GROUP, tokens, MIX_COLS), BF16)] + [((4 * MIX_ROWS, LANES), BF16)] * 2
    out_specs = [in_first_phase(outs[0][0])] + [whole(shape) for shape, _ in outs[1:]]
    scratch = [
        pltpu.VMEM((GROUP * tokens, MIX_COLS), BF16),
        pltpu.VMEM((MIX_COLS, width), F32),
        pltpu.VMEM((MIX_COLS, LANES), F32),
        pltpu.VMEM((8, width), F32),
        pltpu.VMEM((SMALL, LANES), F32),
    ]
    return call(
        attention_grad_body, info, operands, in_specs, outs, out_specs, grid=(8,), scratch=scratch, micros=6
    )


def input_grad_body(info, mixed, pre, mix, expand, vectors, out):
    total = nt(flat(mixed), mix[...]) * vectors[0:1, :] + nt(flat(pre), expand[...]) * vectors[2:3, :]
    out[...] = total.astype(BF16).reshape(out.shape)


def input_backward(info, mixed, pre, mix, expand, vectors, far):
    tokens, width = mixed.shape[1], mix.shape[0]
    operands = [mixed, pre, mix, expand, vectors]
    in_specs = [pairs(mixed.shape, 2 * far), pairs(pre.shape, 2 * far)]
    in_specs += [whole(operand.shape) for operand in operands[2:]]
    shape = (4, tokens, width)
    micros = 0 if far else 6
    return call(input_grad_body, info, operands, in_specs, [(shape, BF16)], [pairs(shape)], grid=(2,), micros=micros)[0]


def norm_body(info, block, cot, upper, upper_got, lower, lower_got, out):
    inputs = block[...].astype(F32)
    average = jnp.mean(inputs, axis=-1, keepdims=True)
    centred = inputs - average
    scale = lax.rsqrt(jnp.mean(centred * centred, axis=-1, keepdims=True) + EPSILON)
    normed = centred * scale
    pulled = jnp.concatenate(
        [upper[...] + upper_got[...].astype(F32), lower[...] + lower_got[...].astype(F32)]
    )
    pulled = pulled - jnp.mean(pulled, axis=-1, keepdims=True) - normed * jnp.mean(pulled * normed, axis=-1, keepdims=True)
    out[...] = cot[...].astype(F32) + scale * pulled


def each_rank(near, far, unit):
    for place, number in enumerate(NEAR):
        rows = pl.ds(place * unit, unit)
        yield number, near.at[rows], far.at[rows]


def last_out_body(info, near, far, own_dense, shrink_out, dense_out):
    rank = info[1]
    for number, one, two in each_rank(near, far, HIDDEN):
        for piece, held in ((one, rank ^ number), (two, rank ^ number ^ 1)):
            for part in range(8):
                rows = piece[64 * part : 64 * (part + 1), :]
                shrink_out[aligned(held, 64), part * LANES : (part + 1) * LANES] = rows.astype(F32)
    for part in range(8):
        start = 4 * HIDDEN + part * LANES
        rows = jnp.where(own_dense[0] == 1, near[start : start + LANES, :], far[start : start + LANES, :])
        dense_out[:, part * LANES : (part + 1) * LANES] = rows.astype(F32)


def expand_out_body(info, near, far, out):
    rank = info[1]
    upper = jnp.bitwise_and(rank, 1) == 1
    for number, one, two in each_rank(near, far, HIDDEN):
        place = (rank ^ number) // 2
        for shard in range(8):
            rows = slice(64 * shard, 64 * (shard + 1))
            lower_rows = jnp.where(upper, two[rows, :], one[rows, :])
            upper_rows = jnp.where(upper, one[rows, :], two[rows, :])
            joined = jnp.concatenate([lower_rows, upper_rows], axis=0)
            out[:, aligned(4 * shard + place, LANES)] = as_columns(joined)


def mix_out_body(info, near, far, out):
    rank = info[1]
    for number, one, two in each_rank(near, far, MIX_ROWS):
        for piece, place in ((one, rank ^ number), (two, rank ^ number ^ 1)):
            for part in range(3):
                out[:, aligned(8 * part + place, LANES)] = as_columns(piece[part * LANES : (part + 1) * LANES, :])


def after(value, *others):
    return jax.tree.map(lambda leaf: lax.optimization_barrier((leaf,) + others)[0], value)


def mark_body(info, out):
    out[...] = jnp.zeros_like(out) + info[0].astype(F32)


def mark(info, *others):
    return call(mark_body, after(info, *others), [], [], [((8, LANES), F32)], [whole((8, LANES))], micros=40)[0]


def gather_first(upper, lower):
    return swap(upper, x=1), swap(lower, low=1)


def gather_second(upper, lower, upper_x, lower_low):
    return swap(jnp.stack([upper, upper_x]), low=1), swap(jnp.stack([lower, lower_low]), x=1)


def gathered(upper, lower, upper_x, lower_low, upper_pair, lower_pair):
    return jnp.concatenate(
        [
            jnp.stack([upper, upper_pair[0], upper_x, upper_pair[1]]),
            jnp.stack([lower, lower_low, lower_pair[0], lower_pair[1]]),
        ],
        axis=1,
    )


def reduce_first(mine, other, unit, *late):
    got = after(swap(other, y=1), *late)
    total = mine.astype(F32) + got.astype(F32)
    return total[: 2 * unit], total[2 * unit :].astype(BF16)


def reduce_second(kept, sent, *late):
    return (kept + after(swap(sent, high=1), *late).astype(F32)).astype(BF16)


def share_first(slices, unit, *late):
    return jnp.concatenate([slices[unit:], after(swap(slices[:unit], low=1), *late)])


def share_second(pair, *late):
    return after(swap(pair, x=1), *late)


def scatter_first(near, far_got):
    cut = near.shape[1] // 2
    total = near.astype(F32) + far_got.astype(F32)
    sent_x = total[2:, :cut].astype(BF16)
    sent_low = total[1::2, cut:].astype(BF16)
    return total[:2, :cut], sent_x, total[0::2, cut:], sent_low


def scatter_second(kept_x, sent_x, kept_low, sent_low, *late):
    upper = kept_x + after(swap(sent_x, x=1), *late).astype(F32)
    lower = kept_low + after(swap(sent_low, low=1), *late).astype(F32)
    return upper[0], upper[1].astype(BF16), lower[0], lower[1].astype(BF16)


def scatter_third(upper, sent_upper, lower, sent_lower, *late):
    upper = upper + after(swap(sent_upper, low=1), *late).astype(F32)
    lower = lower + after(swap(sent_lower, x=1), *late).astype(F32)
    return jnp.concatenate([upper, lower])


def local(
    block_input,
    segments,
    cotangent,
    first_gain,
    first_shift,
    mix_weight,
    mix_bias,
    dense_weight,
    dense_bias,
    second_gain,
    second_shift,
    expand_weight,
    expand_bias,
    shrink_weight,
    shrink_bias,
):
    rep = lax.axis_index("rep")
    shard = lax.axis_index("fsdp")
    x, core, high, low, y = rep // 2, rep % 2, shard // 4, (shard // 2) % 2, shard % 2
    info = jnp.stack([shard, 4 * x + 2 * low + core]).astype(jnp.int32)
    tokens, width = block_input.shape
    rows = mix_weight.shape[0]

    own_y, own_x = y == core, x == high

    small = (first_gain, first_shift, second_gain, second_shift, dense_bias, shrink_bias, mix_bias, expand_bias)
    half = tokens // 2
    own, other = cut_slices(info, mix_weight, expand_weight, small)
    marks = jnp.pad(segments.astype(BF16), ((0, 15), (0, width - tokens)))
    upper, lower = block_input[:half], jnp.concatenate([block_input[half:], marks])
    along = swap(other, low=1), swap(own, high=1), swap(other, high=1, low=1)
    upper_x, lower_low = gather_first(upper, lower)
    first = mark(info, own)
    upper_x, lower_low = after((upper_x, lower_low), first)
    over = swap(after(own, first), y=1)
    upper_pair = swap(jnp.stack([upper, upper_x]), low=1)
    lower_in = jnp.stack([lower, lower_low])
    second = mark(info, upper_x, lower_in)
    along = jnp.stack(after(along, second, over))
    across = swap(along, y=1)
    lower_pair = swap(after(lower_in, along), x=1)

    high_in, low_in, other_shrink = cut_last(after(info, first), shrink_weight, dense_weight, cotangent)
    high_last = swap(after(high_in, along), high=1)
    low_last = swap(after(low_in, along), low=1)
    third = mark(info, along, high_in, low_in)
    upper_pair, lower_pair, across = after((upper_pair, lower_pair, across), third)
    near = gathered(upper, lower, upper_x, lower_low, upper_pair, lower_pair)
    both_last = swap(after(other_shrink, near), high=1, low=1)
    far = swap(near, core=1)
    cot_upper = after(cotangent[:half], near)
    cot_upper_x = swap(cot_upper, x=1)
    frequency = jnp.asarray(turn_constants())
    *near_saved, mix, expand, vectors, bias = forward(info, near, (own, over, along, across), frequency, tokens, width)
    high_last, low_last, both_last, cot_upper_x, far = after((high_last, low_last, both_last, cot_upper_x, far), mix)
    last, dense_held = pack_last(info, high_in, low_last, high_last, both_last, dense_weight)
    last_across = swap(last, y=1)
    cot_pairs = gather_second(cot_upper, cotangent[half:], cot_upper_x, low_last[64:])
    far = after(far, last, cot_upper_x)
    cot_near = gathered(cot_upper, cotangent[half:], cot_upper_x, low_last[64:], *cot_pairs)
    cot_far = swap(cot_near, core=1)
    far = after(far, cot_near)
    far_saved = forward(info, far, (mix, expand, vectors, bias), frequency, tokens, width, True)
    normed, heads, tables, probs, context, act, slope = zip(near_saved, far_saved)
    last_mine, last_other, dense_grad = last_backward(info, cot_near, cot_far, act, context)
    last_across = after(last_across, context[1])
    dense = jnp.where(own_y, dense_held, last_across[256:])
    branch_far, shrink = project(info, after(context[1], last_mine), act[1], dense, (last, last_across), True)
    branch_got = swap(branch_far, core=1)
    (branch_near,) = project(info, context[0], act[0], dense, shrink, False)
    branch_sum = (branch_near.astype(F32) + branch_got.astype(F32)).astype(BF16)
    branch_kept, branch_sent = branch_sum[:2], branch_sum[2:]
    grad_pre, bias_grad, feed_sums, expand_mine, expand_other = expand_backward(
        info, cot_near, cot_far, slope, normed, after(shrink, branch_sent), expand, vectors
    )
    last_part = reduce_first(last_mine, last_other, HIDDEN, grad_pre)
    dense_got = after(swap(dense_grad, high=1), grad_pre)
    dense_grad = (dense_grad.astype(F32) + dense_got.astype(F32)).astype(BF16)
    grad_mixed, mix_mine, mix_other = attention_backward(
        info,
        cot_near,
        cot_far,
        (normed, heads, tables, probs),
        (after(dense, last_part[1], dense_grad), frequency, mix, vectors, bias_grad, feed_sums),
    )
    branch = branch_kept.astype(F32) + after(swap(branch_sent, x=1), grad_mixed).astype(F32)
    branch_own, branch_last = branch[0].astype(BF16), branch[1].astype(BF16)
    last_slices = reduce_second(*last_part, grad_mixed)
    dense_got = after(swap(dense_grad, y=1), grad_mixed)
    dense_grad = (dense_grad.astype(F32) + dense_got.astype(F32)).astype(BF16)
    expand_part = reduce_first(expand_mine, expand_other, HIDDEN, grad_mixed)
    error_far = input_backward(
        info,
        after(grad_mixed, branch_own, branch_last, last_slices, dense_grad, expand_part[1]),
        grad_pre,
        mix,
        expand,
        vectors,
        True,
    )
    error_got = swap(error_far, core=1)
    error_near = input_backward(
        info, after(grad_mixed, error_far), grad_pre, mix, expand, vectors, False
    )
    mix_part = reduce_first(mix_mine, mix_other, MIX_ROWS, error_near)
    last_pair = share_first(last_slices, HIDDEN, error_near)
    dense_x = after(swap(dense_grad, x=1), error_near)
    dense_part = jnp.where(own_x, dense_grad, dense_x)
    error = scatter_first(after(error_near, mix_part[1], last_pair), error_got)
    fourth = mark(info, last_pair, mix_part[1], error[1], error[3], dense_part)
    expand_slices = reduce_second(*expand_part, fourth)
    last_x = share_second(last_pair, fourth)
    last_near = jnp.concatenate([last_pair, last_x, dense_part])
    mix_slices = reduce_second(*mix_part, fourth)
    error = scatter_second(*error, fourth)
    fifth = mark(info, expand_slices, mix_slices, error[1], error[3], last_near)
    expand_pair = share_first(expand_slices, HIDDEN, fifth)
    mix_pair = share_first(mix_slices, MIX_ROWS, fifth)
    last_far = swap(after(last_near, mix_pair), core=1)

    def out(body, near, far, shapes, flag=None):
        operands = [near, far]
        in_specs = [whole(near.shape), whole(far.shape)]
        if flag is not None:
            operands.append(flag)
            in_specs.append(pl.BlockSpec(memory_space=pltpu.SMEM))
        return call(body, info, operands, in_specs, [(shape, F32) for shape in shapes], [whole(shape) for shape in shapes])

    flag = own_y.astype(jnp.int32).reshape(1)
    shapes = [shrink_weight.shape, dense_weight.shape]
    upper_got = after(swap(error[1], low=1), mix_pair, expand_pair)
    lower_got = after(swap(error[3], x=1), mix_pair, expand_pair)
    operands = [block_input, cotangent, error[0], upper_got, error[2], lower_got]
    (input_grad,) = call(
        norm_body,
        info,
        operands,
        [whole(operand.shape) for operand in operands],
        [(block_input.shape, F32)],
        [whole(block_input.shape)],
    )
    shrink_out, dense_out = out(last_out_body, last_near, after(last_far, input_grad), shapes, flag)
    expand_near = jnp.concatenate([expand_pair, share_second(expand_pair, shrink_out)])
    expand_far = swap(expand_near, core=1)
    (expand_out,) = out(expand_out_body, expand_near, expand_far, [expand_weight.shape])
    branch = branch_own.astype(F32) + after(swap(after(branch_last, mix_pair), low=1), expand_near).astype(F32)
    block_out = (block_input.astype(F32) + branch + (vectors[4] + vectors[5])).astype(BF16)
    mix_x = share_second(mix_pair, expand_near)
    mix_parts = [mix_pair[:MIX_ROWS], mix_pair[MIX_ROWS:], mix_x[:MIX_ROWS], mix_x[MIX_ROWS:]]
    mix_sums = [part[MIX_COLS:].astype(F32) for part in mix_parts]
    mix_sums = ((mix_sums[0] + mix_sums[1]) + (mix_sums[2] + mix_sums[3])).astype(BF16)
    near = jnp.concatenate(mix_parts + [mix_sums])
    far = swap(near, core=1)
    sums = mix_sums.astype(F32) + far[4 * MIX_ROWS :].astype(F32)
    (mix_out,) = out(mix_out_body, near, far, [mix_weight.shape])
    return (
        block_out,
        input_grad,
        sums[0],
        sums[1],
        mix_out,
        sums[5:8].reshape(-1),
        dense_out,
        sums[4],
        sums[2],
        sums[3],
        expand_out,
        sums[8:12].reshape(-1),
        shrink_out,
        sums[4],
    )


def solution(mesh):
    tensor_parallel = mesh.shape["rep"] == TP_REP and mesh.shape["fsdp"] == TP_FSDP
    return jax.shard_map(
        local if tensor_parallel else local_general,
        mesh=mesh,
        in_specs=(
            P(("rep", "fsdp"), None),
            P(("rep", "fsdp"), None),
            P(("rep", "fsdp"), None),
            P("fsdp"),
            P("fsdp"),
            P("fsdp", None),
            P("fsdp"),
            P("fsdp", None),
            P("fsdp"),
            P("fsdp"),
            P("fsdp"),
            P("fsdp", None),
            P("fsdp"),
            P("fsdp", None),
            P("fsdp"),
        ),
        out_specs=(
            P(("rep", "fsdp"), None),
            P(("rep", "fsdp"), None),
            P("fsdp"),
            P("fsdp"),
            P("fsdp", None),
            P("fsdp"),
            P("fsdp", None),
            P("fsdp"),
            P("fsdp"),
            P("fsdp"),
            P("fsdp", None),
            P("fsdp"),
            P("fsdp", None),
            P("fsdp"),
        ),
        check_vma=False,
    )
```

```python
import jax
import jax.numpy as jnp
import numpy as np
from jax import lax
from jax.experimental import pallas as pl
from jax.experimental.pallas import tpu as pltpu
from jax.sharding import PartitionSpec as P

HEADS = 16
HEAD = 64
ROT = 16


EPSILON = 1e-05


def layer_norm(inputs, gain_row, shift_row):
    average = jnp.mean(inputs, axis=-1, keepdims=True)
    centred = inputs - average
    variance = jnp.mean(centred * centred, axis=-1, keepdims=True)
    return centred * lax.rsqrt(variance + EPSILON) * gain_row + shift_row


def rotate(heads_in, cos_table, sin_table):
    half_rot = ROT // 2
    first_half = heads_in[..., :half_rot]
    second_half = heads_in[..., half_rot:ROT]
    return jnp.concatenate(
        [
            first_half * cos_table - second_half * sin_table,
            second_half * cos_table + first_half * sin_table,
            heads_in[..., ROT:],
        ],
        axis=-1,
    )


def rotary_tables(segment_row):
    length = segment_row.shape[0]
    same_doc = segment_row[:, None] == segment_row[None, :]
    row_index = lax.broadcasted_iota(jnp.int32, (length, length), 0)
    col_index = lax.broadcasted_iota(jnp.int32, (length, length), 1)
    earlier = jnp.where(same_doc & (col_index < row_index), 1.0, 0.0)
    position = jnp.sum(earlier, axis=-1).astype(jnp.float32)
    allowed = same_doc & (col_index <= row_index)
    frequency = jnp.power(10000.0, -2.0 * jnp.arange(ROT // 2).astype(jnp.float32) / ROT)
    phases = position[:, None] * frequency
    return (jnp.cos(phases)[:, None, :], jnp.sin(phases)[:, None, :], allowed)


def product_left(left, right):
    return lax.dot_general(
        left, right, (((0,), (0,)), ((), ())), preferred_element_type=jnp.float32
    )


def product_right(left, right):
    return lax.dot_general(
        left, right, (((1,), (1,)), ((), ())), preferred_element_type=jnp.float32
    )


def norm_backward(inputs, gain_row, shift_row, upstream):
    _, pullback = jax.vjp(layer_norm, inputs, gain_row, shift_row)
    return pullback(upstream)


def local_general(
    block_input,
    segments,
    cotangent,
    first_gain,
    first_shift,
    mix_weight,
    mix_bias,
    dense_weight,
    dense_bias,
    second_gain,
    second_shift,
    expand_weight,
    expand_bias,
    shrink_weight,
    shrink_bias,
):
    attention_parts = (
        lax.all_gather(first_gain, "fsdp", axis=0, tiled=True),
        lax.all_gather(first_shift, "fsdp", axis=0, tiled=True),
        lax.all_gather(mix_weight, "fsdp", axis=0, tiled=True),
        lax.all_gather(mix_bias, "fsdp", axis=0, tiled=True),
        lax.all_gather(dense_weight, "fsdp", axis=0, tiled=True),
        lax.all_gather(dense_bias, "fsdp", axis=0, tiled=True),
    )
    feed_parts = (
        lax.all_gather(second_gain, "fsdp", axis=0, tiled=True),
        lax.all_gather(second_shift, "fsdp", axis=0, tiled=True),
        lax.all_gather(expand_weight, "fsdp", axis=0, tiled=True),
        lax.all_gather(expand_bias, "fsdp", axis=0, tiled=True),
        lax.all_gather(shrink_weight, "fsdp", axis=0, tiled=True),
        lax.all_gather(shrink_bias, "fsdp", axis=0, tiled=True),
    )
    token_count = block_input.shape[0]
    feature_count = block_input.shape[1]
    score_scale = HEAD ** (-0.5)
    block_float = block_input.astype(jnp.float32)
    cot_float = cotangent.astype(jnp.float32)
    cos_table, sin_table, allowed = rotary_tables(segments[0])
    normed_one = layer_norm(
        block_float, attention_parts[0].astype(jnp.float32), attention_parts[1].astype(jnp.float32)
    ).astype(jnp.bfloat16)
    mixed_rows = jnp.dot(normed_one, attention_parts[2], preferred_element_type=jnp.float32)
    mixed_rows = mixed_rows + attention_parts[3].astype(jnp.float32)
    triple = mixed_rows.reshape(token_count, 3, HEADS, HEAD)
    queries = rotate(triple[:, 0], cos_table, sin_table).astype(jnp.bfloat16)
    keys_all = rotate(triple[:, 1], cos_table, sin_table).astype(jnp.bfloat16)
    values_all = triple[:, 2].astype(jnp.bfloat16)

    def masked_scores():
        raw_scores = (
            jnp.einsum("qhd,khd->hqk", queries, keys_all, preferred_element_type=jnp.float32)
            * score_scale
        )
        return jnp.where(allowed[None], raw_scores, -1e30)

    forward_scores = masked_scores()
    row_peak = jnp.max(forward_scores, axis=-1, keepdims=True)
    weights_raw = jnp.exp(forward_scores - row_peak)
    row_total = jnp.sum(weights_raw, axis=-1, keepdims=True)
    log_total = row_peak + jnp.log(row_total)
    probs_low = (weights_raw / row_total).astype(jnp.bfloat16)
    context = jnp.einsum("hqk,khd->qhd", probs_low, values_all, preferred_element_type=jnp.float32)
    context = context.reshape(token_count, feature_count).astype(jnp.bfloat16)
    attention_branch = jnp.dot(context, attention_parts[4], preferred_element_type=jnp.float32)
    attention_branch = attention_branch + attention_parts[5].astype(jnp.float32)
    normed_two = layer_norm(
        block_float, feed_parts[0].astype(jnp.float32), feed_parts[1].astype(jnp.float32)
    ).astype(jnp.bfloat16)
    hidden_pre = jnp.dot(normed_two, feed_parts[2], preferred_element_type=jnp.float32)
    hidden_pre = hidden_pre + feed_parts[3].astype(jnp.float32)
    hidden_act = jax.nn.gelu(hidden_pre, approximate=False).astype(jnp.bfloat16)
    feedforward_branch = jnp.dot(hidden_act, feed_parts[4], preferred_element_type=jnp.float32)
    feedforward_branch = feedforward_branch + feed_parts[5].astype(jnp.float32)
    block_out = (block_float + attention_branch + feedforward_branch).astype(jnp.bfloat16)
    feed_back = (
        lax.all_gather(second_gain, "fsdp", axis=0, tiled=True),
        lax.all_gather(second_shift, "fsdp", axis=0, tiled=True),
        lax.all_gather(expand_weight, "fsdp", axis=0, tiled=True),
        lax.all_gather(expand_bias, "fsdp", axis=0, tiled=True),
        lax.all_gather(shrink_weight, "fsdp", axis=0, tiled=True),
        lax.all_gather(shrink_bias, "fsdp", axis=0, tiled=True),
    )
    bias_sum = jnp.sum(cot_float, axis=0)
    shrink_grad = product_left(hidden_act, cotangent)
    grad_act = product_right(cotangent, feed_back[4])
    _, gelu_pull = jax.vjp(lambda pre_value: jax.nn.gelu(pre_value, approximate=False), hidden_pre)
    grad_pre = gelu_pull(grad_act)[0].astype(jnp.bfloat16)
    expand_grad = product_left(normed_two, grad_pre)
    expand_bias_grad = jnp.sum(grad_pre.astype(jnp.float32), axis=0)
    grad_normed_two = product_right(grad_pre, feed_back[2])
    part_two, second_gain_grad, second_shift_grad = norm_backward(
        block_float,
        feed_back[0].astype(jnp.float32),
        feed_back[1].astype(jnp.float32),
        grad_normed_two,
    )
    feed_grads = (
        lax.psum_scatter(second_gain_grad, "fsdp", scatter_dimension=0, tiled=True),
        lax.psum_scatter(second_shift_grad, "fsdp", scatter_dimension=0, tiled=True),
        lax.psum_scatter(expand_grad, "fsdp", scatter_dimension=0, tiled=True),
        lax.psum_scatter(expand_bias_grad, "fsdp", scatter_dimension=0, tiled=True),
        lax.psum_scatter(shrink_grad, "fsdp", scatter_dimension=0, tiled=True),
        lax.psum_scatter(bias_sum, "fsdp", scatter_dimension=0, tiled=True),
    )
    gain_two_sum, shift_two_sum, expand_sum, expand_bias_sum, shrink_sum, shrink_bias_sum = (
        feed_grads
    )
    attention_back = (
        lax.all_gather(first_gain, "fsdp", axis=0, tiled=True),
        lax.all_gather(first_shift, "fsdp", axis=0, tiled=True),
        lax.all_gather(mix_weight, "fsdp", axis=0, tiled=True),
        lax.all_gather(mix_bias, "fsdp", axis=0, tiled=True),
        lax.all_gather(dense_weight, "fsdp", axis=0, tiled=True),
        lax.all_gather(dense_bias, "fsdp", axis=0, tiled=True),
    )
    dense_grad = product_left(context, cotangent)
    grad_context = product_right(cotangent, attention_back[4]).astype(jnp.bfloat16)
    grad_context = grad_context.reshape(token_count, HEADS, HEAD)
    grad_values = jnp.einsum(
        "hqk,qhd->khd", probs_low, grad_context, preferred_element_type=jnp.float32
    )
    grad_probs = jnp.einsum(
        "qhd,khd->hqk", grad_context, values_all, preferred_element_type=jnp.float32
    )
    probs_exact = jnp.exp(masked_scores() - log_total)
    grad_scores = probs_exact * (
        grad_probs - jnp.sum(probs_exact * grad_probs, axis=-1, keepdims=True)
    )
    grad_scores = grad_scores.astype(jnp.bfloat16)
    grad_queries = (
        jnp.einsum("hqk,khd->qhd", grad_scores, keys_all, preferred_element_type=jnp.float32)
        * score_scale
    )
    grad_keys = (
        jnp.einsum("hqk,qhd->khd", grad_scores, queries, preferred_element_type=jnp.float32)
        * score_scale
    )
    _, rotate_pull = jax.vjp(lambda heads_in: rotate(heads_in, cos_table, sin_table), grad_queries)
    grad_mixed = jnp.stack(
        [rotate_pull(grad_queries)[0], rotate_pull(grad_keys)[0], grad_values], axis=1
    )
    grad_mixed = grad_mixed.reshape(token_count, 3 * feature_count).astype(jnp.bfloat16)
    mix_grad = product_left(normed_one, grad_mixed)
    mix_bias_grad = jnp.sum(grad_mixed.astype(jnp.float32), axis=0)
    grad_normed_one = product_right(grad_mixed, attention_back[2])
    part_one, first_gain_grad, first_shift_grad = norm_backward(
        block_float,
        attention_back[0].astype(jnp.float32),
        attention_back[1].astype(jnp.float32),
        grad_normed_one,
    )
    attention_grads = (
        lax.psum_scatter(first_gain_grad, "fsdp", scatter_dimension=0, tiled=True),
        lax.psum_scatter(first_shift_grad, "fsdp", scatter_dimension=0, tiled=True),
        lax.psum_scatter(mix_grad, "fsdp", scatter_dimension=0, tiled=True),
        lax.psum_scatter(mix_bias_grad, "fsdp", scatter_dimension=0, tiled=True),
        lax.psum_scatter(dense_grad, "fsdp", scatter_dimension=0, tiled=True),
        lax.psum_scatter(bias_sum, "fsdp", scatter_dimension=0, tiled=True),
    )
    gain_one_sum, shift_one_sum, mix_sum, mix_bias_sum, dense_sum, dense_bias_sum = attention_grads
    (
        gain_one_sum,
        shift_one_sum,
        mix_sum,
        mix_bias_sum,
        dense_sum,
        dense_bias_sum,
        gain_two_sum,
        shift_two_sum,
        expand_sum,
        expand_bias_sum,
        shrink_sum,
        shrink_bias_sum,
    ) = lax.psum(
        (
            gain_one_sum,
            shift_one_sum,
            mix_sum,
            mix_bias_sum,
            dense_sum,
            dense_bias_sum,
            gain_two_sum,
            shift_two_sum,
            expand_sum,
            expand_bias_sum,
            shrink_sum,
            shrink_bias_sum,
        ),
        "rep",
    )
    input_grad = cot_float + part_one + part_two
    return (
        block_out,
        input_grad,
        gain_one_sum,
        shift_one_sum,
        mix_sum,
        mix_bias_sum,
        dense_sum,
        dense_bias_sum,
        gain_two_sum,
        shift_two_sum,
        expand_sum,
        expand_bias_sum,
        shrink_sum,
        shrink_bias_sum,
    )


TP_REP = 4
TP_FSDP = 8
GROUP = 8
NEAR = (0, 2, 4, 6)
MIX_COLS = 384
HIDDEN = 512
SMALL = 16
LANES = 128
FIRST_ROWS = MIX_COLS + SMALL + HIDDEN
MIX_ROWS = MIX_COLS + SMALL
DENSE_START = FIRST_ROWS + HIDDEN
F32 = jnp.float32
BF16 = jnp.bfloat16
COST = 5000
VMEM_LIMIT = 18 * 1024 * 1024
VMEM_FIRST = 28 * 1024 * 1024
VMEM_WHOLE = 56 * 1024 * 1024


def permute(value, target):
    pairs = []
    for rep in range(TP_REP):
        for shard in range(TP_FSDP):
            goal = target(rep // 2, rep % 2, shard // 4, (shard // 2) % 2, shard % 2)
            if goal is not None:
                x, core, high, low, y = goal
                pairs.append((rep * TP_FSDP + shard, (2 * x + core) * TP_FSDP + 4 * high + 2 * low + y))
    return lax.ppermute(value, ("rep", "fsdp"), pairs)


def swap(value, x=0, core=0, high=0, low=0, y=0):
    return permute(value, lambda a, b, c, d, e: (a ^ x, b ^ core, c ^ high, d ^ low, e ^ y))


def nt(left, right):
    return lax.dot_general(left, right, (((1,), (1,)), ((), ())), preferred_element_type=F32)


def nn(left, right):
    return lax.dot_general(left, right, (((1,), (0,)), ((), ())), preferred_element_type=F32)


def tn(left, right):
    return lax.dot_general(left, right, (((0,), (0,)), ((), ())), preferred_element_type=F32)


def whole(shape):
    return pl.BlockSpec(shape, lambda *_: (0,) * len(shape))


def call(body, info, operands, in_specs, outs, out_specs, grid=(1,), scratch=(), micros=4, vmem=VMEM_LIMIT):
    return pl.pallas_call(
        body,
        grid_spec=pltpu.PrefetchScalarGridSpec(
            num_scalar_prefetch=1,
            grid=grid,
            in_specs=in_specs,
            out_specs=out_specs,
            scratch_shapes=list(scratch),
        ),
        out_shape=[jax.ShapeDtypeStruct(shape, dtype) for shape, dtype in outs],
        compiler_params=pltpu.CompilerParams(vmem_limit_bytes=vmem),
        cost_estimate=pl.CostEstimate(flops=micros * COST * 10**6, bytes_accessed=micros * COST * 3 * 10**3, transcendentals=0),
    )(info, *operands)


def as_columns(matrix):
    size = matrix.shape[1]
    rows = lax.broadcasted_iota(jnp.int32, (size, size), 0)
    cols = lax.broadcasted_iota(jnp.int32, (size, size), 1)
    return nt((rows == cols).astype(BF16), matrix)


def aligned(index, unit):
    return pl.ds(pl.multiple_of(index * unit, unit), unit)


def cut_body(info, mix, expand, shrink, dense, *rest):
    vectors, (own, other, own_all), small = rest[:8], rest[8:11], rest[11]
    row = 0
    small[...] = jnp.zeros_like(small)
    for vector in vectors:
        count = vector.shape[0]
        small[row : row + count, :] = vector[...].astype(F32)
        row = row + count if row + count != 6 else 8
    lane = lax.broadcasted_iota(jnp.int32, (LANES, LANES), 1)
    for out, rank in ((own, info[1]), (other, info[1] ^ 2)):
        for part in range(3):
            out[part * LANES : (part + 1) * LANES, :] = mix[:, aligned(8 * part + rank, LANES)]
        out[MIX_COLS:MIX_ROWS, :] = small[...].astype(BF16)
        upper = jnp.bitwise_and(rank, 1) == 1
        for pair in range(4):
            first = expand[:, aligned(8 * pair + rank // 2, LANES)].astype(F32)
            second = expand[:, aligned(8 * pair + 4 + rank // 2, LANES)].astype(F32)
            first = jnp.where(upper, pltpu.roll(first, 64, 1), first)
            second = jnp.where(upper, second, pltpu.roll(second, 64, 1))
            joined = jnp.where(lane < 64, first, second).astype(BF16)
            out[MIX_ROWS + pair * LANES : MIX_ROWS + (pair + 1) * LANES, :] = joined
    own_all[:FIRST_ROWS, :] = own[...]
    rows = shrink[aligned(info[1], 64), :]
    for part in range(8):
        cols = slice(part * LANES, (part + 1) * LANES)
        own_all[FIRST_ROWS + 64 * part : FIRST_ROWS + 64 * (part + 1), :] = rows[:, cols]
        own_all[DENSE_START + LANES * part : DENSE_START + LANES * (part + 1), :] = dense[:, cols]


def cut_slices(info, mix, expand, shrink, dense, vectors):
    operands = [mix, expand, shrink, dense] + [vector.reshape(-1, LANES) for vector in vectors]
    outs = [((rows, LANES), BF16) for rows in (FIRST_ROWS, FIRST_ROWS, DENSE_START + shrink.shape[1])]
    return call(
        cut_body,
        info,
        operands,
        [whole(operand.shape) for operand in operands],
        outs,
        [whole(shape) for shape, _ in outs],
        scratch=[pltpu.VMEM((SMALL, LANES), F32)],
        vmem=VMEM_WHOLE,
    )


def cut_last_body(info, shrink, dense, cot, over, own, other, other_shrink):
    rows = cot.shape[0] // 2
    own[:64, :] = shrink[aligned(info[1], 64), :]
    mine = jnp.bitwise_and(info[0] ^ info[1], 1) == 0
    for part in range(8):
        cols = slice(part * LANES, (part + 1) * LANES)
        start = DENSE_START + part * LANES
        own[64:, cols] = jnp.where(mine, dense[:, cols], over[start : start + LANES, :])
    rest = shrink[aligned(info[1] ^ 2, 64), :]
    other_shrink[...] = rest
    other[:64, :] = rest
    other[64:, :] = cot[rows:, :]


def cut_last(info, shrink, dense, cot, over):
    operands = [shrink, dense, cot, over]
    shapes = [(64 + rows, shrink.shape[1]) for rows in (dense.shape[0], cot.shape[0] // 2, 0)]
    return call(
        cut_last_body,
        info,
        operands,
        [whole(operand.shape) for operand in operands],
        [(shape, BF16) for shape in shapes],
        [whole(shape) for shape in shapes],
        vmem=VMEM_WHOLE,
    )


def pack_body(info, own, low, high, both, out, dense):
    out[:64, :] = low[:64, :]
    out[64:128, :] = high[:64, :]
    out[128:, :] = both[...]
    same = info[1] // 4 == info[0] // 4
    dense[...] = jnp.where(same, own[64:, :], high[64:, :])


def pack_last(info, own, low, high, both):
    operands = [own, low, high, both]
    width = own.shape[1]
    shapes = [(192, width), (own.shape[0] - 64, width)]
    return call(
        pack_body,
        info,
        operands,
        [whole(operand.shape) for operand in operands],
        [(shape, BF16) for shape in shapes],
        [whole(shape) for shape in shapes],
    )


def turn(heads, cos, sin, lane):
    ahead = pltpu.roll(heads, LANES - 8, 1)
    behind = pltpu.roll(heads, 8, 1)
    return heads * cos + jnp.where(lane % HEAD < 8, -ahead, behind) * sin


def spread_tables(table):
    high = table.astype(BF16)
    low = (table - high.astype(F32)).astype(BF16)
    row = lax.broadcasted_iota(jnp.int32, (32, 2 * LANES), 0)
    lane = lax.broadcasted_iota(jnp.int32, (32, 2 * LANES), 1)
    goes = ((row // 8) % 2 == lane // LANES) & (lane % HEAD < ROT) & (lane % 8 == row % 8)
    both = tn(jnp.concatenate([high, low]), goes.astype(BF16))
    still = lax.broadcasted_iota(jnp.int32, (1, LANES), 1) % HEAD >= ROT
    return both[:, :LANES] + still.astype(F32), both[:, LANES:]


def gelu_parts(hidden):
    normal = 0.5 + 0.5 * lax.erf(hidden * (0.5**0.5))
    return normal, hidden * jnp.exp(hidden * hidden * -0.5) * ((2.0 * np.pi) ** -0.5)


def by_head(rows, lane):
    return jnp.concatenate([jnp.where(lane < HEAD, rows, 0), jnp.where(lane < HEAD, 0, rows)]).astype(BF16)


def from_heads(rows, lane):
    tokens = rows.shape[0] // 2
    return jnp.where(lane < HEAD, rows[:tokens], rows[tokens:])


def near_forward_body(info, inputs, own, over, along, across, frequency, *outs):
    mix, expand, vectors, bias = outs[7:]
    shard, rank = info[0], info[1]

    @pl.when(pl.program_id(0) == 0)
    def _():
        for number in range(8):
            if number < 2:
                piece = over if number else own
            else:
                piece = (across if number % 2 else along).at[number // 2 - 1]
            block = aligned(shard ^ number, LANES)
            for part in range(3):
                mix[block, part * LANES : (part + 1) * LANES] = piece[part * LANES : (part + 1) * LANES, :]
            vectors[:, block] = piece[MIX_COLS:MIX_ROWS, :].astype(F32)
            for pair in range(4):
                start = MIX_ROWS + pair * LANES
                expand[block, pair * LANES : (pair + 1) * LANES] = piece[start : start + LANES, :]
        lane = lax.broadcasted_iota(jnp.int32, (8, LANES), 1)
        upper = jnp.bitwise_and(rank, 1) == 1
        bias[...] = jnp.zeros_like(bias)
        line = lax.broadcasted_iota(jnp.int32, (8, LANES), 0)

        def chosen_row(block, number):
            row = jnp.sum(jnp.where(line == number, block, 0.0), axis=0, keepdims=True)
            return jnp.broadcast_to(row, (8, LANES))

        for pair in range(4):
            one = chosen_row(vectors[8:16, 2 * pair * LANES : (2 * pair + 1) * LANES], 3 + rank // 2)
            two = chosen_row(vectors[8:16, (2 * pair + 1) * LANES : (2 * pair + 2) * LANES], 3 + rank // 2)
            one = jnp.where(upper, pltpu.roll(one, 64, 1), one)
            two = jnp.where(upper, two, pltpu.roll(two, 64, 1))
            joined = jnp.where(lane < 64, one, two)
            bias[0:1, pair * LANES : (pair + 1) * LANES] = joined[0:1, :]
        for part in range(3):
            place = 8 * part + rank
            held = chosen_row(vectors[8:16, aligned(place // 3, LANES)], place % 3)
            bias[1:2, part * LANES : (part + 1) * LANES] = held[0:1, :]

    forward_step(inputs, frequency, mix, expand, vectors, bias, *outs[:7])


def far_forward_body(info, inputs, mix, expand, vectors, bias, frequency, *outs):
    forward_step(inputs, frequency, mix, expand, vectors, bias, *outs)


def forward_step(
    rows, frequency, mix, expand, vectors, bias,
    normed_out, heads_out, tables_out, probs_out, context_out, act_out, slope_out,
):
    tokens = normed_out.shape[1]
    flat = (2 * tokens, normed_out.shape[2])
    rows = rows[...]
    inputs = rows[:, :tokens].reshape(flat).astype(F32)
    average = jnp.mean(inputs, axis=-1, keepdims=True)
    centred = inputs - average
    variance = jnp.mean(centred * centred, axis=-1, keepdims=True)
    normed = centred * lax.rsqrt(variance + EPSILON)
    one = (normed * vectors[0:1, :] + vectors[1:2, :]).astype(BF16)
    two = (normed * vectors[2:3, :] + vectors[3:4, :]).astype(BF16)
    normed_out[...] = normed.astype(BF16).reshape(normed_out.shape)
    mixed = nn(one, mix[...]) + bias[1:2, :MIX_COLS]

    row_index = lax.broadcasted_iota(jnp.int32, (tokens, tokens), 0)
    col_index = lax.broadcasted_iota(jnp.int32, (tokens, tokens), 1)
    lane = lax.broadcasted_iota(jnp.int32, (tokens, LANES), 1)
    for sequence in range(2):
        marks = rows[sequence, tokens : tokens + 16, :tokens].astype(F32)[0:1, :]
        across_marks = jnp.broadcast_to(marks, (tokens, tokens))
        same = across_marks == across_marks.T
        allowed = same & (col_index <= row_index)
        position = jnp.sum(jnp.where(same & (row_index < col_index), 1.0, 0.0), axis=0, keepdims=True)
        phases = jnp.broadcast_to(position, (8, tokens)) * frequency[0:8, 0:1]
        table = jnp.concatenate([jnp.cos(phases), jnp.sin(phases)], axis=0)
        tables_out[sequence] = table
        cos, sin = spread_tables(table)
        part = mixed[sequence * tokens : (sequence + 1) * tokens]
        queries = turn(part[:, :LANES], cos, sin, lane).astype(BF16)
        keys = turn(part[:, LANES : 2 * LANES], cos, sin, lane).astype(BF16)
        values = part[:, 2 * LANES :].astype(BF16)
        heads_out[sequence, :, :LANES] = queries
        heads_out[sequence, :, LANES : 2 * LANES] = keys
        heads_out[sequence, :, 2 * LANES :] = values
        scores = nt(by_head(queries * HEAD ** (-0.5), lane), keys)
        scores = jnp.where(jnp.concatenate([allowed, allowed]), scores, -1e30)
        weights = jnp.exp(scores - jnp.max(scores, axis=-1, keepdims=True))
        probs = weights * (1.0 / jnp.sum(weights, axis=-1, keepdims=True))
        probs = probs.astype(BF16)
        probs_out[sequence] = probs.reshape(2, tokens, tokens)
        context_out[sequence] = from_heads(nn(probs, values), lane).astype(BF16)

    hidden = nn(two, expand[...]) + bias[0:1, :]
    normal, slope = gelu_parts(hidden)
    act_out[...] = (hidden * normal).astype(BF16).reshape(act_out.shape)
    slope_out[...] = (normal + slope).astype(BF16).reshape(slope_out.shape)


def turn_constants():
    powers = np.power(np.float32(10000.0), -2.0 * np.arange(ROT // 2, dtype=np.float32) / np.float32(ROT))
    return np.tile(powers[:, None].astype(np.float32), (1, LANES))


def forward(info, inputs, weights, frequency, tokens, width, far=False):
    count = inputs.shape[0]
    outs = [
        ((count, tokens, width), BF16),
        ((count, tokens, MIX_COLS), BF16),
        ((count, 2 * 8, tokens), F32),
        ((count, 2, tokens, tokens), BF16),
        ((count, tokens, LANES), BF16),
        ((count, tokens, HIDDEN), BF16),
        ((count, tokens, HIDDEN), BF16),
    ]
    fixed = [((width, MIX_COLS), BF16), ((width, HIDDEN), BF16), ((SMALL, width), F32), ((8, HIDDEN), F32)]
    operands = [inputs] + list(weights) + [frequency]
    in_specs = [pairs(inputs.shape)] + [whole(operand.shape) for operand in operands[1:]]
    out_specs = [pairs(shape) for shape, _ in outs]
    if far:
        return call(far_forward_body, info, operands, in_specs, outs, out_specs, grid=(2,), micros=9)
    out_specs += [whole(shape) for shape, _ in fixed]
    return call(
        near_forward_body, info, operands, in_specs, outs + fixed, out_specs, grid=(2,), micros=9, vmem=VMEM_FIRST
    )


def pairs(shape, first=0):
    rest = (0,) * (len(shape) - 1)
    return pl.BlockSpec((2,) + shape[1:], lambda i, _: (i + first,) + rest)


def far_project_body(info, context, act, dense, own, over, along, across, out, shrink):
    @pl.when(pl.program_id(0) == 0)
    def _():
        shrink[aligned(info[0], 64), :] = own[:64, :]
        for part in range(8):
            start = FIRST_ROWS + 64 * part
            shrink[aligned(info[0] ^ 1, 64), part * LANES : (part + 1) * LANES] = over[start : start + 64, :]
        for number in range(2, 8):
            piece = across if number % 2 else along
            start = 64 * (number // 2 - 1)
            shrink[aligned(info[0] ^ number, 64), :] = piece[start : start + 64, :]

    near_project_body(info, context, act, dense, shrink, out)


def near_project_body(info, context, act, dense, shrink, out):
    rows = 2 * context.shape[1]
    total = nn(context[...].reshape(rows, LANES), dense[...]) + nn(act[...].reshape(rows, HIDDEN), shrink[...])
    out[...] = total.astype(BF16).reshape(out.shape)


def project(info, context, act, dense, shrink, far):
    tokens, width = context.shape[1], dense.shape[1]
    operands = [context, act, dense] + (list(shrink) if far else [shrink])
    in_specs = [pairs(context.shape), pairs(act.shape)]
    in_specs += [whole(operand.shape) for operand in operands[2:]]
    outs = [((4, tokens, width), BF16)] + [((HIDDEN, width), BF16)] * far
    out_specs = [pairs(outs[0][0])] + [whole((HIDDEN, width))] * far
    body = far_project_body if far else near_project_body
    return call(body, info, operands, in_specs, outs, out_specs, grid=(2,), micros=5)


def flat(ref):
    return ref[...].reshape(ref.shape[0] * ref.shape[1], ref.shape[2])


def clear(*refs):
    @pl.when(pl.program_id(0) == 0)
    def _():
        for ref in refs:
            ref[...] = jnp.zeros_like(ref)


def each_shard(info, mine, other):
    unit = mine.shape[0] // 4
    for place, z in enumerate((1, 0, 3, 2)):
        rows = pl.ds(place * unit, unit)
        yield info[0] ^ (2 * z), mine.at[rows]
        yield info[0] ^ (2 * z + 1), other.at[rows]


def last_grad_body(info, near, far, act, far_act, context, far_context, mine, other, dense_out, total, dense_total):
    step = pl.program_id(0)
    total[...] = tn(act[...], near[...]) + tn(far_act[...], far[...])
    dense_total[...] = tn(context[...], near[...]) + tn(far_context[...], far[...])
    for part in range(2):
        cols = slice(part * LANES, (part + 1) * LANES)
        for shard, out in each_shard(info, mine, other):
            out[pl.ds(pl.multiple_of(64 * (2 * step + part), 64), 64), :] = total[aligned(shard, 64), cols].astype(BF16)
        dense_out[pl.ds(pl.multiple_of(LANES * (2 * step + part), LANES), LANES), :] = dense_total[:, cols].astype(BF16)


def last_backward(info, near, far, act, context):
    operands = [array.reshape(-1, array.shape[2]) for array in (near, far) + act + context]
    near = operands[0]
    width = near.shape[1]
    outs = [((4 * HIDDEN, LANES), BF16)] * 2 + [((width, LANES), BF16)]
    columns = pl.BlockSpec((near.shape[0], 2 * LANES), lambda i, _: (0, i))
    return call(
        last_grad_body,
        info,
        operands,
        [columns, columns] + [whole(operand.shape) for operand in operands[2:]],
        outs,
        [whole(shape) for shape, _ in outs],
        grid=(width // (2 * LANES),),
        scratch=[pltpu.VMEM((HIDDEN, 2 * LANES), F32), pltpu.VMEM((LANES, 2 * LANES), F32)],
        micros=0,
    )


def as_column(row):
    size = row.shape[1]
    high = row.astype(BF16)
    middle = (row - high.astype(F32)).astype(BF16)
    low = (row - high.astype(F32) - middle.astype(F32)).astype(BF16)
    parts = jnp.concatenate([jnp.broadcast_to(part, (16, size)) for part in (high, middle, low)])
    first = lax.broadcasted_iota(jnp.int32, (48, LANES), 0) % 16 == 0
    return tn(parts, first.astype(BF16))


def mirror_body(info, mix, expand, mix_lines, expand_lines):
    mix_lines[...] = as_columns(mix[...]).astype(BF16)
    expand_lines[...] = as_columns(expand[...]).astype(BF16)


def mirror(info, mix, expand):
    outs = [(weight.shape[::-1], BF16) for weight in (mix, expand)]
    return call(
        mirror_body, info, [mix, expand], [whole(mix.shape), whole(expand.shape)], outs, [whole(shape) for shape, _ in outs]
    )


def norm_products(block, grads, normed, far_normed, column, mirrored, vectors, row, total, sums):
    count = normed.shape[0]
    products = tn(grads[:count, :], normed[...]) + tn(grads[count:, :], far_normed[...])
    lines = mirrored[:, block].astype(F32)
    shifts = column[:, 0:1]
    total[:, block] = products * vectors[row : row + 1, block] + shifts * vectors[row + 1 : row + 2, block]
    sums[0:1, block] = jnp.sum(lines * products, axis=0, keepdims=True)
    sums[1:2, block] = jnp.sum(lines * shifts, axis=0, keepdims=True)


def expand_grad_body(
    info, near, far, slope, far_slope, normed, far_normed, shrink, expand, vectors, pre_out, bias_out, sums, mine, other, held, total, column
):
    step = pl.program_id(0)
    clear(bias_out, sums)

    @pl.when(step < 4)
    def _():
        cot = jnp.where(step < 2, near[...], far[...])
        grad_act = nt(cot.reshape(cot.shape[0] * cot.shape[1], cot.shape[2]), shrink[...])
        slopes = jnp.where(step < 2, slope[...], far_slope[...]).reshape(grad_act.shape).astype(F32)
        grad_pre = (grad_act * slopes).astype(BF16)
        pre_out[...] = grad_pre.reshape(pre_out.shape)
        held[pl.ds(pl.multiple_of(step * grad_pre.shape[0], grad_pre.shape[0]), grad_pre.shape[0]), :] = grad_pre
        bias_out[...] += jnp.broadcast_to(jnp.sum(grad_pre.astype(F32), axis=0, keepdims=True), bias_out.shape)

    @pl.when(step == 3)
    def _():
        column[...] = as_column(bias_out[0:1, :])

    @pl.when(step >= 4)
    def _():
        block = aligned(step - 4, 2 * LANES)
        norm_products(block, held, normed, far_normed, column, expand, vectors, 2, total, sums)

    @pl.when(step == 7)
    def _():
        for shard, out in each_shard(info, mine, other):
            out[...] = total[:, aligned(shard, LANES)].astype(BF16)


def two_phases(pair):
    shape = pair[0].shape
    block, rest = (2,) + shape[1:], (0,) * (len(shape) - 1)
    return [
        pl.BlockSpec(block, lambda i, _: (jnp.minimum(i, 1),) + rest),
        pl.BlockSpec(block, lambda i, _: (jnp.clip(i - 2, 0, 1),) + rest),
    ]


def all_tokens(rows):
    return [pl.BlockSpec((rows, 2 * LANES), lambda i, _: (0, jnp.maximum(i - 4, 0)))] * 2


def in_first_phase(shape):
    rest = (0,) * (len(shape) - 1)
    return pl.BlockSpec((2,) + shape[1:], lambda i, _: (jnp.minimum(i, 3),) + rest)


def expand_backward(info, near, far, slope, normed, shrink, expand, vectors):
    tokens, width = near.shape[1:]
    columns = [half.reshape(-1, width) for half in normed]
    operands = [near, far, *slope, *columns, shrink, expand, vectors]
    in_specs = two_phases((near, far)) + two_phases(slope) + all_tokens(columns[0].shape[0])
    in_specs += [whole(operand.shape) for operand in operands[6:]]
    outs = [((GROUP, tokens, HIDDEN), BF16), ((8, HIDDEN), F32), ((8, width), F32)] + [((4 * HIDDEN, LANES), BF16)] * 2
    out_specs = [in_first_phase(outs[0][0])] + [whole(shape) for shape, _ in outs[1:]]
    scratch = [
        pltpu.VMEM((GROUP * tokens, HIDDEN), BF16),
        pltpu.VMEM((HIDDEN, width), F32),
        pltpu.VMEM((HIDDEN, LANES), F32),
    ]
    return call(expand_grad_body, info, operands, in_specs, outs, out_specs, grid=(8,), scratch=scratch, micros=9)


def attention_grad_body(
    info, near, far, normed, far_normed, heads, far_heads, tables, far_tables, probs, far_probs,
    dense, frequency, mix, vectors, bias_grad, feed_sums,
    mixed_out, mine, other, mixed_held, total, column, sums, piece,
):
    step = pl.program_id(0)
    rank = info[1]
    tokens = near.shape[1]
    clear(sums)

    @pl.when(step == 0)
    def _():
        sums[4:5, :] = jnp.sum(near[0].astype(F32), axis=0, keepdims=True)

    @pl.when(step < 4)
    def _():
        cot = jnp.where(step < 2, near[...], far[...])
        all_heads = jnp.where(step < 2, heads[...], far_heads[...])
        all_tables = jnp.where(step < 2, tables[...], far_tables[...])
        all_probs = jnp.where(step < 2, probs[...], far_probs[...])
        lane = lax.broadcasted_iota(jnp.int32, (tokens, LANES), 1)
        grad_context = nt(cot.reshape(2 * tokens, cot.shape[2]), dense[...]).astype(BF16)
        for sequence in range(2):
            queries = all_heads[sequence, :, :LANES]
            keys = all_heads[sequence, :, LANES : 2 * LANES]
            values = all_heads[sequence, :, 2 * LANES :]
            part = by_head(grad_context[sequence * tokens : (sequence + 1) * tokens], lane)
            low = all_probs[sequence].reshape(2 * tokens, tokens)
            exact = low.astype(F32)
            grad_probs = nt(part, values)
            grad_scores = exact * (grad_probs - jnp.sum(exact * grad_probs, axis=-1, keepdims=True))
            grad_scores = grad_scores.astype(BF16)
            grad_values = tn(low, part)
            grad_queries = from_heads(nn(grad_scores, keys), lane)
            grad_keys = tn(grad_scores, by_head(queries, lane))
            cos, sin = spread_tables(all_tables[sequence])
            joined = [
                turn(grad_queries * HEAD ** (-0.5), cos, -sin, lane),
                turn(grad_keys * HEAD ** (-0.5), cos, -sin, lane),
                grad_values,
            ]
            grad_mixed = jnp.concatenate(joined, axis=1).astype(BF16)
            mixed_out[sequence] = grad_mixed
            mixed_held[pl.ds(pl.multiple_of((2 * step + sequence) * tokens, tokens), tokens), :] = grad_mixed
            sums[5:6, :MIX_COLS] += jnp.sum(grad_mixed.astype(F32), axis=0, keepdims=True)

    @pl.when(step == 3)
    def _():
        column[...] = as_column(sums[5:6, :MIX_COLS])

    @pl.when(step >= 4)
    def _():
        block = aligned(step - 4, 2 * LANES)
        norm_products(block, mixed_held, normed, far_normed, column, mix, vectors, 0, total, sums)

    @pl.when(step == 7)
    def _():
        sums[2:4, :] = feed_sums[0:2, :]
        line = lax.broadcasted_iota(jnp.int32, (8, LANES), 1)
        for shard, out in each_shard(info, mine, other):
            block = aligned(shard, LANES)
            out[:MIX_COLS, :] = total[:, block].astype(BF16)
            piece[...] = jnp.zeros_like(piece)
            piece[0:5, :] = sums[0:5, block]
            for row in range(3):
                place = 3 * shard + row
                spread = jnp.zeros((1, LANES), F32)
                for part in range(3):
                    held = sums[5:6, part * LANES : (part + 1) * LANES]
                    spread = spread + jnp.where(place == 8 * part + rank, held, 0.0)
                piece[5 + row : 6 + row, :] = spread
            packed = bias_grad[:, aligned(shard // 2, LANES)]
            moved = jnp.where(jnp.bitwise_and(shard ^ rank, 1) == 1, pltpu.roll(packed, 64, 1), packed)
            moved = jnp.where(line // 64 == jnp.bitwise_and(rank, 1), moved, 0.0)
            for row in range(4):
                piece[8 + row : 9 + row, :] = jnp.where(rank // 2 == row, moved[0:1, :], 0.0)
            out[MIX_COLS:, :] = piece[...].astype(BF16)


def attention_backward(info, near, far, saved, fixed):
    tokens, width = near.shape[1:]
    normed, *saved = saved
    columns = [half.reshape(-1, width) for half in normed]
    operands = [near, far, *columns]
    in_specs = two_phases((near, far)) + all_tokens(columns[0].shape[0])
    for pair in saved:
        operands += pair
        in_specs += two_phases(pair)
    operands += list(fixed)
    in_specs += [whole(operand.shape) for operand in fixed]
    outs = [((GROUP, tokens, MIX_COLS), BF16)] + [((4 * MIX_ROWS, LANES), BF16)] * 2
    out_specs = [in_first_phase(outs[0][0])] + [whole(shape) for shape, _ in outs[1:]]
    scratch = [
        pltpu.VMEM((GROUP * tokens, MIX_COLS), BF16),
        pltpu.VMEM((MIX_COLS, width), F32),
        pltpu.VMEM((MIX_COLS, LANES), F32),
        pltpu.VMEM((8, width), F32),
        pltpu.VMEM((SMALL, LANES), F32),
    ]
    return call(
        attention_grad_body, info, operands, in_specs, outs, out_specs, grid=(8,), scratch=scratch, micros=6
    )


def input_grad_body(info, mixed, pre, mix, expand, vectors, out):
    total = nt(flat(mixed), mix[...]) * vectors[0:1, :] + nt(flat(pre), expand[...]) * vectors[2:3, :]
    out[...] = total.astype(BF16).reshape(out.shape)


def input_backward(info, mixed, pre, mix, expand, vectors, far):
    tokens, width = mixed.shape[1], mix.shape[0]
    operands = [mixed, pre, mix, expand, vectors]
    in_specs = [pairs(mixed.shape, 2 * far), pairs(pre.shape, 2 * far)]
    in_specs += [whole(operand.shape) for operand in operands[2:]]
    shape = (4, tokens, width)
    micros = 0 if far else 6
    return call(input_grad_body, info, operands, in_specs, [(shape, BF16)], [pairs(shape)], grid=(2,), micros=micros)[0]


def norm_body(info, block, cot, upper, upper_got, lower, lower_got, out):
    inputs = block[...].astype(F32)
    average = jnp.mean(inputs, axis=-1, keepdims=True)
    centred = inputs - average
    scale = lax.rsqrt(jnp.mean(centred * centred, axis=-1, keepdims=True) + EPSILON)
    normed = centred * scale
    pulled = jnp.concatenate(
        [upper[...] + upper_got[...].astype(F32), lower[...] + lower_got[...].astype(F32)]
    )
    pulled = pulled - jnp.mean(pulled, axis=-1, keepdims=True) - normed * jnp.mean(pulled * normed, axis=-1, keepdims=True)
    out[...] = cot[...].astype(F32) + scale * pulled


def each_rank(near, far, unit):
    for place, number in enumerate(NEAR):
        rows = pl.ds(place * unit, unit)
        yield number, near.at[rows], far.at[rows]


def last_out_body(info, near, far, own_dense, shrink_out, dense_out):
    rank = info[1]
    for number, one, two in each_rank(near, far, HIDDEN):
        for piece, held in ((one, rank ^ number), (two, rank ^ number ^ 1)):
            for part in range(8):
                rows = piece[64 * part : 64 * (part + 1), :]
                shrink_out[aligned(held, 64), part * LANES : (part + 1) * LANES] = rows.astype(F32)
    for part in range(8):
        start = 4 * HIDDEN + part * LANES
        rows = jnp.where(own_dense[0] == 1, near[start : start + LANES, :], far[start : start + LANES, :])
        dense_out[:, part * LANES : (part + 1) * LANES] = rows.astype(F32)


def expand_out_body(info, near, far, out):
    rank = info[1]
    upper = jnp.bitwise_and(rank, 1) == 1
    for number, one, two in each_rank(near, far, HIDDEN):
        place = (rank ^ number) // 2
        for shard in range(8):
            rows = slice(64 * shard, 64 * (shard + 1))
            lower_rows = jnp.where(upper, two[rows, :], one[rows, :])
            upper_rows = jnp.where(upper, one[rows, :], two[rows, :])
            joined = jnp.concatenate([lower_rows, upper_rows], axis=0)
            out[:, aligned(4 * shard + place, LANES)] = as_columns(joined)


def mix_out_body(info, near, far, out):
    rank = info[1]
    for number, one, two in each_rank(near, far, MIX_ROWS):
        for piece, place in ((one, rank ^ number), (two, rank ^ number ^ 1)):
            for part in range(3):
                out[:, aligned(8 * part + place, LANES)] = as_columns(piece[part * LANES : (part + 1) * LANES, :])


def after(value, *others):
    return jax.tree.map(lambda leaf: lax.optimization_barrier((leaf,) + others)[0], value)


def mark_body(info, out):
    out[...] = jnp.zeros_like(out) + info[0].astype(F32)


def mark(info, *others):
    return call(mark_body, after(info, *others), [], [], [((8, LANES), F32)], [whole((8, LANES))], micros=40)[0]


def gather_first(upper, lower):
    return swap(upper, x=1), swap(lower, low=1)


def gather_second(upper, lower, upper_x, lower_low):
    return swap(jnp.stack([upper, upper_x]), low=1), swap(jnp.stack([lower, lower_low]), x=1)


def gathered(upper, lower, upper_x, lower_low, upper_pair, lower_pair):
    return jnp.concatenate(
        [
            jnp.stack([upper, upper_pair[0], upper_x, upper_pair[1]]),
            jnp.stack([lower, lower_low, lower_pair[0], lower_pair[1]]),
        ],
        axis=1,
    )


def reduce_first(mine, other, unit, *late):
    got = after(swap(other, y=1), *late)
    total = mine.astype(F32) + got.astype(F32)
    return total[: 2 * unit], total[2 * unit :].astype(BF16)


def reduce_second(kept, sent, *late):
    return (kept + after(swap(sent, high=1), *late).astype(F32)).astype(BF16)


def share_first(slices, unit, *late):
    return jnp.concatenate([slices[unit:], after(swap(slices[:unit], low=1), *late)])


def share_second(pair, *late):
    return after(swap(pair, x=1), *late)


def scatter_first(near, far_got):
    cut = near.shape[1] // 2
    total = near.astype(F32) + far_got.astype(F32)
    sent_x = total[2:, :cut].astype(BF16)
    sent_low = total[1::2, cut:].astype(BF16)
    return total[:2, :cut], sent_x, total[0::2, cut:], sent_low


def scatter_second(kept_x, sent_x, kept_low, sent_low, *late):
    upper = kept_x + after(swap(sent_x, x=1), *late).astype(F32)
    lower = kept_low + after(swap(sent_low, low=1), *late).astype(F32)
    return upper[0], upper[1].astype(BF16), lower[0], lower[1].astype(BF16)


def scatter_third(upper, sent_upper, lower, sent_lower, *late):
    upper = upper + after(swap(sent_upper, low=1), *late).astype(F32)
    lower = lower + after(swap(sent_lower, x=1), *late).astype(F32)
    return jnp.concatenate([upper, lower])


def local(
    block_input,
    segments,
    cotangent,
    first_gain,
    first_shift,
    mix_weight,
    mix_bias,
    dense_weight,
    dense_bias,
    second_gain,
    second_shift,
    expand_weight,
    expand_bias,
    shrink_weight,
    shrink_bias,
):
    rep = lax.axis_index("rep")
    shard = lax.axis_index("fsdp")
    x, core, high, low, y = rep // 2, rep % 2, shard // 4, (shard // 2) % 2, shard % 2
    info = jnp.stack([shard, 4 * x + 2 * low + core]).astype(jnp.int32)
    tokens, width = block_input.shape
    rows = mix_weight.shape[0]

    own_y, own_x = y == core, x == high

    small = (first_gain, first_shift, second_gain, second_shift, dense_bias, shrink_bias, mix_bias, expand_bias)
    half = tokens // 2
    own, other, own_all = cut_slices(info, mix_weight, expand_weight, shrink_weight, dense_weight, small)
    marks = jnp.pad(segments.astype(BF16), ((0, 15), (0, width - tokens)))
    upper, lower = block_input[:half], jnp.concatenate([block_input[half:], marks])
    along = swap(other, low=1), swap(own, high=1), swap(other, high=1, low=1)
    upper_x, lower_low = gather_first(upper, lower)
    first = mark(info, own)
    upper_x, lower_low = after((upper_x, lower_low), first)
    over = swap(own_all, y=1)
    upper_pair = swap(jnp.stack([upper, upper_x]), low=1)
    lower_in = jnp.stack([lower, lower_low])
    second = mark(info, upper_x, lower_in)
    along = jnp.stack(after(along, second))
    across = swap(along, y=1)
    lower_pair = swap(after(lower_in, along), x=1)

    over = after(over, along)
    high_in, low_in, other_shrink = cut_last(info, shrink_weight, dense_weight, cotangent, over)
    high_last = swap(high_in, high=1)
    low_last = swap(low_in, low=1)
    third = mark(info, along, high_in, low_in)
    upper_pair, lower_pair, across = after((upper_pair, lower_pair, across), third)
    near = gathered(upper, lower, upper_x, lower_low, upper_pair, lower_pair)
    both_last = swap(after(other_shrink, near), high=1, low=1)
    far = swap(near, core=1)
    cot_upper = after(cotangent[:half], near)
    cot_upper_x = swap(cot_upper, x=1)
    frequency = jnp.asarray(turn_constants())
    *near_saved, mix, expand, vectors, bias = forward(info, near, (own, over, along, across), frequency, tokens, width)
    high_last, low_last, both_last, cot_upper_x, far = after((high_last, low_last, both_last, cot_upper_x, far), mix)
    last, dense = pack_last(info, high_in, low_last, high_last, both_last)
    last_across = swap(last, y=1)
    cot_pairs = gather_second(cot_upper, cotangent[half:], cot_upper_x, low_last[64:])
    far = after(far, last, cot_upper_x)
    far_saved = forward(info, far, (mix, expand, vectors, bias), frequency, tokens, width, True)
    normed, heads, tables, probs, context, act, slope = zip(near_saved, far_saved)
    mix_lines, expand_lines = mirror(info, after(mix, context[1]), expand)
    cot_near = gathered(
        cot_upper, cotangent[half:], cot_upper_x, low_last[64:], *after(cot_pairs, mix_lines)
    )
    cot_far = swap(cot_near, core=1)
    last_across = after(last_across, cot_near)
    branch_far, shrink = project(info, context[1], act[1], dense, (high_in, over, last, last_across), True)
    branch_got = swap(branch_far, core=1)
    (branch_near,) = project(info, context[0], act[0], dense, shrink, False)
    cot_far = after(cot_far, branch_near)
    last_mine, last_other, dense_grad = last_backward(info, cot_near, cot_far, act, context)
    branch_near = after(branch_near, dense_grad)
    branch_sum = (branch_near.astype(F32) + branch_got.astype(F32)).astype(BF16)
    branch_kept, branch_sent = branch_sum[:2], branch_sum[2:]
    grad_pre, bias_grad, feed_sums, expand_mine, expand_other = expand_backward(
        info, cot_near, cot_far, slope, normed, after(shrink, branch_sent), expand_lines, vectors
    )
    last_part = reduce_first(last_mine, last_other, HIDDEN, grad_pre)
    dense_got = after(swap(dense_grad, high=1), grad_pre)
    dense_grad = (dense_grad.astype(F32) + dense_got.astype(F32)).astype(BF16)
    grad_mixed, mix_mine, mix_other = attention_backward(
        info,
        cot_near,
        cot_far,
        (normed, heads, tables, probs),
        (after(dense, last_part[1], dense_grad), frequency, mix_lines, vectors, bias_grad, feed_sums),
    )
    error_far = input_backward(info, grad_mixed, grad_pre, mix, expand, vectors, True)
    error_got = swap(error_far, core=1)
    expand_part = reduce_first(expand_mine, expand_other, HIDDEN, error_far)
    last_slices = reduce_second(*last_part, error_far)
    dense_got = after(swap(dense_grad, y=1), error_far)
    dense_grad = (dense_grad.astype(F32) + dense_got.astype(F32)).astype(BF16)
    branch = branch_kept.astype(F32) + after(swap(branch_sent, x=1), error_far).astype(F32)
    branch_own, branch_last = branch[0].astype(BF16), branch[1].astype(BF16)
    error_near = input_backward(
        info,
        after(grad_mixed, error_far, branch_own, branch_last, last_slices, dense_grad, expand_part[1]),
        grad_pre,
        mix,
        expand,
        vectors,
        False,
    )
    dense_x = after(swap(dense_grad, x=1), error_near)
    dense_part = jnp.where(own_x, dense_grad, dense_x)
    mix_part = reduce_first(mix_mine, mix_other, MIX_ROWS, error_near)
    error = scatter_first(after(error_near, dense_part, mix_part[1]), error_got)
    last_pair = share_first(last_slices, HIDDEN, error[1], error[3])
    fourth = mark(info, last_pair, mix_part[1], error[1], error[3], dense_part)
    expand_slices = reduce_second(*expand_part, fourth)
    last_x = share_second(last_pair, fourth)
    last_near = jnp.concatenate([last_pair, last_x, dense_part])
    mix_slices = reduce_second(*mix_part, fourth)
    error = scatter_second(*error, fourth)
    fifth = mark(info, expand_slices, mix_slices, error[1], error[3], last_near)
    expand_pair = share_first(expand_slices, HIDDEN, fifth)
    mix_pair = share_first(mix_slices, MIX_ROWS, fifth)
    last_far = swap(after(last_near, mix_pair), core=1)

    def out(body, near, far, shapes, flag=None):
        operands = [near, far]
        in_specs = [whole(near.shape), whole(far.shape)]
        if flag is not None:
            operands.append(flag)
            in_specs.append(pl.BlockSpec(memory_space=pltpu.SMEM))
        return call(body, info, operands, in_specs, [(shape, F32) for shape in shapes], [whole(shape) for shape in shapes])

    flag = own_y.astype(jnp.int32).reshape(1)
    shapes = [shrink_weight.shape, dense_weight.shape]
    upper_got = after(swap(error[1], low=1), mix_pair, expand_pair)
    lower_got = after(swap(error[3], x=1), mix_pair, expand_pair)
    operands = [block_input, cotangent, error[0], upper_got, error[2], lower_got]
    (input_grad,) = call(
        norm_body,
        info,
        operands,
        [whole(operand.shape) for operand in operands],
        [(block_input.shape, F32)],
        [whole(block_input.shape)],
    )
    shrink_out, dense_out = out(last_out_body, last_near, after(last_far, input_grad), shapes, flag)
    expand_near = jnp.concatenate([expand_pair, share_second(expand_pair, shrink_out)])
    expand_far = swap(expand_near, core=1)
    (expand_out,) = out(expand_out_body, expand_near, expand_far, [expand_weight.shape])
    branch = branch_own.astype(F32) + after(swap(after(branch_last, mix_pair), low=1), expand_near).astype(F32)
    block_out = (block_input.astype(F32) + branch + (vectors[4] + vectors[5])).astype(BF16)
    mix_x = share_second(mix_pair, expand_near)
    mix_parts = [mix_pair[:MIX_ROWS], mix_pair[MIX_ROWS:], mix_x[:MIX_ROWS], mix_x[MIX_ROWS:]]
    mix_sums = [part[MIX_COLS:].astype(F32) for part in mix_parts]
    mix_sums = ((mix_sums[0] + mix_sums[1]) + (mix_sums[2] + mix_sums[3])).astype(BF16)
    near = jnp.concatenate(mix_parts + [mix_sums])
    far = swap(near, core=1)
    sums = mix_sums.astype(F32) + far[4 * MIX_ROWS :].astype(F32)
    (mix_out,) = out(mix_out_body, near, far, [mix_weight.shape])
    return (
        block_out,
        input_grad,
        sums[0],
        sums[1],
        mix_out,
        sums[5:8].reshape(-1),
        dense_out,
        sums[4],
        sums[2],
        sums[3],
        expand_out,
        sums[8:12].reshape(-1),
        shrink_out,
        sums[4],
    )


def solution(mesh):
    tensor_parallel = mesh.shape["rep"] == TP_REP and mesh.shape["fsdp"] == TP_FSDP
    return jax.shard_map(
        local if tensor_parallel else local_general,
        mesh=mesh,
        in_specs=(
            P(("rep", "fsdp"), None),
            P(("rep", "fsdp"), None),
            P(("rep", "fsdp"), None),
            P("fsdp"),
            P("fsdp"),
            P("fsdp", None),
            P("fsdp"),
            P("fsdp", None),
            P("fsdp"),
            P("fsdp"),
            P("fsdp"),
            P("fsdp", None),
            P("fsdp"),
            P("fsdp", None),
            P("fsdp"),
        ),
        out_specs=(
            P(("rep", "fsdp"), None),
            P(("rep", "fsdp"), None),
            P("fsdp"),
            P("fsdp"),
            P("fsdp", None),
            P("fsdp"),
            P("fsdp", None),
            P("fsdp"),
            P("fsdp"),
            P("fsdp"),
            P("fsdp", None),
            P("fsdp"),
            P("fsdp", None),
            P("fsdp"),
        ),
        check_vma=False,
    )
```

```python
import jax
import jax.numpy as jnp
import numpy as np
from jax import lax
from jax.experimental import pallas as pl
from jax.experimental.pallas import tpu as pltpu
from jax.sharding import PartitionSpec as P

HEADS = 16
HEAD = 64
ROT = 16


EPSILON = 1e-05


def layer_norm(inputs, gain_row, shift_row):
    average = jnp.mean(inputs, axis=-1, keepdims=True)
    centred = inputs - average
    variance = jnp.mean(centred * centred, axis=-1, keepdims=True)
    return centred * lax.rsqrt(variance + EPSILON) * gain_row + shift_row


def rotate(heads_in, cos_table, sin_table):
    half_rot = ROT // 2
    first_half = heads_in[..., :half_rot]
    second_half = heads_in[..., half_rot:ROT]
    return jnp.concatenate(
        [
            first_half * cos_table - second_half * sin_table,
            second_half * cos_table + first_half * sin_table,
            heads_in[..., ROT:],
        ],
        axis=-1,
    )


def rotary_tables(segment_row):
    length = segment_row.shape[0]
    same_doc = segment_row[:, None] == segment_row[None, :]
    row_index = lax.broadcasted_iota(jnp.int32, (length, length), 0)
    col_index = lax.broadcasted_iota(jnp.int32, (length, length), 1)
    earlier = jnp.where(same_doc & (col_index < row_index), 1.0, 0.0)
    position = jnp.sum(earlier, axis=-1).astype(jnp.float32)
    allowed = same_doc & (col_index <= row_index)
    frequency = jnp.power(10000.0, -2.0 * jnp.arange(ROT // 2).astype(jnp.float32) / ROT)
    phases = position[:, None] * frequency
    return (jnp.cos(phases)[:, None, :], jnp.sin(phases)[:, None, :], allowed)


def product_left(left, right):
    return lax.dot_general(
        left, right, (((0,), (0,)), ((), ())), preferred_element_type=jnp.float32
    )


def product_right(left, right):
    return lax.dot_general(
        left, right, (((1,), (1,)), ((), ())), preferred_element_type=jnp.float32
    )


def norm_backward(inputs, gain_row, shift_row, upstream):
    _, pullback = jax.vjp(layer_norm, inputs, gain_row, shift_row)
    return pullback(upstream)


def local_general(
    block_input,
    segments,
    cotangent,
    first_gain,
    first_shift,
    mix_weight,
    mix_bias,
    dense_weight,
    dense_bias,
    second_gain,
    second_shift,
    expand_weight,
    expand_bias,
    shrink_weight,
    shrink_bias,
):
    attention_parts = (
        lax.all_gather(first_gain, "fsdp", axis=0, tiled=True),
        lax.all_gather(first_shift, "fsdp", axis=0, tiled=True),
        lax.all_gather(mix_weight, "fsdp", axis=0, tiled=True),
        lax.all_gather(mix_bias, "fsdp", axis=0, tiled=True),
        lax.all_gather(dense_weight, "fsdp", axis=0, tiled=True),
        lax.all_gather(dense_bias, "fsdp", axis=0, tiled=True),
    )
    feed_parts = (
        lax.all_gather(second_gain, "fsdp", axis=0, tiled=True),
        lax.all_gather(second_shift, "fsdp", axis=0, tiled=True),
        lax.all_gather(expand_weight, "fsdp", axis=0, tiled=True),
        lax.all_gather(expand_bias, "fsdp", axis=0, tiled=True),
        lax.all_gather(shrink_weight, "fsdp", axis=0, tiled=True),
        lax.all_gather(shrink_bias, "fsdp", axis=0, tiled=True),
    )
    token_count = block_input.shape[0]
    feature_count = block_input.shape[1]
    score_scale = HEAD ** (-0.5)
    block_float = block_input.astype(jnp.float32)
    cot_float = cotangent.astype(jnp.float32)
    cos_table, sin_table, allowed = rotary_tables(segments[0])
    normed_one = layer_norm(
        block_float, attention_parts[0].astype(jnp.float32), attention_parts[1].astype(jnp.float32)
    ).astype(jnp.bfloat16)
    mixed_rows = jnp.dot(normed_one, attention_parts[2], preferred_element_type=jnp.float32)
    mixed_rows = mixed_rows + attention_parts[3].astype(jnp.float32)
    triple = mixed_rows.reshape(token_count, 3, HEADS, HEAD)
    queries = rotate(triple[:, 0], cos_table, sin_table).astype(jnp.bfloat16)
    keys_all = rotate(triple[:, 1], cos_table, sin_table).astype(jnp.bfloat16)
    values_all = triple[:, 2].astype(jnp.bfloat16)

    def masked_scores():
        raw_scores = (
            jnp.einsum("qhd,khd->hqk", queries, keys_all, preferred_element_type=jnp.float32)
            * score_scale
        )
        return jnp.where(allowed[None], raw_scores, -1e30)

    forward_scores = masked_scores()
    row_peak = jnp.max(forward_scores, axis=-1, keepdims=True)
    weights_raw = jnp.exp(forward_scores - row_peak)
    row_total = jnp.sum(weights_raw, axis=-1, keepdims=True)
    log_total = row_peak + jnp.log(row_total)
    probs_low = (weights_raw / row_total).astype(jnp.bfloat16)
    context = jnp.einsum("hqk,khd->qhd", probs_low, values_all, preferred_element_type=jnp.float32)
    context = context.reshape(token_count, feature_count).astype(jnp.bfloat16)
    attention_branch = jnp.dot(context, attention_parts[4], preferred_element_type=jnp.float32)
    attention_branch = attention_branch + attention_parts[5].astype(jnp.float32)
    normed_two = layer_norm(
        block_float, feed_parts[0].astype(jnp.float32), feed_parts[1].astype(jnp.float32)
    ).astype(jnp.bfloat16)
    hidden_pre = jnp.dot(normed_two, feed_parts[2], preferred_element_type=jnp.float32)
    hidden_pre = hidden_pre + feed_parts[3].astype(jnp.float32)
    hidden_act = jax.nn.gelu(hidden_pre, approximate=False).astype(jnp.bfloat16)
    feedforward_branch = jnp.dot(hidden_act, feed_parts[4], preferred_element_type=jnp.float32)
    feedforward_branch = feedforward_branch + feed_parts[5].astype(jnp.float32)
    block_out = (block_float + attention_branch + feedforward_branch).astype(jnp.bfloat16)
    feed_back = (
        lax.all_gather(second_gain, "fsdp", axis=0, tiled=True),
        lax.all_gather(second_shift, "fsdp", axis=0, tiled=True),
        lax.all_gather(expand_weight, "fsdp", axis=0, tiled=True),
        lax.all_gather(expand_bias, "fsdp", axis=0, tiled=True),
        lax.all_gather(shrink_weight, "fsdp", axis=0, tiled=True),
        lax.all_gather(shrink_bias, "fsdp", axis=0, tiled=True),
    )
    bias_sum = jnp.sum(cot_float, axis=0)
    shrink_grad = product_left(hidden_act, cotangent)
    grad_act = product_right(cotangent, feed_back[4])
    _, gelu_pull = jax.vjp(lambda pre_value: jax.nn.gelu(pre_value, approximate=False), hidden_pre)
    grad_pre = gelu_pull(grad_act)[0].astype(jnp.bfloat16)
    expand_grad = product_left(normed_two, grad_pre)
    expand_bias_grad = jnp.sum(grad_pre.astype(jnp.float32), axis=0)
    grad_normed_two = product_right(grad_pre, feed_back[2])
    part_two, second_gain_grad, second_shift_grad = norm_backward(
        block_float,
        feed_back[0].astype(jnp.float32),
        feed_back[1].astype(jnp.float32),
        grad_normed_two,
    )
    feed_grads = (
        lax.psum_scatter(second_gain_grad, "fsdp", scatter_dimension=0, tiled=True),
        lax.psum_scatter(second_shift_grad, "fsdp", scatter_dimension=0, tiled=True),
        lax.psum_scatter(expand_grad, "fsdp", scatter_dimension=0, tiled=True),
        lax.psum_scatter(expand_bias_grad, "fsdp", scatter_dimension=0, tiled=True),
        lax.psum_scatter(shrink_grad, "fsdp", scatter_dimension=0, tiled=True),
        lax.psum_scatter(bias_sum, "fsdp", scatter_dimension=0, tiled=True),
    )
    gain_two_sum, shift_two_sum, expand_sum, expand_bias_sum, shrink_sum, shrink_bias_sum = (
        feed_grads
    )
    attention_back = (
        lax.all_gather(first_gain, "fsdp", axis=0, tiled=True),
        lax.all_gather(first_shift, "fsdp", axis=0, tiled=True),
        lax.all_gather(mix_weight, "fsdp", axis=0, tiled=True),
        lax.all_gather(mix_bias, "fsdp", axis=0, tiled=True),
        lax.all_gather(dense_weight, "fsdp", axis=0, tiled=True),
        lax.all_gather(dense_bias, "fsdp", axis=0, tiled=True),
    )
    dense_grad = product_left(context, cotangent)
    grad_context = product_right(cotangent, attention_back[4]).astype(jnp.bfloat16)
    grad_context = grad_context.reshape(token_count, HEADS, HEAD)
    grad_values = jnp.einsum(
        "hqk,qhd->khd", probs_low, grad_context, preferred_element_type=jnp.float32
    )
    grad_probs = jnp.einsum(
        "qhd,khd->hqk", grad_context, values_all, preferred_element_type=jnp.float32
    )
    probs_exact = jnp.exp(masked_scores() - log_total)
    grad_scores = probs_exact * (
        grad_probs - jnp.sum(probs_exact * grad_probs, axis=-1, keepdims=True)
    )
    grad_scores = grad_scores.astype(jnp.bfloat16)
    grad_queries = (
        jnp.einsum("hqk,khd->qhd", grad_scores, keys_all, preferred_element_type=jnp.float32)
        * score_scale
    )
    grad_keys = (
        jnp.einsum("hqk,qhd->khd", grad_scores, queries, preferred_element_type=jnp.float32)
        * score_scale
    )
    _, rotate_pull = jax.vjp(lambda heads_in: rotate(heads_in, cos_table, sin_table), grad_queries)
    grad_mixed = jnp.stack(
        [rotate_pull(grad_queries)[0], rotate_pull(grad_keys)[0], grad_values], axis=1
    )
    grad_mixed = grad_mixed.reshape(token_count, 3 * feature_count).astype(jnp.bfloat16)
    mix_grad = product_left(normed_one, grad_mixed)
    mix_bias_grad = jnp.sum(grad_mixed.astype(jnp.float32), axis=0)
    grad_normed_one = product_right(grad_mixed, attention_back[2])
    part_one, first_gain_grad, first_shift_grad = norm_backward(
        block_float,
        attention_back[0].astype(jnp.float32),
        attention_back[1].astype(jnp.float32),
        grad_normed_one,
    )
    attention_grads = (
        lax.psum_scatter(first_gain_grad, "fsdp", scatter_dimension=0, tiled=True),
        lax.psum_scatter(first_shift_grad, "fsdp", scatter_dimension=0, tiled=True),
        lax.psum_scatter(mix_grad, "fsdp", scatter_dimension=0, tiled=True),
        lax.psum_scatter(mix_bias_grad, "fsdp", scatter_dimension=0, tiled=True),
        lax.psum_scatter(dense_grad, "fsdp", scatter_dimension=0, tiled=True),
        lax.psum_scatter(bias_sum, "fsdp", scatter_dimension=0, tiled=True),
    )
    gain_one_sum, shift_one_sum, mix_sum, mix_bias_sum, dense_sum, dense_bias_sum = attention_grads
    (
        gain_one_sum,
        shift_one_sum,
        mix_sum,
        mix_bias_sum,
        dense_sum,
        dense_bias_sum,
        gain_two_sum,
        shift_two_sum,
        expand_sum,
        expand_bias_sum,
        shrink_sum,
        shrink_bias_sum,
    ) = lax.psum(
        (
            gain_one_sum,
            shift_one_sum,
            mix_sum,
            mix_bias_sum,
            dense_sum,
            dense_bias_sum,
            gain_two_sum,
            shift_two_sum,
            expand_sum,
            expand_bias_sum,
            shrink_sum,
            shrink_bias_sum,
        ),
        "rep",
    )
    input_grad = cot_float + part_one + part_two
    return (
        block_out,
        input_grad,
        gain_one_sum,
        shift_one_sum,
        mix_sum,
        mix_bias_sum,
        dense_sum,
        dense_bias_sum,
        gain_two_sum,
        shift_two_sum,
        expand_sum,
        expand_bias_sum,
        shrink_sum,
        shrink_bias_sum,
    )


TP_REP = 4
TP_FSDP = 8
GROUP = 8
NEAR = (0, 2, 4, 6)
MIX_COLS = 384
HIDDEN = 512
SMALL = 16
LANES = 128
FIRST_ROWS = MIX_COLS + SMALL + HIDDEN
MIX_ROWS = MIX_COLS + SMALL
DENSE_START = FIRST_ROWS + HIDDEN
F32 = jnp.float32
BF16 = jnp.bfloat16
COST = 5000
VMEM_LIMIT = 18 * 1024 * 1024
VMEM_FIRST = 28 * 1024 * 1024
VMEM_WHOLE = 56 * 1024 * 1024


def permute(value, target):
    pairs = []
    for rep in range(TP_REP):
        for shard in range(TP_FSDP):
            goal = target(rep // 2, rep % 2, shard // 4, (shard // 2) % 2, shard % 2)
            if goal is not None:
                x, core, high, low, y = goal
                pairs.append((rep * TP_FSDP + shard, (2 * x + core) * TP_FSDP + 4 * high + 2 * low + y))
    return lax.ppermute(value, ("rep", "fsdp"), pairs)


def swap(value, x=0, core=0, high=0, low=0, y=0):
    return permute(value, lambda a, b, c, d, e: (a ^ x, b ^ core, c ^ high, d ^ low, e ^ y))


def nt(left, right):
    return lax.dot_general(left, right, (((1,), (1,)), ((), ())), preferred_element_type=F32)


def nn(left, right):
    return lax.dot_general(left, right, (((1,), (0,)), ((), ())), preferred_element_type=F32)


def tn(left, right):
    return lax.dot_general(left, right, (((0,), (0,)), ((), ())), preferred_element_type=F32)


def whole(shape):
    return pl.BlockSpec(shape, lambda *_: (0,) * len(shape))


def call(body, info, operands, in_specs, outs, out_specs, grid=(1,), scratch=(), micros=4, vmem=VMEM_LIMIT):
    return pl.pallas_call(
        body,
        grid_spec=pltpu.PrefetchScalarGridSpec(
            num_scalar_prefetch=1,
            grid=grid,
            in_specs=in_specs,
            out_specs=out_specs,
            scratch_shapes=list(scratch),
        ),
        out_shape=[jax.ShapeDtypeStruct(shape, dtype) for shape, dtype in outs],
        compiler_params=pltpu.CompilerParams(vmem_limit_bytes=vmem),
        cost_estimate=pl.CostEstimate(flops=micros * COST * 10**6, bytes_accessed=micros * COST * 3 * 10**3, transcendentals=0),
    )(info, *operands)


def as_columns(matrix):
    size = matrix.shape[1]
    rows = lax.broadcasted_iota(jnp.int32, (size, size), 0)
    cols = lax.broadcasted_iota(jnp.int32, (size, size), 1)
    return nt((rows == cols).astype(BF16), matrix)


def aligned(index, unit):
    return pl.ds(pl.multiple_of(index * unit, unit), unit)


def cut_body(info, mix, expand, *rest):
    vectors, (own, other), small = rest[:8], rest[8:10], rest[10]
    row = 0
    small[...] = jnp.zeros_like(small)
    for vector in vectors:
        count = vector.shape[0]
        small[row : row + count, :] = vector[...].astype(F32)
        row = row + count if row + count != 6 else 8
    lane = lax.broadcasted_iota(jnp.int32, (LANES, LANES), 1)
    for out, rank in ((own, info[1]), (other, info[1] ^ 2)):
        for part in range(3):
            out[part * LANES : (part + 1) * LANES, :] = mix[:, aligned(8 * part + rank, LANES)]
        out[MIX_COLS:MIX_ROWS, :] = small[...].astype(BF16)
        upper = jnp.bitwise_and(rank, 1) == 1
        for pair in range(4):
            first = expand[:, aligned(8 * pair + rank // 2, LANES)].astype(F32)
            second = expand[:, aligned(8 * pair + 4 + rank // 2, LANES)].astype(F32)
            first = jnp.where(upper, pltpu.roll(first, 64, 1), first)
            second = jnp.where(upper, second, pltpu.roll(second, 64, 1))
            joined = jnp.where(lane < 64, first, second).astype(BF16)
            out[MIX_ROWS + pair * LANES : MIX_ROWS + (pair + 1) * LANES, :] = joined


def cut_all_body(info, own, shrink, dense, own_all):
    own_all[:FIRST_ROWS, :] = own[...]
    rows = shrink[aligned(info[1], 64), :]
    for part in range(8):
        cols = slice(part * LANES, (part + 1) * LANES)
        own_all[FIRST_ROWS + 64 * part : FIRST_ROWS + 64 * (part + 1), :] = rows[:, cols]
        own_all[DENSE_START + LANES * part : DENSE_START + LANES * (part + 1), :] = dense[:, cols]


def cut_all(info, own, shrink, dense):
    operands = [own, shrink, dense]
    shape = (DENSE_START + shrink.shape[1], LANES)
    in_specs = [whole(operand.shape) for operand in operands]
    return call(cut_all_body, info, operands, in_specs, [(shape, BF16)], [whole(shape)], vmem=VMEM_WHOLE)[0]


def cut_slices(info, mix, expand, vectors):
    operands = [mix, expand] + [vector.reshape(-1, LANES) for vector in vectors]
    outs = [((FIRST_ROWS, LANES), BF16)] * 2
    return call(
        cut_body,
        info,
        operands,
        [whole(operand.shape) for operand in operands],
        outs,
        [whole(shape) for shape, _ in outs],
        scratch=[pltpu.VMEM((SMALL, LANES), F32)],
        vmem=VMEM_WHOLE,
    )


def cut_last_body(info, shrink, dense, cot, over, own, other, other_shrink):
    rows = cot.shape[0] // 2
    own[:64, :] = shrink[aligned(info[1], 64), :]
    mine = jnp.bitwise_and(info[0] ^ info[1], 1) == 0
    for part in range(8):
        cols = slice(part * LANES, (part + 1) * LANES)
        start = DENSE_START + part * LANES
        own[64:, cols] = jnp.where(mine, dense[:, cols], over[start : start + LANES, :])
    rest = shrink[aligned(info[1] ^ 2, 64), :]
    other_shrink[...] = rest
    other[:64, :] = rest
    other[64:, :] = cot[rows:, :]


def cut_last(info, shrink, dense, cot, over):
    operands = [shrink, dense, cot, over]
    shapes = [(64 + rows, shrink.shape[1]) for rows in (dense.shape[0], cot.shape[0] // 2, 0)]
    return call(
        cut_last_body,
        info,
        operands,
        [whole(operand.shape) for operand in operands],
        [(shape, BF16) for shape in shapes],
        [whole(shape) for shape in shapes],
        vmem=VMEM_WHOLE,
    )


def pack_body(info, own, low, high, both, out, dense):
    out[:64, :] = low[:64, :]
    out[64:128, :] = high[:64, :]
    out[128:, :] = both[...]
    same = info[1] // 4 == info[0] // 4
    dense[...] = jnp.where(same, own[64:, :], high[64:, :])


def pack_last(info, own, low, high, both):
    operands = [own, low, high, both]
    width = own.shape[1]
    shapes = [(192, width), (own.shape[0] - 64, width)]
    return call(
        pack_body,
        info,
        operands,
        [whole(operand.shape) for operand in operands],
        [(shape, BF16) for shape in shapes],
        [whole(shape) for shape in shapes],
    )


def turn(heads, cos, sin, lane):
    ahead = pltpu.roll(heads, LANES - 8, 1)
    behind = pltpu.roll(heads, 8, 1)
    return heads * cos + jnp.where(lane % HEAD < 8, -ahead, behind) * sin


def spread_tables(table):
    high = table.astype(BF16)
    low = (table - high.astype(F32)).astype(BF16)
    row = lax.broadcasted_iota(jnp.int32, (32, 2 * LANES), 0)
    lane = lax.broadcasted_iota(jnp.int32, (32, 2 * LANES), 1)
    goes = ((row // 8) % 2 == lane // LANES) & (lane % HEAD < ROT) & (lane % 8 == row % 8)
    both = tn(jnp.concatenate([high, low]), goes.astype(BF16))
    still = lax.broadcasted_iota(jnp.int32, (1, LANES), 1) % HEAD >= ROT
    return both[:, :LANES] + still.astype(F32), both[:, LANES:]


def gelu_parts(hidden):
    normal = 0.5 + 0.5 * lax.erf(hidden * (0.5**0.5))
    return normal, hidden * jnp.exp(hidden * hidden * -0.5) * ((2.0 * np.pi) ** -0.5)


def by_head(rows, lane):
    return jnp.concatenate([jnp.where(lane < HEAD, rows, 0), jnp.where(lane < HEAD, 0, rows)]).astype(BF16)


def from_heads(rows, lane):
    tokens = rows.shape[0] // 2
    return jnp.where(lane < HEAD, rows[:tokens], rows[tokens:])


def near_forward_body(info, inputs, own, over, along, across, frequency, *outs):
    mix, expand, vectors, bias = outs[7:]
    shard, rank = info[0], info[1]

    @pl.when(pl.program_id(0) == 0)
    def _():
        for number in range(8):
            if number < 2:
                piece = over if number else own
            else:
                piece = (across if number % 2 else along).at[number // 2 - 1]
            block = aligned(shard ^ number, LANES)
            for part in range(3):
                mix[block, part * LANES : (part + 1) * LANES] = piece[part * LANES : (part + 1) * LANES, :]
            vectors[:, block] = piece[MIX_COLS:MIX_ROWS, :].astype(F32)
            for pair in range(4):
                start = MIX_ROWS + pair * LANES
                expand[block, pair * LANES : (pair + 1) * LANES] = piece[start : start + LANES, :]
        lane = lax.broadcasted_iota(jnp.int32, (8, LANES), 1)
        upper = jnp.bitwise_and(rank, 1) == 1
        bias[...] = jnp.zeros_like(bias)
        line = lax.broadcasted_iota(jnp.int32, (8, LANES), 0)

        def chosen_row(block, number):
            row = jnp.sum(jnp.where(line == number, block, 0.0), axis=0, keepdims=True)
            return jnp.broadcast_to(row, (8, LANES))

        for pair in range(4):
            one = chosen_row(vectors[8:16, 2 * pair * LANES : (2 * pair + 1) * LANES], 3 + rank // 2)
            two = chosen_row(vectors[8:16, (2 * pair + 1) * LANES : (2 * pair + 2) * LANES], 3 + rank // 2)
            one = jnp.where(upper, pltpu.roll(one, 64, 1), one)
            two = jnp.where(upper, two, pltpu.roll(two, 64, 1))
            joined = jnp.where(lane < 64, one, two)
            bias[0:1, pair * LANES : (pair + 1) * LANES] = joined[0:1, :]
        for part in range(3):
            place = 8 * part + rank
            held = chosen_row(vectors[8:16, aligned(place // 3, LANES)], place % 3)
            bias[1:2, part * LANES : (part + 1) * LANES] = held[0:1, :]

    forward_step(inputs, frequency, mix, expand, vectors, bias, *outs[:7])


def far_forward_body(info, inputs, mix, expand, vectors, bias, frequency, *outs):
    forward_step(inputs, frequency, mix, expand, vectors, bias, *outs)


def forward_step(
    rows, frequency, mix, expand, vectors, bias,
    normed_out, heads_out, tables_out, probs_out, context_out, act_out, slope_out,
):
    tokens = normed_out.shape[1]
    flat = (2 * tokens, normed_out.shape[2])
    rows = rows[...]
    inputs = rows[:, :tokens].reshape(flat).astype(F32)
    average = jnp.mean(inputs, axis=-1, keepdims=True)
    centred = inputs - average
    variance = jnp.mean(centred * centred, axis=-1, keepdims=True)
    normed = centred * lax.rsqrt(variance + EPSILON)
    one = (normed * vectors[0:1, :] + vectors[1:2, :]).astype(BF16)
    two = (normed * vectors[2:3, :] + vectors[3:4, :]).astype(BF16)
    normed_out[...] = normed.astype(BF16).reshape(normed_out.shape)
    mixed = nn(one, mix[...]) + bias[1:2, :MIX_COLS]

    row_index = lax.broadcasted_iota(jnp.int32, (tokens, tokens), 0)
    col_index = lax.broadcasted_iota(jnp.int32, (tokens, tokens), 1)
    lane = lax.broadcasted_iota(jnp.int32, (tokens, LANES), 1)
    for sequence in range(2):
        marks = rows[sequence, tokens : tokens + 16, :tokens].astype(F32)[0:1, :]
        across_marks = jnp.broadcast_to(marks, (tokens, tokens))
        same = across_marks == across_marks.T
        allowed = same & (col_index <= row_index)
        position = jnp.sum(jnp.where(same & (row_index < col_index), 1.0, 0.0), axis=0, keepdims=True)
        phases = jnp.broadcast_to(position, (8, tokens)) * frequency[0:8, 0:1]
        table = jnp.concatenate([jnp.cos(phases), jnp.sin(phases)], axis=0)
        tables_out[sequence] = table
        cos, sin = spread_tables(table)
        part = mixed[sequence * tokens : (sequence + 1) * tokens]
        queries = turn(part[:, :LANES], cos, sin, lane).astype(BF16)
        keys = turn(part[:, LANES : 2 * LANES], cos, sin, lane).astype(BF16)
        values = part[:, 2 * LANES :].astype(BF16)
        heads_out[sequence, :, :LANES] = queries
        heads_out[sequence, :, LANES : 2 * LANES] = keys
        heads_out[sequence, :, 2 * LANES :] = values
        scores = nt(by_head(queries * HEAD ** (-0.5), lane), keys)
        scores = jnp.where(jnp.concatenate([allowed, allowed]), scores, -1e30)
        weights = jnp.exp(scores - jnp.max(scores, axis=-1, keepdims=True))
        probs = weights * (1.0 / jnp.sum(weights, axis=-1, keepdims=True))
        probs = probs.astype(BF16)
        probs_out[sequence] = probs.reshape(2, tokens, tokens)
        context_out[sequence] = from_heads(nn(probs, values), lane).astype(BF16)

    hidden = nn(two, expand[...]) + bias[0:1, :]
    normal, slope = gelu_parts(hidden)
    act_out[...] = (hidden * normal).astype(BF16).reshape(act_out.shape)
    slope_out[...] = (normal + slope).astype(BF16).reshape(slope_out.shape)


def turn_constants():
    powers = np.power(np.float32(10000.0), -2.0 * np.arange(ROT // 2, dtype=np.float32) / np.float32(ROT))
    return np.tile(powers[:, None].astype(np.float32), (1, LANES))


def forward(info, inputs, weights, frequency, tokens, width, far=False):
    count = inputs.shape[0]
    outs = [
        ((count, tokens, width), BF16),
        ((count, tokens, MIX_COLS), BF16),
        ((count, 2 * 8, tokens), F32),
        ((count, 2, tokens, tokens), BF16),
        ((count, tokens, LANES), BF16),
        ((count, tokens, HIDDEN), BF16),
        ((count, tokens, HIDDEN), BF16),
    ]
    fixed = [((width, MIX_COLS), BF16), ((width, HIDDEN), BF16), ((SMALL, width), F32), ((8, HIDDEN), F32)]
    operands = [inputs] + list(weights) + [frequency]
    in_specs = [pairs(inputs.shape)] + [whole(operand.shape) for operand in operands[1:]]
    out_specs = [pairs(shape) for shape, _ in outs]
    if far:
        return call(far_forward_body, info, operands, in_specs, outs, out_specs, grid=(2,), micros=9)
    out_specs += [whole(shape) for shape, _ in fixed]
    return call(
        near_forward_body, info, operands, in_specs, outs + fixed, out_specs, grid=(2,), micros=9, vmem=VMEM_FIRST
    )


def pairs(shape, first=0):
    rest = (0,) * (len(shape) - 1)
    return pl.BlockSpec((2,) + shape[1:], lambda i, _: (i + first,) + rest)


def far_project_body(info, context, act, dense, own, over, along, across, out, shrink):
    @pl.when(pl.program_id(0) == 0)
    def _():
        shrink[aligned(info[0], 64), :] = own[:64, :]
        for part in range(8):
            start = FIRST_ROWS + 64 * part
            shrink[aligned(info[0] ^ 1, 64), part * LANES : (part + 1) * LANES] = over[start : start + 64, :]
        for number in range(2, 8):
            piece = across if number % 2 else along
            start = 64 * (number // 2 - 1)
            shrink[aligned(info[0] ^ number, 64), :] = piece[start : start + 64, :]

    near_project_body(info, context, act, dense, shrink, out)


def near_project_body(info, context, act, dense, shrink, out):
    rows = 2 * context.shape[1]
    total = nn(context[...].reshape(rows, LANES), dense[...]) + nn(act[...].reshape(rows, HIDDEN), shrink[...])
    out[...] = total.astype(BF16).reshape(out.shape)


def project(info, context, act, dense, shrink, far):
    tokens, width = context.shape[1], dense.shape[1]
    operands = [context, act, dense] + (list(shrink) if far else [shrink])
    in_specs = [pairs(context.shape), pairs(act.shape)]
    in_specs += [whole(operand.shape) for operand in operands[2:]]
    outs = [((4, tokens, width), BF16)] + [((HIDDEN, width), BF16)] * far
    out_specs = [pairs(outs[0][0])] + [whole((HIDDEN, width))] * far
    body = far_project_body if far else near_project_body
    return call(body, info, operands, in_specs, outs, out_specs, grid=(2,), micros=5)


def flat(ref):
    return ref[...].reshape(ref.shape[0] * ref.shape[1], ref.shape[2])


def clear(*refs):
    @pl.when(pl.program_id(0) == 0)
    def _():
        for ref in refs:
            ref[...] = jnp.zeros_like(ref)


def each_shard(info, mine, other):
    unit = mine.shape[0] // 4
    for place, z in enumerate((1, 0, 3, 2)):
        rows = pl.ds(place * unit, unit)
        yield info[0] ^ (2 * z), mine.at[rows]
        yield info[0] ^ (2 * z + 1), other.at[rows]


def last_grad_body(info, near, far, act, far_act, context, far_context, mine, other, dense_out, total, dense_total):
    step = pl.program_id(0)
    total[...] = tn(act[...], near[...]) + tn(far_act[...], far[...])
    dense_total[...] = tn(context[...], near[...]) + tn(far_context[...], far[...])
    for part in range(2):
        cols = slice(part * LANES, (part + 1) * LANES)
        for shard, out in each_shard(info, mine, other):
            out[pl.ds(pl.multiple_of(64 * (2 * step + part), 64), 64), :] = total[aligned(shard, 64), cols].astype(BF16)
        dense_out[pl.ds(pl.multiple_of(LANES * (2 * step + part), LANES), LANES), :] = dense_total[:, cols].astype(BF16)


def last_backward(info, near, far, act, context):
    operands = [array.reshape(-1, array.shape[2]) for array in (near, far) + act + context]
    near = operands[0]
    width = near.shape[1]
    outs = [((4 * HIDDEN, LANES), BF16)] * 2 + [((width, LANES), BF16)]
    columns = pl.BlockSpec((near.shape[0], 2 * LANES), lambda i, _: (0, i))
    return call(
        last_grad_body,
        info,
        operands,
        [columns, columns] + [whole(operand.shape) for operand in operands[2:]],
        outs,
        [whole(shape) for shape, _ in outs],
        grid=(width // (2 * LANES),),
        scratch=[pltpu.VMEM((HIDDEN, 2 * LANES), F32), pltpu.VMEM((LANES, 2 * LANES), F32)],
        micros=0,
    )


def as_column(row):
    size = row.shape[1]
    high = row.astype(BF16)
    middle = (row - high.astype(F32)).astype(BF16)
    low = (row - high.astype(F32) - middle.astype(F32)).astype(BF16)
    parts = jnp.concatenate([jnp.broadcast_to(part, (16, size)) for part in (high, middle, low)])
    first = lax.broadcasted_iota(jnp.int32, (48, LANES), 0) % 16 == 0
    return tn(parts, first.astype(BF16))


def mirror_body(info, mix, expand, mix_lines, expand_lines):
    mix_lines[...] = as_columns(mix[...]).astype(BF16)
    expand_lines[...] = as_columns(expand[...]).astype(BF16)


def mirror(info, mix, expand):
    outs = [(weight.shape[::-1], BF16) for weight in (mix, expand)]
    return call(
        mirror_body, info, [mix, expand], [whole(mix.shape), whole(expand.shape)], outs, [whole(shape) for shape, _ in outs]
    )


def norm_products(block, grads, normed, far_normed, column, mirrored, vectors, row, total, sums):
    count = normed.shape[0]
    products = tn(grads[:count, :], normed[...]) + tn(grads[count:, :], far_normed[...])
    lines = mirrored[:, block].astype(F32)
    shifts = column[:, 0:1]
    total[:, block] = products * vectors[row : row + 1, block] + shifts * vectors[row + 1 : row + 2, block]
    sums[0:1, block] = jnp.sum(lines * products, axis=0, keepdims=True)
    sums[1:2, block] = jnp.sum(lines * shifts, axis=0, keepdims=True)


def expand_grad_body(
    info, near, far, slope, far_slope, normed, far_normed, shrink, expand, vectors, pre_out, bias_out, sums, mine, other, held, total, column
):
    step = pl.program_id(0)
    clear(bias_out, sums)

    @pl.when(step < 4)
    def _():
        cot = jnp.where(step < 2, near[...], far[...])
        grad_act = nt(cot.reshape(cot.shape[0] * cot.shape[1], cot.shape[2]), shrink[...])
        slopes = jnp.where(step < 2, slope[...], far_slope[...]).reshape(grad_act.shape).astype(F32)
        grad_pre = (grad_act * slopes).astype(BF16)
        pre_out[...] = grad_pre.reshape(pre_out.shape)
        held[pl.ds(pl.multiple_of(step * grad_pre.shape[0], grad_pre.shape[0]), grad_pre.shape[0]), :] = grad_pre
        bias_out[...] += jnp.broadcast_to(jnp.sum(grad_pre.astype(F32), axis=0, keepdims=True), bias_out.shape)

    @pl.when(step == 3)
    def _():
        column[...] = as_column(bias_out[0:1, :])

    @pl.when(step >= 4)
    def _():
        block = aligned(step - 4, 2 * LANES)
        norm_products(block, held, normed, far_normed, column, expand, vectors, 2, total, sums)

    @pl.when(step == 7)
    def _():
        for shard, out in each_shard(info, mine, other):
            out[...] = total[:, aligned(shard, LANES)].astype(BF16)


def two_phases(pair):
    shape = pair[0].shape
    block, rest = (2,) + shape[1:], (0,) * (len(shape) - 1)
    return [
        pl.BlockSpec(block, lambda i, _: (jnp.minimum(i, 1),) + rest),
        pl.BlockSpec(block, lambda i, _: (jnp.clip(i - 2, 0, 1),) + rest),
    ]


def all_tokens(rows):
    return [pl.BlockSpec((rows, 2 * LANES), lambda i, _: (0, jnp.maximum(i - 4, 0)))] * 2


def in_first_phase(shape):
    rest = (0,) * (len(shape) - 1)
    return pl.BlockSpec((2,) + shape[1:], lambda i, _: (jnp.minimum(i, 3),) + rest)


def expand_backward(info, near, far, slope, normed, shrink, expand, vectors):
    tokens, width = near.shape[1:]
    columns = [half.reshape(-1, width) for half in normed]
    operands = [near, far, *slope, *columns, shrink, expand, vectors]
    in_specs = two_phases((near, far)) + two_phases(slope) + all_tokens(columns[0].shape[0])
    in_specs += [whole(operand.shape) for operand in operands[6:]]
    outs = [((GROUP, tokens, HIDDEN), BF16), ((8, HIDDEN), F32), ((8, width), F32)] + [((4 * HIDDEN, LANES), BF16)] * 2
    out_specs = [in_first_phase(outs[0][0])] + [whole(shape) for shape, _ in outs[1:]]
    scratch = [
        pltpu.VMEM((GROUP * tokens, HIDDEN), BF16),
        pltpu.VMEM((HIDDEN, width), F32),
        pltpu.VMEM((HIDDEN, LANES), F32),
    ]
    return call(expand_grad_body, info, operands, in_specs, outs, out_specs, grid=(8,), scratch=scratch, micros=9)


def attention_grad_body(
    info, near, far, normed, far_normed, heads, far_heads, tables, far_tables, probs, far_probs,
    dense, frequency, mix, vectors, bias_grad, feed_sums,
    mixed_out, mine, other, mixed_held, total, column, sums, piece,
):
    step = pl.program_id(0)
    rank = info[1]
    tokens = near.shape[1]
    clear(sums)

    @pl.when(step == 0)
    def _():
        sums[4:5, :] = jnp.sum(near[0].astype(F32), axis=0, keepdims=True)

    @pl.when(step < 4)
    def _():
        cot = jnp.where(step < 2, near[...], far[...])
        all_heads = jnp.where(step < 2, heads[...], far_heads[...])
        all_tables = jnp.where(step < 2, tables[...], far_tables[...])
        all_probs = jnp.where(step < 2, probs[...], far_probs[...])
        lane = lax.broadcasted_iota(jnp.int32, (tokens, LANES), 1)
        grad_context = nt(cot.reshape(2 * tokens, cot.shape[2]), dense[...]).astype(BF16)
        for sequence in range(2):
            queries = all_heads[sequence, :, :LANES]
            keys = all_heads[sequence, :, LANES : 2 * LANES]
            values = all_heads[sequence, :, 2 * LANES :]
            part = by_head(grad_context[sequence * tokens : (sequence + 1) * tokens], lane)
            low = all_probs[sequence].reshape(2 * tokens, tokens)
            exact = low.astype(F32)
            grad_probs = nt(part, values)
            grad_scores = exact * (grad_probs - jnp.sum(exact * grad_probs, axis=-1, keepdims=True))
            grad_scores = grad_scores.astype(BF16)
            grad_values = tn(low, part)
            grad_queries = from_heads(nn(grad_scores, keys), lane)
            grad_keys = tn(grad_scores, by_head(queries, lane))
            cos, sin = spread_tables(all_tables[sequence])
            joined = [
                turn(grad_queries * HEAD ** (-0.5), cos, -sin, lane),
                turn(grad_keys * HEAD ** (-0.5), cos, -sin, lane),
                grad_values,
            ]
            grad_mixed = jnp.concatenate(joined, axis=1).astype(BF16)
            mixed_out[sequence] = grad_mixed
            mixed_held[pl.ds(pl.multiple_of((2 * step + sequence) * tokens, tokens), tokens), :] = grad_mixed
            sums[5:6, :MIX_COLS] += jnp.sum(grad_mixed.astype(F32), axis=0, keepdims=True)

    @pl.when(step == 3)
    def _():
        column[...] = as_column(sums[5:6, :MIX_COLS])

    @pl.when(step >= 4)
    def _():
        block = aligned(step - 4, 2 * LANES)
        norm_products(block, mixed_held, normed, far_normed, column, mix, vectors, 0, total, sums)

    @pl.when(step == 7)
    def _():
        sums[2:4, :] = feed_sums[0:2, :]
        line = lax.broadcasted_iota(jnp.int32, (8, LANES), 1)
        for shard, out in each_shard(info, mine, other):
            block = aligned(shard, LANES)
            out[:MIX_COLS, :] = total[:, block].astype(BF16)
            piece[...] = jnp.zeros_like(piece)
            piece[0:5, :] = sums[0:5, block]
            for row in range(3):
                place = 3 * shard + row
                spread = jnp.zeros((1, LANES), F32)
                for part in range(3):
                    held = sums[5:6, part * LANES : (part + 1) * LANES]
                    spread = spread + jnp.where(place == 8 * part + rank, held, 0.0)
                piece[5 + row : 6 + row, :] = spread
            packed = bias_grad[:, aligned(shard // 2, LANES)]
            moved = jnp.where(jnp.bitwise_and(shard ^ rank, 1) == 1, pltpu.roll(packed, 64, 1), packed)
            moved = jnp.where(line // 64 == jnp.bitwise_and(rank, 1), moved, 0.0)
            for row in range(4):
                piece[8 + row : 9 + row, :] = jnp.where(rank // 2 == row, moved[0:1, :], 0.0)
            out[MIX_COLS:, :] = piece[...].astype(BF16)


def attention_backward(info, near, far, saved, fixed):
    tokens, width = near.shape[1:]
    normed, *saved = saved
    columns = [half.reshape(-1, width) for half in normed]
    operands = [near, far, *columns]
    in_specs = two_phases((near, far)) + all_tokens(columns[0].shape[0])
    for pair in saved:
        operands += pair
        in_specs += two_phases(pair)
    operands += list(fixed)
    in_specs += [whole(operand.shape) for operand in fixed]
    outs = [((GROUP, tokens, MIX_COLS), BF16)] + [((4 * MIX_ROWS, LANES), BF16)] * 2
    out_specs = [in_first_phase(outs[0][0])] + [whole(shape) for shape, _ in outs[1:]]
    scratch = [
        pltpu.VMEM((GROUP * tokens, MIX_COLS), BF16),
        pltpu.VMEM((MIX_COLS, width), F32),
        pltpu.VMEM((MIX_COLS, LANES), F32),
        pltpu.VMEM((8, width), F32),
        pltpu.VMEM((SMALL, LANES), F32),
    ]
    return call(
        attention_grad_body, info, operands, in_specs, outs, out_specs, grid=(8,), scratch=scratch, micros=6
    )


def input_grad_body(info, mixed, pre, mix, expand, vectors, out):
    total = nt(flat(mixed), mix[...]) * vectors[0:1, :] + nt(flat(pre), expand[...]) * vectors[2:3, :]
    out[...] = total.astype(BF16).reshape(out.shape)


def input_backward(info, mixed, pre, mix, expand, vectors, far):
    tokens, width = mixed.shape[1], mix.shape[0]
    operands = [mixed, pre, mix, expand, vectors]
    in_specs = [pairs(mixed.shape, 2 * far), pairs(pre.shape, 2 * far)]
    in_specs += [whole(operand.shape) for operand in operands[2:]]
    shape = (4, tokens, width)
    micros = 0 if far else 6
    return call(input_grad_body, info, operands, in_specs, [(shape, BF16)], [pairs(shape)], grid=(2,), micros=micros)[0]


def norm_body(info, block, cot, upper, upper_got, lower, lower_got, out):
    inputs = block[...].astype(F32)
    average = jnp.mean(inputs, axis=-1, keepdims=True)
    centred = inputs - average
    scale = lax.rsqrt(jnp.mean(centred * centred, axis=-1, keepdims=True) + EPSILON)
    normed = centred * scale
    pulled = jnp.concatenate(
        [upper[...] + upper_got[...].astype(F32), lower[...] + lower_got[...].astype(F32)]
    )
    pulled = pulled - jnp.mean(pulled, axis=-1, keepdims=True) - normed * jnp.mean(pulled * normed, axis=-1, keepdims=True)
    out[...] = cot[...].astype(F32) + scale * pulled


def each_rank(near, far, unit):
    for place, number in enumerate(NEAR):
        rows = pl.ds(place * unit, unit)
        yield number, near.at[rows], far.at[rows]


def last_out_body(info, near, far, own_dense, shrink_out, dense_out):
    rank = info[1]
    for number, one, two in each_rank(near, far, HIDDEN):
        for piece, held in ((one, rank ^ number), (two, rank ^ number ^ 1)):
            for part in range(8):
                rows = piece[64 * part : 64 * (part + 1), :]
                shrink_out[aligned(held, 64), part * LANES : (part + 1) * LANES] = rows.astype(F32)
    for part in range(8):
        start = 4 * HIDDEN + part * LANES
        rows = jnp.where(own_dense[0] == 1, near[start : start + LANES, :], far[start : start + LANES, :])
        dense_out[:, part * LANES : (part + 1) * LANES] = rows.astype(F32)


def expand_out_body(info, near, far, out):
    rank = info[1]
    upper = jnp.bitwise_and(rank, 1) == 1
    for number, one, two in each_rank(near, far, HIDDEN):
        place = (rank ^ number) // 2
        for shard in range(8):
            rows = slice(64 * shard, 64 * (shard + 1))
            lower_rows = jnp.where(upper, two[rows, :], one[rows, :])
            upper_rows = jnp.where(upper, one[rows, :], two[rows, :])
            joined = jnp.concatenate([lower_rows, upper_rows], axis=0)
            out[:, aligned(4 * shard + place, LANES)] = as_columns(joined)


def mix_out_body(info, near, far, out):
    rank = info[1]
    for number, one, two in each_rank(near, far, MIX_ROWS):
        for piece, place in ((one, rank ^ number), (two, rank ^ number ^ 1)):
            for part in range(3):
                out[:, aligned(8 * part + place, LANES)] = as_columns(piece[part * LANES : (part + 1) * LANES, :])


def after(value, *others):
    return jax.tree.map(lambda leaf: lax.optimization_barrier((leaf,) + others)[0], value)


def mark_body(info, out):
    out[...] = jnp.zeros_like(out) + info[0].astype(F32)


def mark(info, *others):
    return call(mark_body, after(info, *others), [], [], [((8, LANES), F32)], [whole((8, LANES))], micros=40)[0]


def gather_first(upper, lower):
    return swap(upper, x=1), swap(lower, low=1)


def gather_second(upper, lower, upper_x, lower_low):
    return swap(jnp.stack([upper, upper_x]), low=1), swap(jnp.stack([lower, lower_low]), x=1)


def gathered(upper, lower, upper_x, lower_low, upper_pair, lower_pair):
    return jnp.concatenate(
        [
            jnp.stack([upper, upper_pair[0], upper_x, upper_pair[1]]),
            jnp.stack([lower, lower_low, lower_pair[0], lower_pair[1]]),
        ],
        axis=1,
    )


def reduce_first(mine, other, unit, *late):
    got = after(swap(other, y=1), *late)
    total = mine.astype(F32) + got.astype(F32)
    return total[: 2 * unit], total[2 * unit :].astype(BF16)


def reduce_second(kept, sent, *late):
    return (kept + after(swap(sent, high=1), *late).astype(F32)).astype(BF16)


def share_first(slices, unit, *late):
    return jnp.concatenate([slices[unit:], after(swap(slices[:unit], low=1), *late)])


def share_second(pair, *late):
    return after(swap(pair, x=1), *late)


def scatter_first(near, far_got):
    cut = near.shape[1] // 2
    total = near.astype(F32) + far_got.astype(F32)
    sent_x = total[2:, :cut].astype(BF16)
    sent_low = total[1::2, cut:].astype(BF16)
    return total[:2, :cut], sent_x, total[0::2, cut:], sent_low


def scatter_second(kept_x, sent_x, kept_low, sent_low, *late):
    upper = kept_x + after(swap(sent_x, x=1), *late).astype(F32)
    lower = kept_low + after(swap(sent_low, low=1), *late).astype(F32)
    return upper[0], upper[1].astype(BF16), lower[0], lower[1].astype(BF16)


def scatter_third(upper, sent_upper, lower, sent_lower, *late):
    upper = upper + after(swap(sent_upper, low=1), *late).astype(F32)
    lower = lower + after(swap(sent_lower, x=1), *late).astype(F32)
    return jnp.concatenate([upper, lower])


def local(
    block_input,
    segments,
    cotangent,
    first_gain,
    first_shift,
    mix_weight,
    mix_bias,
    dense_weight,
    dense_bias,
    second_gain,
    second_shift,
    expand_weight,
    expand_bias,
    shrink_weight,
    shrink_bias,
):
    rep = lax.axis_index("rep")
    shard = lax.axis_index("fsdp")
    x, core, high, low, y = rep // 2, rep % 2, shard // 4, (shard // 2) % 2, shard % 2
    info = jnp.stack([shard, 4 * x + 2 * low + core]).astype(jnp.int32)
    tokens, width = block_input.shape
    rows = mix_weight.shape[0]

    own_y, own_x = y == core, x == high

    small = (first_gain, first_shift, second_gain, second_shift, dense_bias, shrink_bias, mix_bias, expand_bias)
    half = tokens // 2
    own, other = cut_slices(info, mix_weight, expand_weight, small)
    marks = jnp.pad(segments.astype(BF16), ((0, 15), (0, width - tokens)))
    upper, lower = block_input[:half], jnp.concatenate([block_input[half:], marks])
    along = swap(other, low=1), swap(own, high=1), swap(other, high=1, low=1)
    upper_x, lower_low = gather_first(upper, lower)
    first = mark(info, own)
    upper_x, lower_low = after((upper_x, lower_low), first)
    over = swap(cut_all(info, after(own, first), shrink_weight, dense_weight), y=1)
    upper_pair = swap(jnp.stack([upper, upper_x]), low=1)
    lower_in = jnp.stack([lower, lower_low])
    second = mark(info, upper_x, lower_in)
    along = jnp.stack(after(along, second))
    across = swap(along, y=1)
    lower_pair = swap(after(lower_in, along), x=1)

    over = after(over, along)
    high_in, low_in, other_shrink = cut_last(info, shrink_weight, dense_weight, cotangent, over)
    high_last = swap(high_in, high=1)
    low_last = swap(low_in, low=1)
    third = mark(info, along, high_in, low_in)
    upper_pair, lower_pair, across = after((upper_pair, lower_pair, across), third)
    near = gathered(upper, lower, upper_x, lower_low, upper_pair, lower_pair)
    both_last = swap(after(other_shrink, near), high=1, low=1)
    far = swap(near, core=1)
    cot_upper = after(cotangent[:half], near)
    cot_upper_x = swap(cot_upper, x=1)
    frequency = jnp.asarray(turn_constants())
    *near_saved, mix, expand, vectors, bias = forward(info, near, (own, over, along, across), frequency, tokens, width)
    high_last, low_last, both_last, cot_upper_x, far = after((high_last, low_last, both_last, cot_upper_x, far), mix)
    last, dense = pack_last(info, high_in, low_last, high_last, both_last)
    last_across = swap(last, y=1)
    cot_pairs = gather_second(cot_upper, cotangent[half:], cot_upper_x, low_last[64:])
    far = after(far, last, cot_upper_x)
    far_saved = forward(info, far, (mix, expand, vectors, bias), frequency, tokens, width, True)
    normed, heads, tables, probs, context, act, slope = zip(near_saved, far_saved)
    mix_lines, expand_lines = mirror(info, after(mix, context[1]), expand)
    cot_near = gathered(
        cot_upper, cotangent[half:], cot_upper_x, low_last[64:], *after(cot_pairs, mix_lines)
    )
    cot_far = swap(cot_near, core=1)
    last_across = after(last_across, cot_near)
    branch_far, shrink = project(info, context[1], act[1], dense, (high_in, over, last, last_across), True)
    branch_got = swap(branch_far, core=1)
    (branch_near,) = project(info, context[0], act[0], dense, shrink, False)
    cot_far = after(cot_far, branch_near)
    last_mine, last_other, dense_grad = last_backward(info, cot_near, cot_far, act, context)
    branch_near = after(branch_near, dense_grad)
    branch_sum = (branch_near.astype(F32) + branch_got.astype(F32)).astype(BF16)
    branch_kept, branch_sent = branch_sum[:2], branch_sum[2:]
    dense_sent = after(dense_grad, mark(info, branch_sent))
    grad_pre, bias_grad, feed_sums, expand_mine, expand_other = expand_backward(
        info, cot_near, cot_far, slope, normed, after(shrink, branch_sent), expand_lines, vectors
    )
    last_part = reduce_first(last_mine, last_other, HIDDEN, grad_pre)
    dense_got = after(swap(dense_sent, high=1), grad_pre)
    dense_grad = (dense_grad.astype(F32) + dense_got.astype(F32)).astype(BF16)
    grad_mixed, mix_mine, mix_other = attention_backward(
        info,
        cot_near,
        cot_far,
        (normed, heads, tables, probs),
        (after(dense, last_part[1], dense_grad), frequency, mix_lines, vectors, bias_grad, feed_sums),
    )
    error_far = input_backward(info, grad_mixed, grad_pre, mix, expand, vectors, True)
    error_got = swap(error_far, core=1)
    expand_part = reduce_first(expand_mine, expand_other, HIDDEN, error_far)
    last_slices = reduce_second(*last_part, error_far)
    dense_got = after(swap(dense_grad, y=1), error_far)
    dense_grad = (dense_grad.astype(F32) + dense_got.astype(F32)).astype(BF16)
    branch = branch_kept.astype(F32) + after(swap(branch_sent, x=1), error_far).astype(F32)
    branch_own, branch_last = branch[0].astype(BF16), branch[1].astype(BF16)
    error_near = input_backward(
        info,
        after(grad_mixed, error_far, branch_own, branch_last, last_slices, dense_grad, expand_part[1]),
        grad_pre,
        mix,
        expand,
        vectors,
        False,
    )
    dense_x = after(swap(dense_grad, x=1), error_near)
    dense_part = jnp.where(own_x, dense_grad, dense_x)
    mix_part = reduce_first(mix_mine, mix_other, MIX_ROWS, error_near)
    error = scatter_first(after(error_near, dense_part, mix_part[1]), error_got)
    last_pair = share_first(last_slices, HIDDEN, error[1], error[3])
    fourth = mark(info, last_pair, mix_part[1], error[1], error[3], dense_part)
    expand_slices = reduce_second(*expand_part, fourth)
    last_x = share_second(last_pair, fourth)
    last_near = jnp.concatenate([last_pair, last_x, dense_part])
    mix_slices = reduce_second(*mix_part, fourth)
    error = scatter_second(*error, fourth)
    fifth = mark(info, expand_slices, mix_slices, error[1], error[3], last_near)
    expand_pair = share_first(expand_slices, HIDDEN, fifth)
    mix_pair = share_first(mix_slices, MIX_ROWS, fifth)
    last_far = swap(after(last_near, mix_pair), core=1)

    def out(body, near, far, shapes, flag=None):
        operands = [near, far]
        in_specs = [whole(near.shape), whole(far.shape)]
        if flag is not None:
            operands.append(flag)
            in_specs.append(pl.BlockSpec(memory_space=pltpu.SMEM))
        return call(body, info, operands, in_specs, [(shape, F32) for shape in shapes], [whole(shape) for shape in shapes])

    flag = own_y.astype(jnp.int32).reshape(1)
    shapes = [shrink_weight.shape, dense_weight.shape]
    upper_got = after(swap(error[1], low=1), mix_pair, expand_pair)
    lower_got = after(swap(error[3], x=1), mix_pair, expand_pair)
    operands = [block_input, cotangent, error[0], upper_got, error[2], lower_got]
    (input_grad,) = call(
        norm_body,
        info,
        operands,
        [whole(operand.shape) for operand in operands],
        [(block_input.shape, F32)],
        [whole(block_input.shape)],
    )
    shrink_out, dense_out = out(last_out_body, last_near, after(last_far, input_grad), shapes, flag)
    expand_near = jnp.concatenate([expand_pair, share_second(expand_pair, shrink_out)])
    expand_far = swap(expand_near, core=1)
    (expand_out,) = out(expand_out_body, expand_near, expand_far, [expand_weight.shape])
    branch = branch_own.astype(F32) + after(swap(after(branch_last, mix_pair), low=1), expand_near).astype(F32)
    block_out = (block_input.astype(F32) + branch + (vectors[4] + vectors[5])).astype(BF16)
    mix_x = share_second(mix_pair, expand_near)
    mix_parts = [mix_pair[:MIX_ROWS], mix_pair[MIX_ROWS:], mix_x[:MIX_ROWS], mix_x[MIX_ROWS:]]
    mix_sums = [part[MIX_COLS:].astype(F32) for part in mix_parts]
    mix_sums = ((mix_sums[0] + mix_sums[1]) + (mix_sums[2] + mix_sums[3])).astype(BF16)
    near = jnp.concatenate(mix_parts + [mix_sums])
    far = swap(near, core=1)
    sums = mix_sums.astype(F32) + far[4 * MIX_ROWS :].astype(F32)
    (mix_out,) = out(mix_out_body, near, far, [mix_weight.shape])
    return (
        block_out,
        input_grad,
        sums[0],
        sums[1],
        mix_out,
        sums[5:8].reshape(-1),
        dense_out,
        sums[4],
        sums[2],
        sums[3],
        expand_out,
        sums[8:12].reshape(-1),
        shrink_out,
        sums[4],
    )


def solution(mesh):
    tensor_parallel = mesh.shape["rep"] == TP_REP and mesh.shape["fsdp"] == TP_FSDP
    return jax.shard_map(
        local if tensor_parallel else local_general,
        mesh=mesh,
        in_specs=(
            P(("rep", "fsdp"), None),
            P(("rep", "fsdp"), None),
            P(("rep", "fsdp"), None),
            P("fsdp"),
            P("fsdp"),
            P("fsdp", None),
            P("fsdp"),
            P("fsdp", None),
            P("fsdp"),
            P("fsdp"),
            P("fsdp"),
            P("fsdp", None),
            P("fsdp"),
            P("fsdp", None),
            P("fsdp"),
        ),
        out_specs=(
            P(("rep", "fsdp"), None),
            P(("rep", "fsdp"), None),
            P("fsdp"),
            P("fsdp"),
            P("fsdp", None),
            P("fsdp"),
            P("fsdp", None),
            P("fsdp"),
            P("fsdp"),
            P("fsdp"),
            P("fsdp", None),
            P("fsdp"),
            P("fsdp", None),
            P("fsdp"),
        ),
        check_vma=False,
    )
```

```python
import jax
import jax.numpy as jnp
import numpy as np
from jax import lax
from jax.experimental import pallas as pl
from jax.experimental.pallas import tpu as pltpu
from jax.sharding import PartitionSpec as P

HEADS = 16
HEAD = 64
ROT = 16


EPSILON = 1e-05


def layer_norm(inputs, gain_row, shift_row):
    average = jnp.mean(inputs, axis=-1, keepdims=True)
    centred = inputs - average
    variance = jnp.mean(centred * centred, axis=-1, keepdims=True)
    return centred * lax.rsqrt(variance + EPSILON) * gain_row + shift_row


def rotate(heads_in, cos_table, sin_table):
    half_rot = ROT // 2
    first_half = heads_in[..., :half_rot]
    second_half = heads_in[..., half_rot:ROT]
    return jnp.concatenate(
        [
            first_half * cos_table - second_half * sin_table,
            second_half * cos_table + first_half * sin_table,
            heads_in[..., ROT:],
        ],
        axis=-1,
    )


def rotary_tables(segment_row):
    length = segment_row.shape[0]
    same_doc = segment_row[:, None] == segment_row[None, :]
    row_index = lax.broadcasted_iota(jnp.int32, (length, length), 0)
    col_index = lax.broadcasted_iota(jnp.int32, (length, length), 1)
    earlier = jnp.where(same_doc & (col_index < row_index), 1.0, 0.0)
    position = jnp.sum(earlier, axis=-1).astype(jnp.float32)
    allowed = same_doc & (col_index <= row_index)
    frequency = jnp.power(10000.0, -2.0 * jnp.arange(ROT // 2).astype(jnp.float32) / ROT)
    phases = position[:, None] * frequency
    return (jnp.cos(phases)[:, None, :], jnp.sin(phases)[:, None, :], allowed)


def product_left(left, right):
    return lax.dot_general(
        left, right, (((0,), (0,)), ((), ())), preferred_element_type=jnp.float32
    )


def product_right(left, right):
    return lax.dot_general(
        left, right, (((1,), (1,)), ((), ())), preferred_element_type=jnp.float32
    )


def norm_backward(inputs, gain_row, shift_row, upstream):
    _, pullback = jax.vjp(layer_norm, inputs, gain_row, shift_row)
    return pullback(upstream)


def local_general(
    block_input,
    segments,
    cotangent,
    first_gain,
    first_shift,
    mix_weight,
    mix_bias,
    dense_weight,
    dense_bias,
    second_gain,
    second_shift,
    expand_weight,
    expand_bias,
    shrink_weight,
    shrink_bias,
):
    attention_parts = (
        lax.all_gather(first_gain, "fsdp", axis=0, tiled=True),
        lax.all_gather(first_shift, "fsdp", axis=0, tiled=True),
        lax.all_gather(mix_weight, "fsdp", axis=0, tiled=True),
        lax.all_gather(mix_bias, "fsdp", axis=0, tiled=True),
        lax.all_gather(dense_weight, "fsdp", axis=0, tiled=True),
        lax.all_gather(dense_bias, "fsdp", axis=0, tiled=True),
    )
    feed_parts = (
        lax.all_gather(second_gain, "fsdp", axis=0, tiled=True),
        lax.all_gather(second_shift, "fsdp", axis=0, tiled=True),
        lax.all_gather(expand_weight, "fsdp", axis=0, tiled=True),
        lax.all_gather(expand_bias, "fsdp", axis=0, tiled=True),
        lax.all_gather(shrink_weight, "fsdp", axis=0, tiled=True),
        lax.all_gather(shrink_bias, "fsdp", axis=0, tiled=True),
    )
    token_count = block_input.shape[0]
    feature_count = block_input.shape[1]
    score_scale = HEAD ** (-0.5)
    block_float = block_input.astype(jnp.float32)
    cot_float = cotangent.astype(jnp.float32)
    cos_table, sin_table, allowed = rotary_tables(segments[0])
    normed_one = layer_norm(
        block_float, attention_parts[0].astype(jnp.float32), attention_parts[1].astype(jnp.float32)
    ).astype(jnp.bfloat16)
    mixed_rows = jnp.dot(normed_one, attention_parts[2], preferred_element_type=jnp.float32)
    mixed_rows = mixed_rows + attention_parts[3].astype(jnp.float32)
    triple = mixed_rows.reshape(token_count, 3, HEADS, HEAD)
    queries = rotate(triple[:, 0], cos_table, sin_table).astype(jnp.bfloat16)
    keys_all = rotate(triple[:, 1], cos_table, sin_table).astype(jnp.bfloat16)
    values_all = triple[:, 2].astype(jnp.bfloat16)

    def masked_scores():
        raw_scores = (
            jnp.einsum("qhd,khd->hqk", queries, keys_all, preferred_element_type=jnp.float32)
            * score_scale
        )
        return jnp.where(allowed[None], raw_scores, -1e30)

    forward_scores = masked_scores()
    row_peak = jnp.max(forward_scores, axis=-1, keepdims=True)
    weights_raw = jnp.exp(forward_scores - row_peak)
    row_total = jnp.sum(weights_raw, axis=-1, keepdims=True)
    log_total = row_peak + jnp.log(row_total)
    probs_low = (weights_raw / row_total).astype(jnp.bfloat16)
    context = jnp.einsum("hqk,khd->qhd", probs_low, values_all, preferred_element_type=jnp.float32)
    context = context.reshape(token_count, feature_count).astype(jnp.bfloat16)
    attention_branch = jnp.dot(context, attention_parts[4], preferred_element_type=jnp.float32)
    attention_branch = attention_branch + attention_parts[5].astype(jnp.float32)
    normed_two = layer_norm(
        block_float, feed_parts[0].astype(jnp.float32), feed_parts[1].astype(jnp.float32)
    ).astype(jnp.bfloat16)
    hidden_pre = jnp.dot(normed_two, feed_parts[2], preferred_element_type=jnp.float32)
    hidden_pre = hidden_pre + feed_parts[3].astype(jnp.float32)
    hidden_act = jax.nn.gelu(hidden_pre, approximate=False).astype(jnp.bfloat16)
    feedforward_branch = jnp.dot(hidden_act, feed_parts[4], preferred_element_type=jnp.float32)
    feedforward_branch = feedforward_branch + feed_parts[5].astype(jnp.float32)
    block_out = (block_float + attention_branch + feedforward_branch).astype(jnp.bfloat16)
    feed_back = (
        lax.all_gather(second_gain, "fsdp", axis=0, tiled=True),
        lax.all_gather(second_shift, "fsdp", axis=0, tiled=True),
        lax.all_gather(expand_weight, "fsdp", axis=0, tiled=True),
        lax.all_gather(expand_bias, "fsdp", axis=0, tiled=True),
        lax.all_gather(shrink_weight, "fsdp", axis=0, tiled=True),
        lax.all_gather(shrink_bias, "fsdp", axis=0, tiled=True),
    )
    bias_sum = jnp.sum(cot_float, axis=0)
    shrink_grad = product_left(hidden_act, cotangent)
    grad_act = product_right(cotangent, feed_back[4])
    _, gelu_pull = jax.vjp(lambda pre_value: jax.nn.gelu(pre_value, approximate=False), hidden_pre)
    grad_pre = gelu_pull(grad_act)[0].astype(jnp.bfloat16)
    expand_grad = product_left(normed_two, grad_pre)
    expand_bias_grad = jnp.sum(grad_pre.astype(jnp.float32), axis=0)
    grad_normed_two = product_right(grad_pre, feed_back[2])
    part_two, second_gain_grad, second_shift_grad = norm_backward(
        block_float,
        feed_back[0].astype(jnp.float32),
        feed_back[1].astype(jnp.float32),
        grad_normed_two,
    )
    feed_grads = (
        lax.psum_scatter(second_gain_grad, "fsdp", scatter_dimension=0, tiled=True),
        lax.psum_scatter(second_shift_grad, "fsdp", scatter_dimension=0, tiled=True),
        lax.psum_scatter(expand_grad, "fsdp", scatter_dimension=0, tiled=True),
        lax.psum_scatter(expand_bias_grad, "fsdp", scatter_dimension=0, tiled=True),
        lax.psum_scatter(shrink_grad, "fsdp", scatter_dimension=0, tiled=True),
        lax.psum_scatter(bias_sum, "fsdp", scatter_dimension=0, tiled=True),
    )
    gain_two_sum, shift_two_sum, expand_sum, expand_bias_sum, shrink_sum, shrink_bias_sum = (
        feed_grads
    )
    attention_back = (
        lax.all_gather(first_gain, "fsdp", axis=0, tiled=True),
        lax.all_gather(first_shift, "fsdp", axis=0, tiled=True),
        lax.all_gather(mix_weight, "fsdp", axis=0, tiled=True),
        lax.all_gather(mix_bias, "fsdp", axis=0, tiled=True),
        lax.all_gather(dense_weight, "fsdp", axis=0, tiled=True),
        lax.all_gather(dense_bias, "fsdp", axis=0, tiled=True),
    )
    dense_grad = product_left(context, cotangent)
    grad_context = product_right(cotangent, attention_back[4]).astype(jnp.bfloat16)
    grad_context = grad_context.reshape(token_count, HEADS, HEAD)
    grad_values = jnp.einsum(
        "hqk,qhd->khd", probs_low, grad_context, preferred_element_type=jnp.float32
    )
    grad_probs = jnp.einsum(
        "qhd,khd->hqk", grad_context, values_all, preferred_element_type=jnp.float32
    )
    probs_exact = jnp.exp(masked_scores() - log_total)
    grad_scores = probs_exact * (
        grad_probs - jnp.sum(probs_exact * grad_probs, axis=-1, keepdims=True)
    )
    grad_scores = grad_scores.astype(jnp.bfloat16)
    grad_queries = (
        jnp.einsum("hqk,khd->qhd", grad_scores, keys_all, preferred_element_type=jnp.float32)
        * score_scale
    )
    grad_keys = (
        jnp.einsum("hqk,qhd->khd", grad_scores, queries, preferred_element_type=jnp.float32)
        * score_scale
    )
    _, rotate_pull = jax.vjp(lambda heads_in: rotate(heads_in, cos_table, sin_table), grad_queries)
    grad_mixed = jnp.stack(
        [rotate_pull(grad_queries)[0], rotate_pull(grad_keys)[0], grad_values], axis=1
    )
    grad_mixed = grad_mixed.reshape(token_count, 3 * feature_count).astype(jnp.bfloat16)
    mix_grad = product_left(normed_one, grad_mixed)
    mix_bias_grad = jnp.sum(grad_mixed.astype(jnp.float32), axis=0)
    grad_normed_one = product_right(grad_mixed, attention_back[2])
    part_one, first_gain_grad, first_shift_grad = norm_backward(
        block_float,
        attention_back[0].astype(jnp.float32),
        attention_back[1].astype(jnp.float32),
        grad_normed_one,
    )
    attention_grads = (
        lax.psum_scatter(first_gain_grad, "fsdp", scatter_dimension=0, tiled=True),
        lax.psum_scatter(first_shift_grad, "fsdp", scatter_dimension=0, tiled=True),
        lax.psum_scatter(mix_grad, "fsdp", scatter_dimension=0, tiled=True),
        lax.psum_scatter(mix_bias_grad, "fsdp", scatter_dimension=0, tiled=True),
        lax.psum_scatter(dense_grad, "fsdp", scatter_dimension=0, tiled=True),
        lax.psum_scatter(bias_sum, "fsdp", scatter_dimension=0, tiled=True),
    )
    gain_one_sum, shift_one_sum, mix_sum, mix_bias_sum, dense_sum, dense_bias_sum = attention_grads
    (
        gain_one_sum,
        shift_one_sum,
        mix_sum,
        mix_bias_sum,
        dense_sum,
        dense_bias_sum,
        gain_two_sum,
        shift_two_sum,
        expand_sum,
        expand_bias_sum,
        shrink_sum,
        shrink_bias_sum,
    ) = lax.psum(
        (
            gain_one_sum,
            shift_one_sum,
            mix_sum,
            mix_bias_sum,
            dense_sum,
            dense_bias_sum,
            gain_two_sum,
            shift_two_sum,
            expand_sum,
            expand_bias_sum,
            shrink_sum,
            shrink_bias_sum,
        ),
        "rep",
    )
    input_grad = cot_float + part_one + part_two
    return (
        block_out,
        input_grad,
        gain_one_sum,
        shift_one_sum,
        mix_sum,
        mix_bias_sum,
        dense_sum,
        dense_bias_sum,
        gain_two_sum,
        shift_two_sum,
        expand_sum,
        expand_bias_sum,
        shrink_sum,
        shrink_bias_sum,
    )


TP_REP = 4
TP_FSDP = 8
GROUP = 8
NEAR = (0, 2, 4, 6)
MIX_COLS = 384
HIDDEN = 512
SMALL = 16
LANES = 128
FIRST_ROWS = MIX_COLS + SMALL + HIDDEN
MIX_ROWS = MIX_COLS + SMALL
DENSE_START = FIRST_ROWS + HIDDEN
F32 = jnp.float32
BF16 = jnp.bfloat16
COST = 5000
VMEM_LIMIT = 16 * 1024 * 1024
VMEM_FIRST = 28 * 1024 * 1024
VMEM_WHOLE = 56 * 1024 * 1024


def permute(value, target):
    pairs = []
    for rep in range(TP_REP):
        for shard in range(TP_FSDP):
            goal = target(rep // 2, rep % 2, shard // 4, (shard // 2) % 2, shard % 2)
            if goal is not None:
                x, core, high, low, y = goal
                pairs.append((rep * TP_FSDP + shard, (2 * x + core) * TP_FSDP + 4 * high + 2 * low + y))
    return lax.ppermute(value, ("rep", "fsdp"), pairs)


def swap(value, x=0, core=0, high=0, low=0, y=0):
    return permute(value, lambda a, b, c, d, e: (a ^ x, b ^ core, c ^ high, d ^ low, e ^ y))


def nt(left, right):
    return lax.dot_general(left, right, (((1,), (1,)), ((), ())), preferred_element_type=F32)


def nn(left, right):
    return lax.dot_general(left, right, (((1,), (0,)), ((), ())), preferred_element_type=F32)


def tn(left, right):
    return lax.dot_general(left, right, (((0,), (0,)), ((), ())), preferred_element_type=F32)


def whole(shape):
    return pl.BlockSpec(shape, lambda *_: (0,) * len(shape))


def call(body, info, operands, in_specs, outs, out_specs, grid=(1,), scratch=(), micros=4, vmem=VMEM_LIMIT):
    return pl.pallas_call(
        body,
        grid_spec=pltpu.PrefetchScalarGridSpec(
            num_scalar_prefetch=1,
            grid=grid,
            in_specs=in_specs,
            out_specs=out_specs,
            scratch_shapes=list(scratch),
        ),
        out_shape=[jax.ShapeDtypeStruct(shape, dtype) for shape, dtype in outs],
        compiler_params=pltpu.CompilerParams(vmem_limit_bytes=vmem),
        cost_estimate=pl.CostEstimate(flops=micros * COST * 10**6, bytes_accessed=micros * COST * 3 * 10**3, transcendentals=0),
    )(info, *operands)


def as_columns(matrix):
    size = matrix.shape[1]
    rows = lax.broadcasted_iota(jnp.int32, (size, size), 0)
    cols = lax.broadcasted_iota(jnp.int32, (size, size), 1)
    return nt((rows == cols).astype(BF16), matrix)


def aligned(index, unit):
    return pl.ds(pl.multiple_of(index * unit, unit), unit)


def cut_body(info, mix, expand, *rest):
    vectors, (own, other), small = rest[:8], rest[8:10], rest[10]
    row = 0
    small[...] = jnp.zeros_like(small)
    for vector in vectors:
        count = vector.shape[0]
        small[row : row + count, :] = vector[...].astype(F32)
        row = row + count if row + count != 6 else 8
    lane = lax.broadcasted_iota(jnp.int32, (LANES, LANES), 1)
    for out, rank in ((own, info[1]), (other, info[1] ^ 2)):
        for part in range(3):
            out[part * LANES : (part + 1) * LANES, :] = mix[:, aligned(8 * part + rank, LANES)]
        out[MIX_COLS:MIX_ROWS, :] = small[...].astype(BF16)
        upper = jnp.bitwise_and(rank, 1) == 1
        for pair in range(4):
            first = expand[:, aligned(8 * pair + rank // 2, LANES)].astype(F32)
            second = expand[:, aligned(8 * pair + 4 + rank // 2, LANES)].astype(F32)
            first = jnp.where(upper, pltpu.roll(first, 64, 1), first)
            second = jnp.where(upper, second, pltpu.roll(second, 64, 1))
            joined = jnp.where(lane < 64, first, second).astype(BF16)
            out[MIX_ROWS + pair * LANES : MIX_ROWS + (pair + 1) * LANES, :] = joined


def cut_all_body(info, own, shrink, dense, own_all):
    own_all[:FIRST_ROWS, :] = own[...]
    rows = shrink[aligned(info[1], 64), :]
    for part in range(8):
        cols = slice(part * LANES, (part + 1) * LANES)
        own_all[FIRST_ROWS + 64 * part : FIRST_ROWS + 64 * (part + 1), :] = rows[:, cols]
        own_all[DENSE_START + LANES * part : DENSE_START + LANES * (part + 1), :] = dense[:, cols]


def cut_all(info, own, shrink, dense):
    operands = [own, shrink, dense]
    shape = (DENSE_START + shrink.shape[1], LANES)
    in_specs = [whole(operand.shape) for operand in operands]
    return call(cut_all_body, info, operands, in_specs, [(shape, BF16)], [whole(shape)], vmem=VMEM_WHOLE)[0]


def cut_slices(info, mix, expand, vectors):
    operands = [mix, expand] + [vector.reshape(-1, LANES) for vector in vectors]
    outs = [((FIRST_ROWS, LANES), BF16)] * 2
    return call(
        cut_body,
        info,
        operands,
        [whole(operand.shape) for operand in operands],
        outs,
        [whole(shape) for shape, _ in outs],
        scratch=[pltpu.VMEM((SMALL, LANES), F32)],
        vmem=VMEM_WHOLE,
    )


def cut_last_body(info, shrink, dense, cot, over, own, other, other_shrink):
    rows = cot.shape[0] // 2
    own[:64, :] = shrink[aligned(info[1], 64), :]
    mine = jnp.bitwise_and(info[0] ^ info[1], 1) == 0
    for part in range(8):
        cols = slice(part * LANES, (part + 1) * LANES)
        start = DENSE_START + part * LANES
        own[64:, cols] = jnp.where(mine, dense[:, cols], over[start : start + LANES, :])
    rest = shrink[aligned(info[1] ^ 2, 64), :]
    other_shrink[...] = rest
    other[:64, :] = rest
    other[64:, :] = cot[rows:, :]


def cut_last(info, shrink, dense, cot, over):
    operands = [shrink, dense, cot, over]
    shapes = [(64 + rows, shrink.shape[1]) for rows in (dense.shape[0], cot.shape[0] // 2, 0)]
    return call(
        cut_last_body,
        info,
        operands,
        [whole(operand.shape) for operand in operands],
        [(shape, BF16) for shape in shapes],
        [whole(shape) for shape in shapes],
        vmem=VMEM_WHOLE,
    )


def pack_body(info, own, low, high, both, out, dense):
    out[:64, :] = low[:64, :]
    out[64:128, :] = high[:64, :]
    out[128:, :] = both[...]
    same = info[1] // 4 == info[0] // 4
    dense[...] = jnp.where(same, own[64:, :], high[64:, :])


def pack_last(info, own, low, high, both):
    operands = [own, low, high, both]
    width = own.shape[1]
    shapes = [(192, width), (own.shape[0] - 64, width)]
    return call(
        pack_body,
        info,
        operands,
        [whole(operand.shape) for operand in operands],
        [(shape, BF16) for shape in shapes],
        [whole(shape) for shape in shapes],
    )


def turn(heads, cos, sin, lane):
    ahead = pltpu.roll(heads, LANES - 8, 1)
    behind = pltpu.roll(heads, 8, 1)
    return heads * cos + jnp.where(lane % HEAD < 8, -ahead, behind) * sin


def spread_tables(table):
    high = table.astype(BF16)
    low = (table - high.astype(F32)).astype(BF16)
    row = lax.broadcasted_iota(jnp.int32, (32, 2 * LANES), 0)
    lane = lax.broadcasted_iota(jnp.int32, (32, 2 * LANES), 1)
    goes = ((row // 8) % 2 == lane // LANES) & (lane % HEAD < ROT) & (lane % 8 == row % 8)
    both = tn(jnp.concatenate([high, low]), goes.astype(BF16))
    still = lax.broadcasted_iota(jnp.int32, (1, LANES), 1) % HEAD >= ROT
    return both[:, :LANES] + still.astype(F32), both[:, LANES:]


def gelu_parts(hidden):
    normal = 0.5 + 0.5 * lax.erf(hidden * (0.5**0.5))
    return normal, hidden * jnp.exp(hidden * hidden * -0.5) * ((2.0 * np.pi) ** -0.5)


def by_head(rows, lane):
    return jnp.concatenate([jnp.where(lane < HEAD, rows, 0), jnp.where(lane < HEAD, 0, rows)]).astype(BF16)


def from_heads(rows, lane):
    tokens = rows.shape[0] // 2
    return jnp.where(lane < HEAD, rows[:tokens], rows[tokens:])


def near_forward_body(info, inputs, own, over, along, across, frequency, *outs):
    mix, expand, vectors, bias = outs[7:]
    shard, rank = info[0], info[1]

    @pl.when(pl.program_id(0) == 0)
    def _():
        for number in range(8):
            if number < 2:
                piece = over if number else own
            else:
                piece = (across if number % 2 else along).at[number // 2 - 1]
            block = aligned(shard ^ number, LANES)
            for part in range(3):
                mix[block, part * LANES : (part + 1) * LANES] = piece[part * LANES : (part + 1) * LANES, :]
            vectors[:, block] = piece[MIX_COLS:MIX_ROWS, :].astype(F32)
            for pair in range(4):
                start = MIX_ROWS + pair * LANES
                expand[block, pair * LANES : (pair + 1) * LANES] = piece[start : start + LANES, :]
        lane = lax.broadcasted_iota(jnp.int32, (8, LANES), 1)
        upper = jnp.bitwise_and(rank, 1) == 1
        bias[...] = jnp.zeros_like(bias)
        line = lax.broadcasted_iota(jnp.int32, (8, LANES), 0)

        def chosen_row(block, number):
            row = jnp.sum(jnp.where(line == number, block, 0.0), axis=0, keepdims=True)
            return jnp.broadcast_to(row, (8, LANES))

        for pair in range(4):
            one = chosen_row(vectors[8:16, 2 * pair * LANES : (2 * pair + 1) * LANES], 3 + rank // 2)
            two = chosen_row(vectors[8:16, (2 * pair + 1) * LANES : (2 * pair + 2) * LANES], 3 + rank // 2)
            one = jnp.where(upper, pltpu.roll(one, 64, 1), one)
            two = jnp.where(upper, two, pltpu.roll(two, 64, 1))
            joined = jnp.where(lane < 64, one, two)
            bias[0:1, pair * LANES : (pair + 1) * LANES] = joined[0:1, :]
        for part in range(3):
            place = 8 * part + rank
            held = chosen_row(vectors[8:16, aligned(place // 3, LANES)], place % 3)
            bias[1:2, part * LANES : (part + 1) * LANES] = held[0:1, :]

    forward_step(inputs, frequency, mix, expand, vectors, bias, *outs[:7])


def far_forward_body(info, inputs, mix, expand, vectors, bias, frequency, *outs):
    forward_step(inputs, frequency, mix, expand, vectors, bias, *outs)


def forward_step(
    rows, frequency, mix, expand, vectors, bias,
    normed_out, heads_out, tables_out, probs_out, context_out, act_out, slope_out,
):
    tokens = normed_out.shape[1]
    flat = (2 * tokens, normed_out.shape[2])
    rows = rows[...]
    inputs = rows[:, :tokens].reshape(flat).astype(F32)
    average = jnp.mean(inputs, axis=-1, keepdims=True)
    centred = inputs - average
    variance = jnp.mean(centred * centred, axis=-1, keepdims=True)
    normed = centred * lax.rsqrt(variance + EPSILON)
    one = (normed * vectors[0:1, :] + vectors[1:2, :]).astype(BF16)
    two = (normed * vectors[2:3, :] + vectors[3:4, :]).astype(BF16)
    normed_out[...] = normed.astype(BF16).reshape(normed_out.shape)
    mixed = nn(one, mix[...]) + bias[1:2, :MIX_COLS]

    row_index = lax.broadcasted_iota(jnp.int32, (tokens, tokens), 0)
    col_index = lax.broadcasted_iota(jnp.int32, (tokens, tokens), 1)
    lane = lax.broadcasted_iota(jnp.int32, (tokens, LANES), 1)
    for sequence in range(2):
        marks = rows[sequence, tokens : tokens + 16, :tokens].astype(F32)[0:1, :]
        across_marks = jnp.broadcast_to(marks, (tokens, tokens))
        same = across_marks == across_marks.T
        allowed = same & (col_index <= row_index)
        position = jnp.sum(jnp.where(same & (row_index < col_index), 1.0, 0.0), axis=0, keepdims=True)
        phases = jnp.broadcast_to(position, (8, tokens)) * frequency[0:8, 0:1]
        table = jnp.concatenate([jnp.cos(phases), jnp.sin(phases)], axis=0)
        tables_out[sequence] = table
        cos, sin = spread_tables(table)
        part = mixed[sequence * tokens : (sequence + 1) * tokens]
        queries = turn(part[:, :LANES], cos, sin, lane).astype(BF16)
        keys = turn(part[:, LANES : 2 * LANES], cos, sin, lane).astype(BF16)
        values = part[:, 2 * LANES :].astype(BF16)
        heads_out[sequence, :, :LANES] = queries
        heads_out[sequence, :, LANES : 2 * LANES] = keys
        heads_out[sequence, :, 2 * LANES :] = values
        scores = nt(by_head(queries * HEAD ** (-0.5), lane), keys)
        scores = jnp.where(jnp.concatenate([allowed, allowed]), scores, -1e30)
        weights = jnp.exp(scores - jnp.max(scores, axis=-1, keepdims=True))
        probs = weights * (1.0 / jnp.sum(weights, axis=-1, keepdims=True))
        probs = probs.astype(BF16)
        probs_out[sequence] = probs.reshape(2, tokens, tokens)
        context_out[sequence] = from_heads(nn(probs, values), lane).astype(BF16)

    hidden = nn(two, expand[...]) + bias[0:1, :]
    normal, slope = gelu_parts(hidden)
    act_out[...] = (hidden * normal).astype(BF16).reshape(act_out.shape)
    slope_out[...] = (normal + slope).astype(BF16).reshape(slope_out.shape)


def turn_constants():
    powers = np.power(np.float32(10000.0), -2.0 * np.arange(ROT // 2, dtype=np.float32) / np.float32(ROT))
    return np.tile(powers[:, None].astype(np.float32), (1, LANES))


def forward(info, inputs, weights, frequency, tokens, width, far=False):
    count = inputs.shape[0]
    outs = [
        ((count, tokens, width), BF16),
        ((count, tokens, MIX_COLS), BF16),
        ((count, 2 * 8, tokens), F32),
        ((count, 2, tokens, tokens), BF16),
        ((count, tokens, LANES), BF16),
        ((count, tokens, HIDDEN), BF16),
        ((count, tokens, HIDDEN), BF16),
    ]
    fixed = [((width, MIX_COLS), BF16), ((width, HIDDEN), BF16), ((SMALL, width), F32), ((8, HIDDEN), F32)]
    operands = [inputs] + list(weights) + [frequency]
    in_specs = [pairs(inputs.shape)] + [whole(operand.shape) for operand in operands[1:]]
    out_specs = [pairs(shape) for shape, _ in outs]
    if far:
        return call(far_forward_body, info, operands, in_specs, outs, out_specs, grid=(2,), micros=9)
    out_specs += [whole(shape) for shape, _ in fixed]
    return call(
        near_forward_body, info, operands, in_specs, outs + fixed, out_specs, grid=(2,), micros=9, vmem=VMEM_FIRST
    )


def pairs(shape, first=0):
    rest = (0,) * (len(shape) - 1)
    return pl.BlockSpec((2,) + shape[1:], lambda i, _: (i + first,) + rest)


def far_project_body(info, context, act, dense, own, over, along, across, out, shrink):
    @pl.when(pl.program_id(0) == 0)
    def _():
        shrink[aligned(info[0], 64), :] = own[:64, :]
        for part in range(8):
            start = FIRST_ROWS + 64 * part
            shrink[aligned(info[0] ^ 1, 64), part * LANES : (part + 1) * LANES] = over[start : start + 64, :]
        for number in range(2, 8):
            piece = across if number % 2 else along
            start = 64 * (number // 2 - 1)
            shrink[aligned(info[0] ^ number, 64), :] = piece[start : start + 64, :]

    near_project_body(info, context, act, dense, shrink, out)


def near_project_body(info, context, act, dense, shrink, out):
    rows = 2 * context.shape[1]
    total = nn(context[...].reshape(rows, LANES), dense[...]) + nn(act[...].reshape(rows, HIDDEN), shrink[...])
    out[...] = total.astype(BF16).reshape(out.shape)


def project(info, context, act, dense, shrink, far):
    tokens, width = context.shape[1], dense.shape[1]
    operands = [context, act, dense] + (list(shrink) if far else [shrink])
    in_specs = [pairs(context.shape), pairs(act.shape)]
    in_specs += [whole(operand.shape) for operand in operands[2:]]
    outs = [((4, tokens, width), BF16)] + [((HIDDEN, width), BF16)] * far
    out_specs = [pairs(outs[0][0])] + [whole((HIDDEN, width))] * far
    body = far_project_body if far else near_project_body
    return call(body, info, operands, in_specs, outs, out_specs, grid=(2,), micros=5)


def flat(ref):
    return ref[...].reshape(ref.shape[0] * ref.shape[1], ref.shape[2])


def clear(*refs):
    @pl.when(pl.program_id(0) == 0)
    def _():
        for ref in refs:
            ref[...] = jnp.zeros_like(ref)


def each_shard(info, mine, other):
    unit = mine.shape[0] // 4
    for place, z in enumerate((1, 0, 3, 2)):
        rows = pl.ds(place * unit, unit)
        yield info[0] ^ (2 * z), mine.at[rows]
        yield info[0] ^ (2 * z + 1), other.at[rows]


def last_grad_body(info, near, far, act, far_act, context, far_context, mine, other, dense_out, total, dense_total):
    step = pl.program_id(0)
    total[...] = tn(act[...], near[...]) + tn(far_act[...], far[...])
    dense_total[...] = tn(context[...], near[...]) + tn(far_context[...], far[...])
    for part in range(2):
        cols = slice(part * LANES, (part + 1) * LANES)
        for shard, out in each_shard(info, mine, other):
            out[pl.ds(pl.multiple_of(64 * (2 * step + part), 64), 64), :] = total[aligned(shard, 64), cols].astype(BF16)
        dense_out[pl.ds(pl.multiple_of(LANES * (2 * step + part), LANES), LANES), :] = dense_total[:, cols].astype(BF16)


def last_backward(info, near, far, act, context):
    operands = [array.reshape(-1, array.shape[2]) for array in (near, far) + act + context]
    near = operands[0]
    width = near.shape[1]
    outs = [((4 * HIDDEN, LANES), BF16)] * 2 + [((width, LANES), BF16)]
    columns = pl.BlockSpec((near.shape[0], 2 * LANES), lambda i, _: (0, i))
    return call(
        last_grad_body,
        info,
        operands,
        [columns, columns] + [whole(operand.shape) for operand in operands[2:]],
        outs,
        [whole(shape) for shape, _ in outs],
        grid=(width // (2 * LANES),),
        scratch=[pltpu.VMEM((HIDDEN, 2 * LANES), F32), pltpu.VMEM((LANES, 2 * LANES), F32)],
        micros=0,
    )


def as_column(row):
    size = row.shape[1]
    high = row.astype(BF16)
    middle = (row - high.astype(F32)).astype(BF16)
    low = (row - high.astype(F32) - middle.astype(F32)).astype(BF16)
    parts = jnp.concatenate([jnp.broadcast_to(part, (16, size)) for part in (high, middle, low)])
    first = lax.broadcasted_iota(jnp.int32, (48, LANES), 0) % 16 == 0
    return tn(parts, first.astype(BF16))


def mirror_body(info, mix, expand, mix_lines, expand_lines):
    mix_lines[...] = as_columns(mix[...]).astype(BF16)
    expand_lines[...] = as_columns(expand[...]).astype(BF16)


def mirror(info, mix, expand):
    outs = [(weight.shape[::-1], BF16) for weight in (mix, expand)]
    return call(
        mirror_body, info, [mix, expand], [whole(mix.shape), whole(expand.shape)], outs, [whole(shape) for shape, _ in outs]
    )


def norm_products(block, grads, normed, far_normed, column, mirrored, vectors, row, total, sums):
    count = normed.shape[0]
    products = tn(grads[:count, :], normed[...]) + tn(grads[count:, :], far_normed[...])
    lines = mirrored[:, block].astype(F32)
    shifts = column[:, 0:1]
    total[:, block] = products * vectors[row : row + 1, block] + shifts * vectors[row + 1 : row + 2, block]
    sums[0:1, block] = jnp.sum(lines * products, axis=0, keepdims=True)
    sums[1:2, block] = jnp.sum(lines * shifts, axis=0, keepdims=True)


def expand_grad_body(
    info, near, far, slope, far_slope, normed, far_normed, shrink, expand, vectors, pre_out, bias_out, sums, mine, other, held, total, column
):
    step = pl.program_id(0)
    clear(bias_out, sums)

    @pl.when(step < 4)
    def _():
        cot = jnp.where(step < 2, near[...], far[...])
        grad_act = nt(cot.reshape(cot.shape[0] * cot.shape[1], cot.shape[2]), shrink[...])
        slopes = jnp.where(step < 2, slope[...], far_slope[...]).reshape(grad_act.shape).astype(F32)
        grad_pre = (grad_act * slopes).astype(BF16)
        pre_out[...] = grad_pre.reshape(pre_out.shape)
        held[pl.ds(pl.multiple_of(step * grad_pre.shape[0], grad_pre.shape[0]), grad_pre.shape[0]), :] = grad_pre
        bias_out[...] += jnp.broadcast_to(jnp.sum(grad_pre.astype(F32), axis=0, keepdims=True), bias_out.shape)

    @pl.when(step == 3)
    def _():
        column[...] = as_column(bias_out[0:1, :])

    @pl.when(step >= 4)
    def _():
        block = aligned(step - 4, 2 * LANES)
        norm_products(block, held, normed, far_normed, column, expand, vectors, 2, total, sums)

    @pl.when(step == 7)
    def _():
        for shard, out in each_shard(info, mine, other):
            out[...] = total[:, aligned(shard, LANES)].astype(BF16)


def two_phases(pair):
    shape = pair[0].shape
    block, rest = (2,) + shape[1:], (0,) * (len(shape) - 1)
    return [
        pl.BlockSpec(block, lambda i, _: (jnp.minimum(i, 1),) + rest),
        pl.BlockSpec(block, lambda i, _: (jnp.clip(i - 2, 0, 1),) + rest),
    ]


def all_tokens(rows):
    return [pl.BlockSpec((rows, 2 * LANES), lambda i, _: (0, jnp.maximum(i - 4, 0)))] * 2


def in_first_phase(shape):
    rest = (0,) * (len(shape) - 1)
    return pl.BlockSpec((2,) + shape[1:], lambda i, _: (jnp.minimum(i, 3),) + rest)


def expand_backward(info, near, far, slope, normed, shrink, expand, vectors):
    tokens, width = near.shape[1:]
    columns = [half.reshape(-1, width) for half in normed]
    operands = [near, far, *slope, *columns, shrink, expand, vectors]
    in_specs = two_phases((near, far)) + two_phases(slope) + all_tokens(columns[0].shape[0])
    in_specs += [whole(operand.shape) for operand in operands[6:]]
    outs = [((GROUP, tokens, HIDDEN), BF16), ((8, HIDDEN), F32), ((8, width), F32)] + [((4 * HIDDEN, LANES), BF16)] * 2
    out_specs = [in_first_phase(outs[0][0])] + [whole(shape) for shape, _ in outs[1:]]
    scratch = [
        pltpu.VMEM((GROUP * tokens, HIDDEN), BF16),
        pltpu.VMEM((HIDDEN, width), F32),
        pltpu.VMEM((HIDDEN, LANES), F32),
    ]
    return call(expand_grad_body, info, operands, in_specs, outs, out_specs, grid=(8,), scratch=scratch, micros=9)


def attention_grad_body(
    info, near, far, normed, far_normed, heads, far_heads, tables, far_tables, probs, far_probs,
    dense, frequency, mix, vectors, bias_grad, feed_sums,
    mixed_out, mine, other, mixed_held, total, column, sums, piece,
):
    step = pl.program_id(0)
    rank = info[1]
    tokens = near.shape[1]
    clear(sums)

    @pl.when(step == 0)
    def _():
        sums[4:5, :] = jnp.sum(near[0].astype(F32), axis=0, keepdims=True)

    @pl.when(step < 4)
    def _():
        cot = jnp.where(step < 2, near[...], far[...])
        all_heads = jnp.where(step < 2, heads[...], far_heads[...])
        all_tables = jnp.where(step < 2, tables[...], far_tables[...])
        all_probs = jnp.where(step < 2, probs[...], far_probs[...])
        lane = lax.broadcasted_iota(jnp.int32, (tokens, LANES), 1)
        grad_context = nt(cot.reshape(2 * tokens, cot.shape[2]), dense[...]).astype(BF16)
        for sequence in range(2):
            queries = all_heads[sequence, :, :LANES]
            keys = all_heads[sequence, :, LANES : 2 * LANES]
            values = all_heads[sequence, :, 2 * LANES :]
            part = by_head(grad_context[sequence * tokens : (sequence + 1) * tokens], lane)
            low = all_probs[sequence].reshape(2 * tokens, tokens)
            exact = low.astype(F32)
            grad_probs = nt(part, values)
            grad_scores = exact * (grad_probs - jnp.sum(exact * grad_probs, axis=-1, keepdims=True))
            grad_scores = grad_scores.astype(BF16)
            grad_values = tn(low, part)
            grad_queries = from_heads(nn(grad_scores, keys), lane)
            grad_keys = tn(grad_scores, by_head(queries, lane))
            cos, sin = spread_tables(all_tables[sequence])
            joined = [
                turn(grad_queries * HEAD ** (-0.5), cos, -sin, lane),
                turn(grad_keys * HEAD ** (-0.5), cos, -sin, lane),
                grad_values,
            ]
            grad_mixed = jnp.concatenate(joined, axis=1).astype(BF16)
            mixed_out[sequence] = grad_mixed
            mixed_held[pl.ds(pl.multiple_of((2 * step + sequence) * tokens, tokens), tokens), :] = grad_mixed
            sums[5:6, :MIX_COLS] += jnp.sum(grad_mixed.astype(F32), axis=0, keepdims=True)

    @pl.when(step == 3)
    def _():
        column[...] = as_column(sums[5:6, :MIX_COLS])

    @pl.when(step >= 4)
    def _():
        block = aligned(step - 4, 2 * LANES)
        norm_products(block, mixed_held, normed, far_normed, column, mix, vectors, 0, total, sums)

    @pl.when(step == 7)
    def _():
        sums[2:4, :] = feed_sums[0:2, :]
        line = lax.broadcasted_iota(jnp.int32, (8, LANES), 1)
        for shard, out in each_shard(info, mine, other):
            block = aligned(shard, LANES)
            out[:MIX_COLS, :] = total[:, block].astype(BF16)
            piece[...] = jnp.zeros_like(piece)
            piece[0:5, :] = sums[0:5, block]
            for row in range(3):
                place = 3 * shard + row
                spread = jnp.zeros((1, LANES), F32)
                for part in range(3):
                    held = sums[5:6, part * LANES : (part + 1) * LANES]
                    spread = spread + jnp.where(place == 8 * part + rank, held, 0.0)
                piece[5 + row : 6 + row, :] = spread
            packed = bias_grad[:, aligned(shard // 2, LANES)]
            moved = jnp.where(jnp.bitwise_and(shard ^ rank, 1) == 1, pltpu.roll(packed, 64, 1), packed)
            moved = jnp.where(line // 64 == jnp.bitwise_and(rank, 1), moved, 0.0)
            for row in range(4):
                piece[8 + row : 9 + row, :] = jnp.where(rank // 2 == row, moved[0:1, :], 0.0)
            out[MIX_COLS:, :] = piece[...].astype(BF16)


def attention_backward(info, near, far, saved, fixed):
    tokens, width = near.shape[1:]
    normed, *saved = saved
    columns = [half.reshape(-1, width) for half in normed]
    operands = [near, far, *columns]
    in_specs = two_phases((near, far)) + all_tokens(columns[0].shape[0])
    for pair in saved:
        operands += pair
        in_specs += two_phases(pair)
    operands += list(fixed)
    in_specs += [whole(operand.shape) for operand in fixed]
    outs = [((GROUP, tokens, MIX_COLS), BF16)] + [((4 * MIX_ROWS, LANES), BF16)] * 2
    out_specs = [in_first_phase(outs[0][0])] + [whole(shape) for shape, _ in outs[1:]]
    scratch = [
        pltpu.VMEM((GROUP * tokens, MIX_COLS), BF16),
        pltpu.VMEM((MIX_COLS, width), F32),
        pltpu.VMEM((MIX_COLS, LANES), F32),
        pltpu.VMEM((8, width), F32),
        pltpu.VMEM((SMALL, LANES), F32),
    ]
    return call(
        attention_grad_body, info, operands, in_specs, outs, out_specs, grid=(8,), scratch=scratch, micros=6
    )


def input_grad_body(info, mixed, pre, mix, expand, vectors, out):
    total = nt(flat(mixed), mix[...]) * vectors[0:1, :] + nt(flat(pre), expand[...]) * vectors[2:3, :]
    out[...] = total.astype(BF16).reshape(out.shape)


def input_backward(info, mixed, pre, mix, expand, vectors, far):
    tokens, width = mixed.shape[1], mix.shape[0]
    operands = [mixed, pre, mix, expand, vectors]
    in_specs = [pairs(mixed.shape, 2 * far), pairs(pre.shape, 2 * far)]
    in_specs += [whole(operand.shape) for operand in operands[2:]]
    shape = (4, tokens, width)
    micros = 0 if far else 6
    return call(input_grad_body, info, operands, in_specs, [(shape, BF16)], [pairs(shape)], grid=(2,), micros=micros)[0]


def norm_body(info, block, cot, upper, upper_got, lower, lower_got, out):
    inputs = block[...].astype(F32)
    average = jnp.mean(inputs, axis=-1, keepdims=True)
    centred = inputs - average
    scale = lax.rsqrt(jnp.mean(centred * centred, axis=-1, keepdims=True) + EPSILON)
    normed = centred * scale
    pulled = jnp.concatenate(
        [upper[...] + upper_got[...].astype(F32), lower[...] + lower_got[...].astype(F32)]
    )
    pulled = pulled - jnp.mean(pulled, axis=-1, keepdims=True) - normed * jnp.mean(pulled * normed, axis=-1, keepdims=True)
    out[...] = cot[...].astype(F32) + scale * pulled


def each_rank(near, far, unit):
    for place, number in enumerate(NEAR):
        rows = pl.ds(place * unit, unit)
        yield number, near.at[rows], far.at[rows]


def last_out_body(info, near, far, own_dense, shrink_out, dense_out):
    rank = info[1]
    for number, one, two in each_rank(near, far, HIDDEN):
        for piece, held in ((one, rank ^ number), (two, rank ^ number ^ 1)):
            for part in range(8):
                rows = piece[64 * part : 64 * (part + 1), :]
                shrink_out[aligned(held, 64), part * LANES : (part + 1) * LANES] = rows.astype(F32)
    for part in range(8):
        start = 4 * HIDDEN + part * LANES
        rows = jnp.where(own_dense[0] == 1, near[start : start + LANES, :], far[start : start + LANES, :])
        dense_out[:, part * LANES : (part + 1) * LANES] = rows.astype(F32)


def expand_out_body(info, near, far, out):
    rank = info[1]
    upper = jnp.bitwise_and(rank, 1) == 1
    for number, one, two in each_rank(near, far, HIDDEN):
        place = (rank ^ number) // 2
        for shard in range(8):
            rows = slice(64 * shard, 64 * (shard + 1))
            lower_rows = jnp.where(upper, two[rows, :], one[rows, :])
            upper_rows = jnp.where(upper, one[rows, :], two[rows, :])
            joined = jnp.concatenate([lower_rows, upper_rows], axis=0)
            out[:, aligned(4 * shard + place, LANES)] = as_columns(joined)


def mix_out_body(info, near, far, out):
    rank = info[1]
    for number, one, two in each_rank(near, far, MIX_ROWS):
        for piece, place in ((one, rank ^ number), (two, rank ^ number ^ 1)):
            for part in range(3):
                out[:, aligned(8 * part + place, LANES)] = as_columns(piece[part * LANES : (part + 1) * LANES, :])


def after(value, *others):
    return jax.tree.map(lambda leaf: lax.optimization_barrier((leaf,) + others)[0], value)


def mark_body(info, out):
    out[...] = jnp.zeros_like(out) + info[0].astype(F32)


def mark(info, *others):
    return call(mark_body, after(info, *others), [], [], [((8, LANES), F32)], [whole((8, LANES))], micros=40)[0]


def gather_first(upper, lower):
    return swap(upper, x=1), swap(lower, low=1)


def gather_second(upper, lower, upper_x, lower_low):
    return swap(jnp.stack([upper, upper_x]), low=1), swap(jnp.stack([lower, lower_low]), x=1)


def gathered(upper, lower, upper_x, lower_low, upper_pair, lower_pair):
    return jnp.concatenate(
        [
            jnp.stack([upper, upper_pair[0], upper_x, upper_pair[1]]),
            jnp.stack([lower, lower_low, lower_pair[0], lower_pair[1]]),
        ],
        axis=1,
    )


def reduce_first(mine, other, unit, *late):
    got = after(swap(other, y=1), *late)
    total = mine.astype(F32) + got.astype(F32)
    return total[: 2 * unit], total[2 * unit :].astype(BF16)


def reduce_second(kept, sent, *late):
    return (kept + after(swap(sent, high=1), *late).astype(F32)).astype(BF16)


def share_first(slices, unit, *late):
    return jnp.concatenate([slices[unit:], after(swap(slices[:unit], low=1), *late)])


def share_second(pair, *late):
    return after(swap(pair, x=1), *late)


def scatter_first(near, far_got):
    cut = near.shape[1] // 2
    total = near.astype(F32) + far_got.astype(F32)
    sent_x = total[2:, :cut].astype(BF16)
    sent_low = total[1::2, cut:].astype(BF16)
    return total[:2, :cut], sent_x, total[0::2, cut:], sent_low


def scatter_second(kept_x, sent_x, kept_low, sent_low, *late):
    upper = kept_x + after(swap(sent_x, x=1), *late).astype(F32)
    lower = kept_low + after(swap(sent_low, low=1), *late).astype(F32)
    return upper[0], upper[1].astype(BF16), lower[0], lower[1].astype(BF16)


def scatter_third(upper, sent_upper, lower, sent_lower, *late):
    upper = upper + after(swap(sent_upper, low=1), *late).astype(F32)
    lower = lower + after(swap(sent_lower, x=1), *late).astype(F32)
    return jnp.concatenate([upper, lower])


def local(
    block_input,
    segments,
    cotangent,
    first_gain,
    first_shift,
    mix_weight,
    mix_bias,
    dense_weight,
    dense_bias,
    second_gain,
    second_shift,
    expand_weight,
    expand_bias,
    shrink_weight,
    shrink_bias,
):
    rep = lax.axis_index("rep")
    shard = lax.axis_index("fsdp")
    x, core, high, low, y = rep // 2, rep % 2, shard // 4, (shard // 2) % 2, shard % 2
    info = jnp.stack([shard, 4 * x + 2 * low + core]).astype(jnp.int32)
    tokens, width = block_input.shape
    rows = mix_weight.shape[0]

    own_y, own_x = y == core, x == high

    small = (first_gain, first_shift, second_gain, second_shift, dense_bias, shrink_bias, mix_bias, expand_bias)
    half = tokens // 2
    own, other = cut_slices(info, mix_weight, expand_weight, small)
    marks = jnp.pad(segments.astype(BF16), ((0, 15), (0, width - tokens)))
    upper, lower = block_input[:half], jnp.concatenate([block_input[half:], marks])
    along = swap(other, low=1), swap(own, high=1), swap(other, high=1, low=1)
    upper_x, lower_low = gather_first(upper, lower)
    first = mark(info, own)
    upper_x, lower_low = after((upper_x, lower_low), first)
    over = swap(cut_all(info, after(own, first), shrink_weight, dense_weight), y=1)
    upper_pair = swap(jnp.stack([upper, upper_x]), low=1)
    lower_in = jnp.stack([lower, lower_low])
    second = mark(info, upper_x, lower_in)
    along = jnp.stack(after(along, second))
    across = swap(along, y=1)
    lower_pair = swap(after(lower_in, along), x=1)

    over = after(over, along)
    high_in, low_in, other_shrink = cut_last(info, shrink_weight, dense_weight, cotangent, over)
    high_last = swap(high_in, high=1)
    low_last = swap(low_in, low=1)
    third = mark(info, along, high_in, low_in)
    upper_pair, lower_pair, across = after((upper_pair, lower_pair, across), third)
    near = gathered(upper, lower, upper_x, lower_low, upper_pair, lower_pair)
    both_last = swap(after(other_shrink, near), high=1, low=1)
    far = swap(near, core=1)
    cot_upper = after(cotangent[:half], near)
    cot_upper_x = swap(cot_upper, x=1)
    frequency = jnp.asarray(turn_constants())
    *near_saved, mix, expand, vectors, bias = forward(info, near, (own, over, along, across), frequency, tokens, width)
    high_last, low_last, both_last, cot_upper_x, far = after((high_last, low_last, both_last, cot_upper_x, far), mix)
    last, dense = pack_last(info, high_in, low_last, high_last, both_last)
    last_across = swap(last, y=1)
    cot_pairs = gather_second(cot_upper, cotangent[half:], cot_upper_x, low_last[64:])
    far = after(far, last, cot_upper_x)
    far_saved = forward(info, far, (mix, expand, vectors, bias), frequency, tokens, width, True)
    normed, heads, tables, probs, context, act, slope = zip(near_saved, far_saved)
    mix_lines, expand_lines = mirror(info, after(mix, context[1]), expand)
    cot_near = gathered(
        cot_upper, cotangent[half:], cot_upper_x, low_last[64:], *after(cot_pairs, mix_lines)
    )
    cot_far = swap(cot_near, core=1)
    last_across = after(last_across, cot_near)
    branch_far, shrink = project(info, context[1], act[1], dense, (high_in, over, last, last_across), True)
    branch_got = swap(branch_far, core=1)
    (branch_near,) = project(info, context[0], act[0], dense, shrink, False)
    cot_far = after(cot_far, branch_near)
    last_mine, last_other, dense_grad = last_backward(info, cot_near, cot_far, act, context)
    branch_near = after(branch_near, dense_grad)
    branch_sum = (branch_near.astype(F32) + branch_got.astype(F32)).astype(BF16)
    branch_kept, branch_sent = branch_sum[:2], branch_sum[2:]
    dense_sent = after(dense_grad, mark(info, branch_sent))
    grad_pre, bias_grad, feed_sums, expand_mine, expand_other = expand_backward(
        info, cot_near, cot_far, slope, normed, after(shrink, branch_sent), expand_lines, vectors
    )
    last_part = reduce_first(last_mine, last_other, HIDDEN, grad_pre)
    dense_got = after(swap(dense_sent, high=1), grad_pre)
    dense_grad = (dense_grad.astype(F32) + dense_got.astype(F32)).astype(BF16)
    grad_mixed, mix_mine, mix_other = attention_backward(
        info,
        cot_near,
        cot_far,
        (normed, heads, tables, probs),
        (after(dense, last_part[1], dense_grad), frequency, mix_lines, vectors, bias_grad, feed_sums),
    )
    error_far = input_backward(info, grad_mixed, grad_pre, mix, expand, vectors, True)
    error_got = swap(error_far, core=1)
    expand_part = reduce_first(expand_mine, expand_other, HIDDEN, error_far)
    last_slices = reduce_second(*last_part, error_far)
    dense_got = after(swap(dense_grad, y=1), error_far)
    dense_grad = (dense_grad.astype(F32) + dense_got.astype(F32)).astype(BF16)
    branch = branch_kept.astype(F32) + after(swap(branch_sent, x=1), error_far).astype(F32)
    branch_own, branch_last = branch[0].astype(BF16), branch[1].astype(BF16)
    error_near = input_backward(
        info,
        after(grad_mixed, error_far, branch_own, branch_last, last_slices, dense_grad, expand_part[1]),
        grad_pre,
        mix,
        expand,
        vectors,
        False,
    )
    dense_x = after(swap(dense_grad, x=1), error_near)
    dense_part = jnp.where(own_x, dense_grad, dense_x)
    mix_part = reduce_first(mix_mine, mix_other, MIX_ROWS, error_near)
    error = scatter_first(after(error_near, dense_part, mix_part[1]), error_got)
    last_pair = share_first(last_slices, HIDDEN, error[1], error[3])
    fourth = mark(info, last_pair, mix_part[1], error[1], error[3], dense_part)
    expand_slices = reduce_second(*expand_part, fourth)
    last_x = share_second(last_pair, fourth)
    last_near = jnp.concatenate([last_pair, last_x, dense_part])
    mix_slices = reduce_second(*mix_part, fourth)
    error = scatter_second(*error, fourth)
    fifth = mark(info, expand_slices, mix_slices, error[1], error[3], last_near)
    expand_pair = share_first(expand_slices, HIDDEN, fifth)
    mix_pair = share_first(mix_slices, MIX_ROWS, fifth)
    last_far = swap(after(last_near, mix_pair), core=1)

    def out(body, near, far, shapes, flag=None):
        operands = [near, far]
        in_specs = [whole(near.shape), whole(far.shape)]
        if flag is not None:
            operands.append(flag)
            in_specs.append(pl.BlockSpec(memory_space=pltpu.SMEM))
        return call(body, info, operands, in_specs, [(shape, F32) for shape in shapes], [whole(shape) for shape in shapes])

    flag = own_y.astype(jnp.int32).reshape(1)
    shapes = [shrink_weight.shape, dense_weight.shape]
    upper_got = after(swap(error[1], low=1), mix_pair, expand_pair)
    lower_got = after(swap(error[3], x=1), mix_pair, expand_pair)
    operands = [block_input, cotangent, error[0], upper_got, error[2], lower_got]
    (input_grad,) = call(
        norm_body,
        info,
        operands,
        [whole(operand.shape) for operand in operands],
        [(block_input.shape, F32)],
        [whole(block_input.shape)],
    )
    shrink_out, dense_out = out(last_out_body, last_near, after(last_far, input_grad), shapes, flag)
    expand_near = jnp.concatenate([expand_pair, share_second(expand_pair, shrink_out)])
    expand_far = swap(expand_near, core=1)
    (expand_out,) = out(expand_out_body, expand_near, expand_far, [expand_weight.shape])
    branch = branch_own.astype(F32) + after(swap(after(branch_last, mix_pair), low=1), expand_near).astype(F32)
    block_out = (block_input.astype(F32) + branch + (vectors[4] + vectors[5])).astype(BF16)
    mix_x = share_second(mix_pair, expand_near)
    mix_parts = [mix_pair[:MIX_ROWS], mix_pair[MIX_ROWS:], mix_x[:MIX_ROWS], mix_x[MIX_ROWS:]]
    mix_sums = [part[MIX_COLS:].astype(F32) for part in mix_parts]
    mix_sums = ((mix_sums[0] + mix_sums[1]) + (mix_sums[2] + mix_sums[3])).astype(BF16)
    near = jnp.concatenate(mix_parts + [mix_sums])
    far = swap(near, core=1)
    sums = mix_sums.astype(F32) + far[4 * MIX_ROWS :].astype(F32)
    (mix_out,) = out(mix_out_body, near, far, [mix_weight.shape])
    again = lax.optimization_barrier(sums)
    return (
        block_out,
        input_grad,
        sums[0],
        sums[1],
        mix_out,
        sums[5:8].reshape(-1),
        dense_out,
        sums[4],
        sums[2],
        sums[3],
        expand_out,
        sums[8:12].reshape(-1),
        shrink_out,
        again[4],
    )


def solution(mesh):
    tensor_parallel = mesh.shape["rep"] == TP_REP and mesh.shape["fsdp"] == TP_FSDP
    return jax.shard_map(
        local if tensor_parallel else local_general,
        mesh=mesh,
        in_specs=(
            P(("rep", "fsdp"), None),
            P(("rep", "fsdp"), None),
            P(("rep", "fsdp"), None),
            P("fsdp"),
            P("fsdp"),
            P("fsdp", None),
            P("fsdp"),
            P("fsdp", None),
            P("fsdp"),
            P("fsdp"),
            P("fsdp"),
            P("fsdp", None),
            P("fsdp"),
            P("fsdp", None),
            P("fsdp"),
        ),
        out_specs=(
            P(("rep", "fsdp"), None),
            P(("rep", "fsdp"), None),
            P("fsdp"),
            P("fsdp"),
            P("fsdp", None),
            P("fsdp"),
            P("fsdp", None),
            P("fsdp"),
            P("fsdp"),
            P("fsdp"),
            P("fsdp", None),
            P("fsdp"),
            P("fsdp", None),
            P("fsdp"),
        ),
        check_vma=False,
    )
```
